32 devices in a mesh: parts: 2 (over y), dp: 4 (over z), seq: 4 (over x, core).
Axes of the slice: x: 2, y: 2, z: 4, core: 2. Of those that a mesh axis runs over, the one named last changes fastest.
Arguments:
- queries: bfloat16 [8, 4, 128, 32, 128], P(('parts', 'dp'), None, 'seq'), parts along dimension 0, may hold values from -6 to 6
- key_rows: bfloat16 [8, 4, 128, 32, 128], P(('parts', 'dp'), None, 'seq'), parts along dimension 0, may hold values from -6 to 6
- value_rows: bfloat16 [8, 4, 128, 32, 128], P(('parts', 'dp'), None, 'seq'), parts along dimension 0, may hold values from -6 to 6
- out_grad: bfloat16 [8, 4, 128, 32, 128], P(('parts', 'dp'), None, 'seq'), parts along dimension 0, may hold values from -6 to 6
- norm_gains: float32 [2, 32, 128], P(None, 'seq'), may hold values from 0.1 to 1.9
- clip_units: int32 [8, 4], P('parts'), parts along dimension 0, may hold values from 0 to 3, as said below
Outputs:
- gain_grads: float32 [4, 32, 128], P('parts', 'seq', 'dp'), parts along dimension 0
The draws below stay inside these ranges and needn't reach their ends.
There are 2 independent parts, one for each index of `parts`. The reference program is written for one: setup_inputs(seed, part) draws one part's arguments, and reference() takes and returns one part's arrays. A program takes and returns all parts, laid end to end along the dimension named above; an argument that names none is the same for every part. Nothing has to cross between parts.
Inputs may be any that keep to these rules, and one draw needn't show every extreme that they name: `clip_units`: row g describes group g's 4 slots: entry j is the number of token blocks of the clip that begins at slot j, and 0 where no clip begins. The clips of a row are consecutive and fill all 4 slots; each spans 1 to 3 slots, and some row holds a clip of 3 slots.
All inputs are finite; a program needn't handle non-finite values.
Results may differ from the reference program's by a relative error of at most 0.0065.
Values may be sent and summed in bfloat16 or wider, within the bound.
No kernel may reach another device: no remote copies, remote signals or barrier semaphores. Data moves between devices by JAX's collectives and lax.ppermute only.
A program may use at most 64 MiB of HBM per device.

```python
import jax
import jax.numpy as jnp
from jax import lax

HEADS = 32
HS = 128
SLOTS = 4
MAXCLIP = 3
UNIT = 128
N_DP = 4


def draw_clip_units(key, part):
    key = jax.random.fold_in(key, 11)
    coin_key, pick_key = jax.random.split(key)
    coins = jax.random.randint(coin_key, (N_DP, SLOTS - 1), 0, 2).astype(jnp.int32)
    chosen = jax.random.randint(pick_key, (), 0, N_DP).astype(jnp.int32)
    groups = jnp.arange(N_DP, dtype=jnp.int32)
    bounds = jnp.arange(SLOTS - 1, dtype=jnp.int32)
    forced = jnp.where(bounds[None, :] < MAXCLIP - 1, 0, jnp.where(bounds[None, :] == MAXCLIP - 1, 1, coins))
    coins = jnp.where((groups == chosen)[:, None], forced, coins)

    def advance(run_length, coin):
        cutting = (coin > 0) | (run_length >= MAXCLIP)
        return (jnp.where(cutting, 1, run_length + 1).astype(jnp.int32), cutting.astype(jnp.int32))
    _, cuts = lax.scan(advance, jnp.ones((N_DP,), jnp.int32), coins.T)
    begins = jnp.concatenate([jnp.ones((N_DP, 1), jnp.int32), cuts.T], axis=1)
    positions = jnp.arange(SLOTS, dtype=jnp.int32)
    later = jnp.where((positions[None, None, :] > positions[None, :, None]) & (begins[:, None, :] > 0), positions[None, None, :], SLOTS)
    following = jnp.min(later, axis=2)
    return jnp.where(begins > 0, following - positions[None, :], 0).astype(jnp.int32)


def strengthened(values, key, source, target, shards_of, factor):
    owner, partner = [(jnp.arange(values.shape[dim]) // (values.shape[dim] // shards_of)).reshape([-1 if axis == dim else 1 for axis in range(values.ndim)]) for dim in (source, target)]
    chosen = jax.random.permutation(key, shards_of)[partner]
    strong = (owner == chosen) | (owner == (partner + shards_of // 2) % shards_of)
    return jnp.where(strong, factor * values, values)


def levels(key, shape, cuts, least, largest):
    def one(dim, parts):
        steps = jax.random.uniform(jax.random.fold_in(jax.random.fold_in(key, 6), dim), (parts,), jnp.float32, least / len(cuts), largest / len(cuts))
        return jnp.repeat(jnp.exp(steps), shape[dim] // parts).reshape((-1,) + (1,) * (len(shape) - dim - 1))

    gain = one(*cuts[0])
    for cut in cuts[1:]:
        gain = gain * one(*cut)
    return gain


def scatter_about(key, shape, scale, bound, shards=(), held_as=jnp.bfloat16):
    drawn = scale * jax.random.normal(key, shape, jnp.float32)
    if shards:
        drawn = drawn * levels(key, shape, shards, -0.22, 0.18)
    return jnp.clip(drawn, -bound, bound).astype(held_as)


def bell_draw_with(stream_key, shape, width, bound, cuts, heavy, kind=jnp.bfloat16):
    result = width * jax.random.normal(stream_key, shape, jnp.float32)
    if cuts:
        result = result * levels(stream_key, shape, cuts, -0.22, 0.18)
    return jnp.clip(strengthened(result, jax.random.fold_in(stream_key, 3), *heavy), -bound, bound).astype(kind)


def setup_inputs(seed: int = 0, part: int = 0) -> dict:
    streams_of = jax.random.split(jax.random.key(seed), 7)
    own_keys = jax.random.split(jax.random.fold_in(streams_of[6], part), 7)
    return {
        "queries": scatter_about(own_keys[0], (N_DP, SLOTS, UNIT, HEADS, HS), 1.0, 6.0, ((0, 4), (2, 4))),
        "key_rows": scatter_about(own_keys[1], (N_DP, SLOTS, UNIT, HEADS, HS), 1.0, 6.0, ((0, 4), (2, 4))),
        "value_rows": scatter_about(own_keys[2], (N_DP, SLOTS, UNIT, HEADS, HS), 1.0, 6.0, ((0, 4), (2, 4))),
        "out_grad": bell_draw_with(own_keys[3], (N_DP, SLOTS, UNIT, HEADS, HS), 1.0, 6.0, ((0, 4), (2, 4)), (0, 4, 4, 2.0)),
        "norm_gains": jnp.clip(1.0 + 0.18 * jax.random.normal(streams_of[4], (2, HEADS, HS), jnp.float32), 0.1, 1.9),
        "clip_units": draw_clip_units(jax.random.fold_in(jax.random.fold_in(streams_of[6], part), 71), part),
    }


def unit_plan(clip_table):
    positions = jnp.arange(clip_table.shape[0], dtype=jnp.int32)
    earlier = (positions[None, :] <= positions[:, None]) & (clip_table[None, :] > 0)
    unit_starts = lax.optimization_barrier(jnp.max(jnp.where(earlier, positions[None, :], 0), axis=1)).astype(jnp.int32)
    unit_sizes = lax.optimization_barrier(jnp.sum(jnp.where(positions[None, :] == unit_starts[:, None], clip_table[None, :], 0), axis=1))
    unit_sizes = jnp.where(positions < unit_starts + unit_sizes, unit_sizes, 0).astype(jnp.int32)
    return (unit_starts, unit_sizes)

def normalize(values):
    widened = values.astype(jnp.float32)
    return widened * lax.rsqrt(lax.optimization_barrier(jnp.mean(widened * widened, axis=-1, keepdims=True)) + 1e-06)

def clip_terms(query_unit, key_clip, value_clip, grad_unit, gains):
    score_scale = query_unit.shape[-1] ** (-0.5)
    query_hat = normalize(query_unit)
    key_hat = normalize(key_clip)
    query_norm = (query_hat * gains[0]).astype(jnp.bfloat16).astype(jnp.float32)
    key_norm = (key_hat * gains[1]).astype(jnp.bfloat16).astype(jnp.float32)
    value_wide = value_clip.astype(jnp.float32)
    grad_wide = grad_unit.astype(jnp.float32)
    scores = jnp.einsum('qhd,khd->hqk', query_norm, key_norm) * score_scale
    expo = jnp.exp(scores)
    prob = expo / lax.optimization_barrier(jnp.sum(expo, axis=-1, keepdims=True))
    prob_low = prob.astype(jnp.bfloat16).astype(jnp.float32)
    attn_out = jnp.einsum('hqk,khd->qhd', prob_low, value_wide)
    delta = jnp.einsum('qhd,qhd->hq', grad_wide, attn_out)
    dprob = jnp.einsum('qhd,khd->hqk', grad_wide, value_wide)
    dscore = (prob * (dprob - delta[:, :, None])).astype(jnp.bfloat16).astype(jnp.float32)
    dq_norm = jnp.einsum('hqk,khd->qhd', dscore, key_norm) * score_scale
    dk_norm = jnp.einsum('hqk,qhd->khd', dscore, query_norm) * score_scale
    return jnp.stack([lax.optimization_barrier(jnp.sum(dq_norm * query_hat, axis=0)), lax.optimization_barrier(jnp.sum(dk_norm * key_hat, axis=0))])

def piece_terms(pieces, clip_table, gains):
    query_all, key_all, value_all, grad_all = pieces
    unit_starts, unit_sizes = unit_plan(clip_table)
    unit_rows = query_all.shape[1]
    head_count = query_all.shape[2]
    head_size = query_all.shape[3]

    def branch_for(unit_count):

        def run(slot_index, clip_start):
            query_unit = lax.dynamic_slice_in_dim(query_all, slot_index, 1, 0)[0]
            grad_unit = lax.dynamic_slice_in_dim(grad_all, slot_index, 1, 0)[0]
            key_clip = lax.dynamic_slice_in_dim(key_all, clip_start, unit_count, 0).reshape(unit_count * unit_rows, head_count, head_size)
            value_clip = lax.dynamic_slice_in_dim(value_all, clip_start, unit_count, 0).reshape(unit_count * unit_rows, head_count, head_size)
            return clip_terms(query_unit, key_clip, value_clip, grad_unit, gains)
        return run

    def empty_branch(slot_index, clip_start):
        return jnp.zeros((2, head_count, head_size), jnp.float32)
    branches = [empty_branch] + [branch_for(unit_count) for unit_count in range(1, MAXCLIP + 1)]

    def advance(slot_index, running):
        slot_index = jnp.asarray(slot_index).astype(jnp.int32)
        return running + lax.switch(unit_sizes[slot_index], branches, slot_index, unit_starts[slot_index])
    return lax.fori_loop(0, clip_table.shape[0], advance, jnp.zeros((2, head_count, head_size), jnp.float32))

def reference(queries, key_rows, value_rows, out_grad, norm_gains, clip_units):

    def group_step(group_index, running):
        group_index = jnp.asarray(group_index).astype(jnp.int32)
        pieces = tuple((lax.dynamic_index_in_dim(array, group_index, 0, keepdims=False) for array in (queries, key_rows, value_rows, out_grad)))
        clip_table = lax.dynamic_index_in_dim(clip_units, group_index, 0, keepdims=False)
        return running + piece_terms(pieces, clip_table, norm_gains)
    start = jnp.zeros((2, queries.shape[3], queries.shape[4]), jnp.float32)
    return lax.fori_loop(0, queries.shape[0], group_step, start)
```

```python
import functools
import math

import jax
import jax.numpy as jnp
from jax import lax
from jax.experimental import pallas as pl
from jax.experimental.pallas import tpu as pltpu
from jax.sharding import PartitionSpec as P

MAXCLIP = 3
TILE = 8
EPS = 1e-06
VMEM_LIMIT = 48 * 1024 * 1024


def head_chunks(heads):
    sizes = {8: (2, 2, 2, 2)}.get(heads)
    if sizes is None:
        sizes = (1,) * heads if heads <= 2 else (heads - heads // 2, heads // 2)
    bounds, start = [], 0
    for size in sizes:
        bounds.append((start, start + size))
        start += size
    return bounds


def pack_kernel(plan, heads, *refs):
    arrays = refs[:4]
    outs = refs[4 : 4 + sum(len(chunks) for _, chunks in plan)]
    raw, wide, sems = refs[4 + len(outs) :]
    me = lax.axis_index("seq")
    slots, rows = raw.shape[2], raw.shape[3]
    spans = max(1, heads // TILE)

    def copy(index, array, span, first):
        return pltpu.make_async_copy(
            arrays[array].at[0, :, :, pl.ds(first + span * TILE, TILE), :],
            raw.at[index, array * spans + span],
            sems.at[index, array * spans + span],
        )

    firsts, offsets = [], []
    for flip, _ in plan:
        head = jnp.bitwise_xor(me, flip) * heads
        firsts.append(pl.multiple_of((head // TILE) * TILE, TILE))
        offsets.append(0 if heads % TILE == 0 else lax.rem(head, TILE))
    for index in range(len(plan)):
        for array in range(4):
            for span in range(spans):
                copy(index, array, span, firsts[index]).start()
    place = 0
    for index, (_, chunks) in enumerate(plan):
        for array in range(4):
            for span in range(spans):
                copy(index, array, span, firsts[index]).wait()
                for slot in range(slots):
                    wide[slot] = (
                        raw[index, array * spans + span, slot]
                        .astype(jnp.float32)
                        .reshape(rows * TILE, wide.shape[-1])
                    )
                    for number, (low, high) in enumerate(chunks):
                        for head in range(max(low, span * TILE), min(high, (span + 1) * TILE)):
                            outs[place + number][head - low, array, slot * rows : (slot + 1) * rows, :] = wide[
                                slot, pl.ds(offsets[index] + head - span * TILE, rows, stride=TILE), :
                            ].astype(jnp.bfloat16)
        place += len(chunks)


def pack(arrays, plan, heads):
    _, slots, rows, _, size = arrays[0].shape
    spans = max(1, heads // TILE)
    shapes = [
        jax.ShapeDtypeStruct((high - low, 4, slots * rows, size), jnp.bfloat16)
        for _, chunks in plan
        for low, high in chunks
    ]
    count = len(plan)
    moved = count * 4 * spans * slots * rows * TILE * size * 2
    return pl.pallas_call(
        functools.partial(pack_kernel, plan, heads),
        out_shape=shapes,
        in_specs=[pl.BlockSpec(memory_space=pl.ANY)] * 4,
        out_specs=[pl.BlockSpec(memory_space=pltpu.VMEM)] * len(shapes),
        scratch_shapes=[
            pltpu.VMEM((count, 4 * spans, slots, rows, TILE, size), jnp.bfloat16),
            pltpu.VMEM((slots, rows * TILE, size), jnp.float32),
            pltpu.SemaphoreType.DMA((count, 4 * spans)),
        ],
        compiler_params=pltpu.CompilerParams(vmem_limit_bytes=VMEM_LIMIT),
        cost_estimate=pl.CostEstimate(flops=moved, bytes_accessed=2 * moved, transcendentals=0),
        name="pack",
    )(*arrays)


def contract_last(left, right):
    return lax.dot_general(left, right, (((1,), (1,)), ((), ())), preferred_element_type=jnp.float32)


def attention_chunk(low, units, gains, pieces, held, total):
    query, key, value, grad = held
    group = lax.axis_index("dp")
    count, _, tokens, size = pieces[0].shape
    slots = units.shape[1]
    rows = tokens // slots
    unit = rows * len(pieces)
    for head in range(count):
        for array, kept in ((0, query), (1, key)):
            gain = gains[array, low + head : low + head + 1, :]
            for source, piece in enumerate(pieces):
                wide = piece[head, array].astype(jnp.float32)
                normed = wide * lax.rsqrt(jnp.mean(wide * wide, axis=-1, keepdims=True) + EPS)
                normed = (normed * gain).astype(jnp.bfloat16)
                for slot in range(slots):
                    kept[head, slot * unit + source * rows : slot * unit + (source + 1) * rows, :] = normed[
                        slot * rows : (slot + 1) * rows
                    ]
        for array, kept in ((2, value), (3, grad)):
            for source, piece in enumerate(pieces):
                for slot in range(slots):
                    kept[head, slot * unit + source * rows : slot * unit + (source + 1) * rows, :] = piece[
                        head, array, slot * rows : (slot + 1) * rows, :
                    ]
    total[...] = jnp.zeros_like(total)
    factor = size ** (-0.5) * math.log2(math.e)

    def clip(slot, span):
        length = span * unit
        start = pl.multiple_of(slot * unit, unit)
        for head in range(count):
            q = query[head, pl.ds(start, length), :]
            k = key[head, pl.ds(start, length), :]
            expo = jnp.exp2(contract_last(k, q) * factor)
            dprob = contract_last(value[head, pl.ds(start, length), :], grad[head, pl.ds(start, length), :])
            prob = expo * (1.0 / jnp.sum(expo, axis=0, keepdims=True))
            delta = jnp.sum(prob * dprob, axis=0, keepdims=True)
            dscore = (prob * (dprob - delta)).astype(jnp.bfloat16)
            mixed = jnp.dot(dscore, q, preferred_element_type=jnp.float32)
            total[head : head + 1, :] += jnp.sum(mixed * k.astype(jnp.float32), axis=0, keepdims=True)

    def at_slot(slot, carry):
        span_here = units[group, slot]
        for span in range(1, min(MAXCLIP, slots) + 1):

            @pl.when(jnp.logical_and(span_here == span, slot + span <= slots))
            def _():
                clip(slot, span)

        return carry

    lax.fori_loop(0, slots, at_slot, 0)


def chunk_kernel(low, sources, units, gains, *refs):
    pieces, out, held = refs[:sources], refs[sources], refs[sources + 1 :]
    attention_chunk(low, units, gains, pieces, held, out)


def last_kernel(low, sources, earlier, peers, units, gains, *refs):
    pieces = refs[:sources]
    before = refs[sources : sources + earlier]
    outs = refs[sources + earlier : sources + earlier + len(peers)]
    held, total = refs[sources + earlier + len(peers) : -1], refs[-1]
    attention_chunk(low, units, gains, pieces, held, total)
    group = lax.axis_index("dp")
    size = total.shape[-1]
    width = outs[0].shape[-1]
    scaled = jnp.concatenate([ref[...] for ref in before] + [total[...]], axis=0) * (size ** (-0.5))
    for side in range(2):
        grads = scaled / gains[side]
        for out, flip in zip(outs, peers):
            shift = lax.rem(size - jnp.bitwise_xor(group, flip) * width, size)
            out[side] = pltpu.roll(grads, shift, 1)[:, :width]


def attend(low, units, gains, pieces, earlier=None, peers=None):
    count, _, tokens, size = pieces[0].shape
    all_tokens = tokens * len(pieces)
    held = [pltpu.VMEM((count, all_tokens, size), jnp.bfloat16)] * 4
    if earlier is None:
        kernel = functools.partial(chunk_kernel, low, len(pieces))
        shapes = jax.ShapeDtypeStruct((count, size), jnp.float32)
        earlier = []
        outs = pl.BlockSpec(memory_space=pltpu.VMEM)
    else:
        kernel = functools.partial(last_kernel, low, len(pieces), len(earlier), peers)
        heads = gains.shape[1]
        shapes = [jax.ShapeDtypeStruct((2, heads, size // len(peers)), jnp.float32)] * len(peers)
        held.append(pltpu.VMEM((count, size), jnp.float32))
        outs = [pl.BlockSpec(memory_space=pltpu.VMEM)] * len(peers)
    pairs = count * all_tokens * all_tokens // 2
    return pl.pallas_call(
        kernel,
        out_shape=shapes,
        in_specs=[pl.BlockSpec(memory_space=pltpu.SMEM)]
        + [pl.BlockSpec(memory_space=pltpu.VMEM)] * (1 + len(pieces) + len(earlier)),
        out_specs=outs,
        scratch_shapes=held,
        compiler_params=pltpu.CompilerParams(vmem_limit_bytes=VMEM_LIMIT),
        cost_estimate=pl.CostEstimate(
            flops=6 * pairs * size, bytes_accessed=len(pieces) * count * 4 * tokens * size * 2, transcendentals=pairs
        ),
        name="attend",
    )(units, gains, *pieces, *earlier)


def body(sequence, groups, queries, key_rows, value_rows, out_grad, norm_gains, clip_units):
    arrays = (queries, key_rows, value_rows, out_grad)
    heads = norm_gains.shape[1]
    chunks = head_chunks(heads)
    far = list(range(2, sequence)) or [1]
    near = [flip for flip in range(1, sequence) if flip not in far]

    def send(block, flip):
        return lax.ppermute(block, "seq", [(s, s ^ flip) for s in range(sequence)])

    held = [{} for _ in chunks]
    first = pack(arrays, [(flip, chunks[:1]) for flip in far], heads)
    for flip, block in zip(far, first):
        held[0][flip] = send(block, flip)
    plan = [(flip, chunks[1:]) for flip in far] + [(flip, chunks) for flip in near] + [(0, chunks)]
    blocks = iter(pack(arrays, plan, heads))
    for flip, wanted in plan:
        for bounds in wanted:
            block = next(blocks)
            held[chunks.index(bounds)][flip] = send(block, flip) if flip else block
    sums = []
    for number, (low, _) in enumerate(chunks[:-1]):
        pieces = [held[number][flip] for flip in range(sequence)]
        sums.append(attend(low, clip_units, norm_gains, pieces))
    pieces = [held[-1][flip] for flip in range(sequence)]
    parts = attend(chunks[-1][0], clip_units, norm_gains, pieces, sums, list(range(groups)))
    result = parts[0]
    for flip in range(1, groups):
        result = result + lax.ppermute(parts[flip], "dp", [(g, g ^ flip) for g in range(groups)])
    return result


def solution(mesh):
    return jax.shard_map(
        functools.partial(body, mesh.shape["seq"], mesh.shape["dp"]),
        mesh=mesh,
        in_specs=(
            P(("parts", "dp"), None, "seq", None, None),
            P(("parts", "dp"), None, "seq", None, None),
            P(("parts", "dp"), None, "seq", None, None),
            P(("parts", "dp"), None, "seq", None, None),
            P(None, "seq", None),
            P("parts", None),
        ),
        out_specs=P("parts", "seq", "dp"),
        check_vma=False,
    )
```

```python
import functools
import math

import jax
import jax.numpy as jnp
from jax import lax
from jax.experimental import pallas as pl
from jax.experimental.pallas import tpu as pltpu
from jax.sharding import PartitionSpec as P

MAXCLIP = 3
TILE = 8
EPS = 1e-06
VMEM_LIMIT = 48 * 1024 * 1024
PACK_VMEM_LIMIT = 60 * 1024 * 1024


def head_chunks(heads):
    sizes = {8: (2, 3, 2, 1)}.get(heads)
    if sizes is None:
        sizes = (1,) * heads if heads <= 2 else (heads - heads // 2, heads // 2)
    bounds, start = [], 0
    for size in sizes:
        bounds.append((start, start + size))
        start += size
    return bounds


def pack_kernel(plan, heads, after, *refs):
    arrays = refs[:4]
    outs = refs[4 + after : 4 + after + sum(len(chunks) for _, chunks in plan)]
    raw, wide, sems = refs[4 + after + len(outs) :]
    me = lax.axis_index("seq")
    slots, rows = raw.shape[2], raw.shape[3]
    spans = max(1, heads // TILE)

    def copy(index, array, span, first):
        return pltpu.make_async_copy(
            arrays[array].at[0, :, :, pl.ds(first + span * TILE, TILE), :],
            raw.at[index, array * spans + span],
            sems.at[index, array * spans + span],
        )

    firsts, offsets = [], []
    for flip, _ in plan:
        head = jnp.bitwise_xor(me, flip) * heads
        firsts.append(pl.multiple_of((head // TILE) * TILE, TILE))
        offsets.append(0 if heads % TILE == 0 else lax.rem(head, TILE))
    for index in range(len(plan)):
        for array in range(4):
            for span in range(spans):
                copy(index, array, span, firsts[index]).start()
    place = 0
    for index, (_, chunks) in enumerate(plan):
        for array in range(4):
            for span in range(spans):
                copy(index, array, span, firsts[index]).wait()
                for slot in range(slots):
                    wide[slot] = (
                        raw[index, array * spans + span, slot]
                        .astype(jnp.float32)
                        .reshape(rows * TILE, wide.shape[-1])
                    )
                    for number, (low, high) in enumerate(chunks):
                        for head in range(max(low, span * TILE), min(high, (span + 1) * TILE)):
                            outs[place + number][head - low, array, slot * rows : (slot + 1) * rows, :] = wide[
                                slot, pl.ds(offsets[index] + head - span * TILE, rows, stride=TILE), :
                            ].astype(jnp.bfloat16)
        place += len(chunks)


def pack(arrays, plan, heads, after=()):
    _, slots, rows, _, size = arrays[0].shape
    spans = max(1, heads // TILE)
    shapes = [
        jax.ShapeDtypeStruct((high - low, 4, slots * rows, size), jnp.bfloat16)
        for _, chunks in plan
        for low, high in chunks
    ]
    count = len(plan)
    moved = count * 4 * spans * slots * rows * TILE * size * 2
    return pl.pallas_call(
        functools.partial(pack_kernel, plan, heads, len(after)),
        out_shape=shapes,
        in_specs=[pl.BlockSpec(memory_space=pltpu.HBM)] * 4 + [pl.BlockSpec(memory_space=pl.ANY)] * len(after),
        out_specs=[pl.BlockSpec(memory_space=pltpu.VMEM)] * len(shapes),
        scratch_shapes=[
            pltpu.VMEM((count, 4 * spans, slots, rows, TILE, size), jnp.bfloat16),
            pltpu.VMEM((slots, rows * TILE, size), jnp.float32),
            pltpu.SemaphoreType.DMA((count, 4 * spans)),
        ],
        compiler_params=pltpu.CompilerParams(vmem_limit_bytes=PACK_VMEM_LIMIT),
        cost_estimate=pl.CostEstimate(flops=moved, bytes_accessed=2 * moved, transcendentals=0),
        name="pack",
    )(*arrays, *after)


def contract_last(left, right):
    return lax.dot_general(left, right, (((1,), (1,)), ((), ())), preferred_element_type=jnp.float32)


def attention_chunk(low, units, gains, pieces, held, total):
    query, key, value, grad = held
    group = lax.axis_index("dp")
    count, _, tokens, size = pieces[0].shape
    slots = units.shape[1]
    rows = tokens // slots
    unit = rows * len(pieces)
    for head in range(count):
        for array, kept in ((0, query), (1, key)):
            gain = gains[array, low + head : low + head + 1, :]
            for source, piece in enumerate(pieces):
                wide = piece[head, array].astype(jnp.float32)
                normed = wide * lax.rsqrt(jnp.mean(wide * wide, axis=-1, keepdims=True) + EPS)
                normed = (normed * gain).astype(jnp.bfloat16)
                for slot in range(slots):
                    kept[head, slot * unit + source * rows : slot * unit + (source + 1) * rows, :] = normed[
                        slot * rows : (slot + 1) * rows
                    ]
        for array, kept in ((2, value), (3, grad)):
            for source, piece in enumerate(pieces):
                for slot in range(slots):
                    kept[head, slot * unit + source * rows : slot * unit + (source + 1) * rows, :] = piece[
                        head, array, slot * rows : (slot + 1) * rows, :
                    ]
    total[...] = jnp.zeros_like(total)
    factor = size ** (-0.5) * math.log2(math.e)

    def clip(slot, span):
        length = span * unit
        start = pl.multiple_of(slot * unit, unit)
        for head in range(count):
            q = query[head, pl.ds(start, length), :]
            k = key[head, pl.ds(start, length), :]
            expo = jnp.exp2(contract_last(k, q) * factor)
            dprob = contract_last(value[head, pl.ds(start, length), :], grad[head, pl.ds(start, length), :])
            prob = expo * (1.0 / jnp.sum(expo, axis=0, keepdims=True))
            delta = jnp.sum(prob * dprob, axis=0, keepdims=True)
            dscore = (prob * (dprob - delta)).astype(jnp.bfloat16)
            mixed = jnp.dot(dscore, q, preferred_element_type=jnp.float32)
            total[head : head + 1, :] += jnp.sum(mixed * k.astype(jnp.float32), axis=0, keepdims=True)

    def at_slot(slot, carry):
        span_here = units[group, slot]
        for span in range(1, min(MAXCLIP, slots) + 1):

            @pl.when(jnp.logical_and(span_here == span, slot + span <= slots))
            def _():
                clip(slot, span)

        return carry

    lax.fori_loop(0, slots, at_slot, 0)


def chunk_kernel(low, sources, units, gains, *refs):
    pieces, out, held = refs[:sources], refs[sources], refs[sources + 1 :]
    attention_chunk(low, units, gains, pieces, held, out)


def last_kernel(low, sources, earlier, peers, units, gains, *refs):
    pieces = refs[:sources]
    before = refs[sources : sources + earlier]
    outs = refs[sources + earlier : sources + earlier + len(peers)]
    held, total = refs[sources + earlier + len(peers) : -1], refs[-1]
    attention_chunk(low, units, gains, pieces, held, total)
    group = lax.axis_index("dp")
    size = total.shape[-1]
    width = outs[0].shape[-1]
    scaled = jnp.concatenate([ref[...] for ref in before] + [total[...]], axis=0) * (size ** (-0.5))
    for side in range(2):
        grads = scaled / gains[side]
        for out, flip in zip(outs, peers):
            shift = lax.rem(size - jnp.bitwise_xor(group, flip) * width, size)
            out[side] = pltpu.roll(grads, shift, 1)[:, :width]


def attend(low, units, gains, pieces, earlier=None, peers=None):
    count, _, tokens, size = pieces[0].shape
    all_tokens = tokens * len(pieces)
    held = [pltpu.VMEM((count, all_tokens, size), jnp.bfloat16)] * 4
    if earlier is None:
        kernel = functools.partial(chunk_kernel, low, len(pieces))
        shapes = jax.ShapeDtypeStruct((count, size), jnp.float32)
        earlier = []
        outs = pl.BlockSpec(memory_space=pltpu.VMEM)
    else:
        kernel = functools.partial(last_kernel, low, len(pieces), len(earlier), peers)
        heads = gains.shape[1]
        shapes = [jax.ShapeDtypeStruct((2, heads, size // len(peers)), jnp.float32)] * len(peers)
        held.append(pltpu.VMEM((count, size), jnp.float32))
        outs = [pl.BlockSpec(memory_space=pltpu.VMEM)] * len(peers)
    pairs = count * all_tokens * all_tokens // 2
    return pl.pallas_call(
        kernel,
        out_shape=shapes,
        in_specs=[pl.BlockSpec(memory_space=pltpu.SMEM)]
        + [pl.BlockSpec(memory_space=pltpu.VMEM)] * (1 + len(pieces) + len(earlier)),
        out_specs=outs,
        scratch_shapes=held,
        compiler_params=pltpu.CompilerParams(vmem_limit_bytes=VMEM_LIMIT),
        cost_estimate=pl.CostEstimate(
            flops=6 * pairs * size, bytes_accessed=len(pieces) * count * 4 * tokens * size * 2, transcendentals=pairs
        ),
        name="attend",
    )(units, gains, *pieces, *earlier)


def body(sequence, groups, queries, key_rows, value_rows, out_grad, norm_gains, clip_units):
    arrays = (queries, key_rows, value_rows, out_grad)
    heads = norm_gains.shape[1]
    chunks = head_chunks(heads)
    far = list(range(2, sequence)) or [1]
    near = [flip for flip in range(1, sequence) if flip not in far]

    def send(block, flip):
        return lax.ppermute(block, "seq", [(s, s ^ flip) for s in range(sequence)])

    held = [{} for _ in chunks]
    first = pack(arrays, [(flip, chunks[:1]) for flip in far], heads)
    for flip, block in zip(far, first):
        held[0][flip] = send(block, flip)
    plan = [(flip, chunks[1:]) for flip in far] + [(flip, chunks) for flip in near] + [(0, chunks)]
    blocks = iter(pack(arrays, plan, heads, first[:1]))
    for flip, wanted in plan:
        for bounds in wanted:
            block = next(blocks)
            held[chunks.index(bounds)][flip] = send(block, flip) if flip else block
    sums = []
    for number, (low, _) in enumerate(chunks[:-1]):
        pieces = [held[number][flip] for flip in range(sequence)]
        sums.append(attend(low, clip_units, norm_gains, pieces))
    pieces = [held[-1][flip] for flip in range(sequence)]
    parts = attend(chunks[-1][0], clip_units, norm_gains, pieces, sums, list(range(groups)))
    result = parts[0]
    for flip in range(1, groups):
        result = result + lax.ppermute(parts[flip], "dp", [(g, g ^ flip) for g in range(groups)])
    return result


def solution(mesh):
    return jax.shard_map(
        functools.partial(body, mesh.shape["seq"], mesh.shape["dp"]),
        mesh=mesh,
        in_specs=(
            P(("parts", "dp"), None, "seq", None, None),
            P(("parts", "dp"), None, "seq", None, None),
            P(("parts", "dp"), None, "seq", None, None),
            P(("parts", "dp"), None, "seq", None, None),
            P(None, "seq", None),
            P("parts", None),
        ),
        out_specs=P("parts", "seq", "dp"),
        check_vma=False,
    )
```

```python
import functools
import math

import jax
import jax.numpy as jnp
from jax import lax
from jax.experimental import pallas as pl
from jax.experimental.pallas import tpu as pltpu
from jax.sharding import PartitionSpec as P

MAXCLIP = 3
TILE = 8
EPS = 1e-06
VMEM_LIMIT = 48 * 1024 * 1024
PACK_VMEM_LIMIT = 60 * 1024 * 1024


def head_chunks(heads):
    sizes = {8: (3, 2, 2, 1)}.get(heads)
    if sizes is None:
        sizes = (1,) * heads if heads <= 2 else (heads - heads // 2, heads // 2)
    bounds, start = [], 0
    for size in sizes:
        bounds.append((start, start + size))
        start += size
    return bounds


def pack_kernel(plan, heads, after, *refs):
    arrays = refs[:4]
    outs = refs[4 + after : 4 + after + sum(len(chunks) for _, chunks in plan)]
    token, raw, wide, sems = refs[4 + after + len(outs) :]
    token[...] = jnp.zeros_like(token)
    me = lax.axis_index("seq")
    slots, rows = raw.shape[2], raw.shape[3]
    spans = max(1, heads // TILE)

    def copy(index, array, span, first):
        return pltpu.make_async_copy(
            arrays[array].at[0, :, :, pl.ds(first + span * TILE, TILE), :],
            raw.at[index, array * spans + span],
            sems.at[index, array * spans + span],
        )

    firsts, offsets = [], []
    for flip, _ in plan:
        head = jnp.bitwise_xor(me, flip) * heads
        firsts.append(pl.multiple_of((head // TILE) * TILE, TILE))
        offsets.append(0 if heads % TILE == 0 else lax.rem(head, TILE))
    for index in range(len(plan)):
        for array in range(4):
            for span in range(spans):
                copy(index, array, span, firsts[index]).start()
    place = 0
    for index, (_, chunks) in enumerate(plan):
        for array in range(4):
            for span in range(spans):
                copy(index, array, span, firsts[index]).wait()
                for slot in range(slots):
                    wide[slot] = (
                        raw[index, array * spans + span, slot]
                        .astype(jnp.float32)
                        .reshape(rows * TILE, wide.shape[-1])
                    )
                    for number, (low, high) in enumerate(chunks):
                        for head in range(max(low, span * TILE), min(high, (span + 1) * TILE)):
                            outs[place + number][head - low, array, slot * rows : (slot + 1) * rows, :] = wide[
                                slot, pl.ds(offsets[index] + head - span * TILE, rows, stride=TILE), :
                            ].astype(jnp.bfloat16)
        place += len(chunks)


def pack(arrays, plan, heads, after=()):
    _, slots, rows, _, size = arrays[0].shape
    spans = max(1, heads // TILE)
    shapes = [
        jax.ShapeDtypeStruct((high - low, 4, slots * rows, size), jnp.bfloat16)
        for _, chunks in plan
        for low, high in chunks
    ] + [jax.ShapeDtypeStruct((TILE, size), jnp.float32)]
    count = len(plan)
    moved = count * 4 * spans * slots * rows * TILE * size * 2
    return pl.pallas_call(
        functools.partial(pack_kernel, plan, heads, len(after)),
        out_shape=shapes,
        in_specs=[pl.BlockSpec(memory_space=pltpu.HBM)] * 4 + [pl.BlockSpec(memory_space=pl.ANY)] * len(after),
        out_specs=[pl.BlockSpec(memory_space=pltpu.VMEM)] * len(shapes),
        scratch_shapes=[
            pltpu.VMEM((count, 4 * spans, slots, rows, TILE, size), jnp.bfloat16),
            pltpu.VMEM((slots, rows * TILE, size), jnp.float32),
            pltpu.SemaphoreType.DMA((count, 4 * spans)),
        ],
        compiler_params=pltpu.CompilerParams(vmem_limit_bytes=PACK_VMEM_LIMIT),
        cost_estimate=pl.CostEstimate(flops=moved, bytes_accessed=2 * moved, transcendentals=0),
        name="pack",
    )(*arrays, *after)


def contract_last(left, right):
    return lax.dot_general(left, right, (((1,), (1,)), ((), ())), preferred_element_type=jnp.float32)


def layouts(slots):
    found = []

    def extend(start, clips):
        if start == slots:
            found.append(tuple(clips))
        for span in range(1, min(MAXCLIP, slots - start) + 1):
            extend(start + span, clips + [(start, span)])

    extend(0, [])
    return found


def normalized(block, gain):
    wide = block.astype(jnp.float32)
    wide = wide * lax.rsqrt(jnp.mean(wide * wide, axis=-1, keepdims=True) + EPS)
    return (wide * gain).astype(jnp.bfloat16)


def prepare_kernel(low, after, gains, *refs):
    pieces, out = refs[after:-1], refs[-1]
    heads, _, tokens, _ = pieces[0].shape
    slots = out.shape[2]
    rows = tokens // slots

    for head in range(heads):
        for array in range(4):
            for source, piece in enumerate(pieces):
                block = piece[head, array]
                if array < 2:
                    block = normalized(block, gains[array, low + head : low + head + 1, :])
                for slot in range(slots):
                    out[head, array, slot, source * rows : (source + 1) * rows, :] = block[
                        slot * rows : (slot + 1) * rows
                    ]


def prepare(low, gains, pieces, slots, after):
    heads, _, tokens, size = pieces[0].shape
    moved = len(pieces) * heads * 4 * tokens * size * 2
    return pl.pallas_call(
        functools.partial(prepare_kernel, low, len(after)),
        out_shape=jax.ShapeDtypeStruct((heads, 4, slots, len(pieces) * tokens // slots, size), jnp.bfloat16),
        in_specs=[pl.BlockSpec(memory_space=pltpu.VMEM)] * (1 + len(after) + len(pieces)),
        out_specs=pl.BlockSpec(memory_space=pltpu.VMEM),
        compiler_params=pltpu.CompilerParams(vmem_limit_bytes=VMEM_LIMIT),
        cost_estimate=pl.CostEstimate(flops=1, bytes_accessed=1, transcendentals=0),
        name="prepare",
    )(gains, *after, *pieces)


def attention_chunk(low, count, units, gains, close, pieces, held, total):
    query, key, value, grad = held
    group = lax.axis_index("dp")
    _, _, tokens, size = pieces[0].shape
    slots, near = close.shape[2:4]
    rows = tokens // slots
    unit = near + rows * len(pieces)
    for head in range(count):
        for array, kept in enumerate(held):
            for slot in range(slots):
                kept[head, slot * unit : slot * unit + near, :] = close[head, array, slot]
            for source, piece in enumerate(pieces):
                block = piece[head, array]
                if array < 2:
                    block = normalized(block, gains[array, low + head : low + head + 1, :])
                for slot in range(slots):
                    start = slot * unit + near + source * rows
                    kept[head, start : start + rows, :] = block[slot * rows : (slot + 1) * rows]
    factor = size ** (-0.5) * math.log2(math.e)

    def clip(head, slot, span):
        where = slice(slot * unit, (slot + span) * unit)
        q, k = query[head, where, :], key[head, where, :]
        expo = jnp.exp2(contract_last(k, q) * factor)
        dprob = contract_last(value[head, where, :], grad[head, where, :])
        prob = expo * (1.0 / jnp.sum(expo, axis=0, keepdims=True))
        delta = jnp.sum(prob * dprob, axis=0, keepdims=True)
        dscore = (prob * (dprob - delta)).astype(jnp.bfloat16)
        mixed = jnp.dot(dscore, q, preferred_element_type=jnp.float32)
        return jnp.sum(mixed * k.astype(jnp.float32), axis=0, keepdims=True)

    begins = sum(jnp.where(units[group, slot] > 0, 1 << slot, 0) for slot in range(slots))
    for layout in layouts(slots):

        @pl.when(begins == sum(1 << slot for slot, _ in layout))
        def _():
            for head in range(count):
                total[head : head + 1, :] = sum(clip(head, slot, span) for slot, span in layout)


def chunk_kernel(low, units, gains, close, *refs):
    pieces, out, held = refs[:-5], refs[-5], refs[-4:]
    attention_chunk(low, out.shape[0], units, gains, close, pieces, held, out)


def last_kernel(low, sources, earlier, peers, units, gains, close, *refs):
    pieces = refs[:sources]
    before = refs[sources : sources + earlier]
    outs = refs[sources + earlier : sources + earlier + len(peers)]
    held, total = refs[sources + earlier + len(peers) : -1], refs[-1]
    attention_chunk(low, total.shape[0], units, gains, close, pieces, held, total)
    group = lax.axis_index("dp")
    size = total.shape[-1]
    width = outs[0].shape[-1]
    scaled = jnp.concatenate([ref[...] for ref in before] + [total[...]], axis=0) * (size ** (-0.5))
    for side in range(2):
        grads = scaled / gains[side]
        for out, flip in zip(outs, peers):
            shift = lax.rem(size - jnp.bitwise_xor(group, flip) * width, size)
            out[side] = pltpu.roll(grads, shift, 1)[:, :width]


def attend(low, count, units, gains, close, pieces, earlier=None, peers=None):
    _, _, tokens, size = pieces[0].shape
    all_tokens = close.shape[2] * close.shape[3] + tokens * len(pieces)
    held = [pltpu.VMEM((count, all_tokens, size), jnp.bfloat16)] * 4
    if earlier is None:
        kernel = functools.partial(chunk_kernel, low)
        shapes = jax.ShapeDtypeStruct((count, size), jnp.float32)
        earlier = []
        outs = pl.BlockSpec(memory_space=pltpu.VMEM)
    else:
        kernel = functools.partial(last_kernel, low, len(pieces), len(earlier), peers)
        heads = gains.shape[1]
        shapes = [jax.ShapeDtypeStruct((2, heads, size // len(peers)), jnp.float32)] * len(peers)
        held.append(pltpu.VMEM((count, size), jnp.float32))
        outs = [pl.BlockSpec(memory_space=pltpu.VMEM)] * len(peers)
    pairs = count * all_tokens * all_tokens // 2
    return pl.pallas_call(
        kernel,
        out_shape=shapes,
        in_specs=[pl.BlockSpec(memory_space=pltpu.SMEM)]
        + [pl.BlockSpec(memory_space=pltpu.VMEM)] * (2 + len(pieces) + len(earlier)),
        out_specs=outs,
        scratch_shapes=held,
        compiler_params=pltpu.CompilerParams(vmem_limit_bytes=VMEM_LIMIT),
        cost_estimate=pl.CostEstimate(
            flops=6 * pairs * size, bytes_accessed=len(pieces) * count * 4 * tokens * size * 2, transcendentals=pairs
        ),
        name="attend",
    )(units, gains, close, *pieces, *earlier)


def seen_kernel(*refs):
    refs[-1][...] = jnp.zeros_like(refs[-1])


def seen(blocks):
    return pl.pallas_call(
        seen_kernel,
        out_shape=jax.ShapeDtypeStruct((TILE, blocks[0].shape[-1]), jnp.float32),
        in_specs=[pl.BlockSpec(memory_space=pl.ANY)] * len(blocks),
        out_specs=pl.BlockSpec(memory_space=pltpu.VMEM),
        compiler_params=pltpu.CompilerParams(vmem_limit_bytes=1024 * 1024),
        cost_estimate=pl.CostEstimate(flops=1, bytes_accessed=1024 * 1024, transcendentals=0),
        name="seen",
    )(*blocks)


def body(sequence, groups, queries, key_rows, value_rows, out_grad, norm_gains, clip_units):
    arrays = (queries, key_rows, value_rows, out_grad)
    heads = norm_gains.shape[1]
    chunks = head_chunks(heads)
    far = list(range(2, sequence)) or [1]
    near = [flip for flip in range(1, sequence) if flip not in far]

    def send(block, flip):
        return lax.ppermute(block, "seq", [(s, s ^ flip) for s in range(sequence)])

    slots = clip_units.shape[1]
    close = near + [0]

    def pack_and_send(number, after):
        plan = [(flip, [chunks[number]]) for flip in far]
        if number == 1:
            plan += [(flip, chunks) for flip in close]
        *blocks, token = pack(arrays, plan, heads, after)
        received.append([send(block, flip) for flip, block in zip(far, blocks)])
        return blocks[len(far) :], token

    received, sums = [], []
    _, token = pack_and_send(0, [])
    rest, _ = pack_and_send(1, [token])
    for number, (low, high) in enumerate(chunks):
        if 0 < number < len(chunks) - 1:
            pack_and_send(number + 1, sums[number - 1 :])
        pieces = [
            send(block, flip) if flip else block for flip, block in zip(close, rest[number :: len(chunks)])
        ]
        after = [seen(received[0])] if number == 0 else []
        prepared = prepare(low, norm_gains, pieces, slots, after)
        if number + 1 < len(chunks):
            sums.append(attend(low, high - low, clip_units, norm_gains, prepared, received[number]))
    parts = attend(low, high - low, clip_units, norm_gains, prepared, received[-1], sums, list(range(groups)))
    result = parts[0]
    for flip in range(1, groups):
        result = result + lax.ppermute(parts[flip], "dp", [(g, g ^ flip) for g in range(groups)])
    return result


def solution(mesh):
    return jax.shard_map(
        functools.partial(body, mesh.shape["seq"], mesh.shape["dp"]),
        mesh=mesh,
        in_specs=(
            P(("parts", "dp"), None, "seq", None, None),
            P(("parts", "dp"), None, "seq", None, None),
            P(("parts", "dp"), None, "seq", None, None),
            P(("parts", "dp"), None, "seq", None, None),
            P(None, "seq", None),
            P("parts", None),
        ),
        out_specs=P("parts", "seq", "dp"),
        check_vma=False,
    )
```

```python
import functools
import math

import jax
import jax.numpy as jnp
from jax import lax
from jax.experimental import pallas as pl
from jax.experimental.pallas import tpu as pltpu
from jax.sharding import PartitionSpec as P

MAXCLIP = 3
VALUES = 2
OTHERS = (0, 1, 3)
TILE = 8
EPS = 1e-06
VMEM_LIMIT = 48 * 1024 * 1024
PACK_VMEM_LIMIT = 60 * 1024 * 1024


def head_chunks(heads):
    sizes = {8: (4, 3, 1)}.get(heads)
    if sizes is None:
        sizes = (1,) * heads if heads <= 2 else (heads - heads // 2, heads // 2)
    bounds, start = [], 0
    for size in sizes:
        bounds.append((start, start + size))
        start += size
    return bounds


def tile_start(heads, flip):
    head = jnp.bitwise_xor(lax.axis_index("seq"), flip) * heads
    offset = 0 if heads % TILE == 0 else lax.rem(head, TILE)
    return pl.multiple_of((head // TILE) * TILE, TILE), offset


def cut_kernel(flips, heads, array, *refs):
    outs, token, sems = refs[:-2], refs[-2], refs[-1]
    token[...] = jnp.zeros_like(token)
    copies = []
    for index, flip in enumerate(flips):
        start, _ = tile_start(heads, flip)
        source = array.at[0, :, :, pl.ds(start, outs[index].shape[2]), :]
        copies.append(pltpu.make_async_copy(source, outs[index], sems.at[index]))
        copies[-1].start()
    for copy in copies:
        copy.wait()


def cut(array, flips, heads):
    _, slots, rows, _, size = array.shape
    shape = jax.ShapeDtypeStruct((slots, rows, max(heads, TILE), size), array.dtype)
    return pl.pallas_call(
        functools.partial(cut_kernel, flips, heads),
        out_shape=[shape] * len(flips) + [jax.ShapeDtypeStruct((TILE, size), jnp.float32)],
        in_specs=[pl.BlockSpec(memory_space=pltpu.HBM)],
        out_specs=[pl.BlockSpec(memory_space=pltpu.HBM)] * len(flips) + [pl.BlockSpec(memory_space=pltpu.VMEM)],
        scratch_shapes=[pltpu.SemaphoreType.DMA((len(flips),))],
        compiler_params=pltpu.CompilerParams(vmem_limit_bytes=PACK_VMEM_LIMIT),
        name="cut",
    )(array)


def arrange_kernel(*refs):
    pieces, out, wide = refs[:-2], refs[-2], refs[-1]
    heads, slots = out.shape[:2]
    rows, held = pieces[0].shape[1:3]
    _, offset = tile_start(heads, 0)
    for source, piece in enumerate(pieces):
        for slot in range(slots):
            for span in range(held // TILE):
                place = (source * slots + slot) % wide.shape[0]
                block = piece[slot, :, span * TILE : (span + 1) * TILE, :]
                wide[place] = block.astype(jnp.float32).reshape(rows * TILE, wide.shape[-1])
                for head in range(span * TILE, min(heads, (span + 1) * TILE)):
                    out[head, slot, source * rows : (source + 1) * rows, :] = wide[
                        place, pl.ds(offset + head - span * TILE, rows, stride=TILE), :
                    ].astype(jnp.bfloat16)


def arrange(pieces, heads):
    slots, rows, held, size = pieces[0].shape
    moved = len(pieces) * slots * rows * held * size * 2
    return pl.pallas_call(
        arrange_kernel,
        out_shape=jax.ShapeDtypeStruct((heads, slots, len(pieces) * rows, size), jnp.bfloat16),
        in_specs=[pl.BlockSpec(memory_space=pltpu.VMEM)] * len(pieces),
        out_specs=pl.BlockSpec(memory_space=pltpu.VMEM),
        scratch_shapes=[pltpu.VMEM((slots, rows * TILE, size), jnp.float32)],
        compiler_params=pltpu.CompilerParams(vmem_limit_bytes=VMEM_LIMIT),
        cost_estimate=pl.CostEstimate(flops=moved, bytes_accessed=2 * moved, transcendentals=0),
        name="arrange",
    )(*pieces)


def pack_kernel(plan, heads, after, *refs):
    arrays = refs[:4]
    outs = refs[4 + after : 4 + after + sum(len(chunks) for _, _, chunks in plan)]
    token, raw, wide, sems = refs[4 + after + len(outs) :]
    token[...] = jnp.zeros_like(token)
    slots, rows = raw.shape[2], raw.shape[3]
    spans = max(1, heads // TILE)

    def copy(index, array, span, first):
        return pltpu.make_async_copy(
            arrays[array].at[0, :, :, pl.ds(first + span * TILE, TILE), :],
            raw.at[index, array * spans + span],
            sems.at[index, array * spans + span],
        )

    firsts, offsets = zip(*[tile_start(heads, flip) for flip, _, _ in plan])
    for index, (_, wanted, _) in enumerate(plan):
        for array in wanted:
            for span in range(spans):
                copy(index, array, span, firsts[index]).start()
    place = 0
    for index, (_, wanted, chunks) in enumerate(plan):
        for position, array in enumerate(wanted):
            for span in range(spans):
                copy(index, array, span, firsts[index]).wait()
                for slot in range(slots):
                    wide[slot] = (
                        raw[index, array * spans + span, slot]
                        .astype(jnp.float32)
                        .reshape(rows * TILE, wide.shape[-1])
                    )
                    for number, (low, high) in enumerate(chunks):
                        for head in range(max(low, span * TILE), min(high, (span + 1) * TILE)):
                            outs[place + number][head - low, position, slot * rows : (slot + 1) * rows, :] = wide[
                                slot, pl.ds(offsets[index] + head - span * TILE, rows, stride=TILE), :
                            ].astype(jnp.bfloat16)
        place += len(chunks)


def pack(arrays, plan, heads, after=()):
    _, slots, rows, _, size = arrays[0].shape
    spans = max(1, heads // TILE)
    shapes = [
        jax.ShapeDtypeStruct((high - low, len(wanted), slots * rows, size), jnp.bfloat16)
        for _, wanted, chunks in plan
        for low, high in chunks
    ] + [jax.ShapeDtypeStruct((TILE, size), jnp.float32)]
    count = len(plan)
    moved = count * 4 * spans * slots * rows * TILE * size * 2
    return pl.pallas_call(
        functools.partial(pack_kernel, plan, heads, len(after)),
        out_shape=shapes,
        in_specs=[pl.BlockSpec(memory_space=pltpu.HBM)] * 4 + [pl.BlockSpec(memory_space=pl.ANY)] * len(after),
        out_specs=[pl.BlockSpec(memory_space=pltpu.VMEM)] * len(shapes),
        scratch_shapes=[
            pltpu.VMEM((count, 4 * spans, slots, rows, TILE, size), jnp.bfloat16),
            pltpu.VMEM((slots, rows * TILE, size), jnp.float32),
            pltpu.SemaphoreType.DMA((count, 4 * spans)),
        ],
        compiler_params=pltpu.CompilerParams(vmem_limit_bytes=PACK_VMEM_LIMIT),
        cost_estimate=pl.CostEstimate(flops=moved, bytes_accessed=2 * moved, transcendentals=0),
        name="pack",
    )(*arrays, *after)


def contract_last(left, right):
    return lax.dot_general(left, right, (((1,), (1,)), ((), ())), preferred_element_type=jnp.float32)


def layouts(slots):
    found = []

    def extend(start, clips):
        if start == slots:
            found.append(tuple(clips))
        for span in range(1, min(MAXCLIP, slots - start) + 1):
            extend(start + span, clips + [(start, span)])

    extend(0, [])
    return found


def normalized(block, gain):
    wide = block.astype(jnp.float32)
    wide = wide * lax.rsqrt(jnp.mean(wide * wide, axis=-1, keepdims=True) + EPS)
    return (wide * gain).astype(jnp.bfloat16)


def prepare_kernel(low, after, gains, *refs):
    pieces, out = refs[after:-1], refs[-1]
    heads, _, tokens, _ = pieces[0].shape
    slots = out.shape[2]
    rows = tokens // slots
    for head in range(heads):
        for array in range(4):
            for source, piece in enumerate(pieces[array // 2 :: 2]):
                block = piece[head, array % 2]
                if array < 2:
                    block = normalized(block, gains[array, low + head : low + head + 1, :])
                for slot in range(slots):
                    out[head, array, slot, source * rows : (source + 1) * rows, :] = block[
                        slot * rows : (slot + 1) * rows
                    ]


def prepare(low, gains, pieces, slots, after):
    heads, _, tokens, size = pieces[0].shape
    moved = len(pieces) * heads * 2 * tokens * size * 2
    return pl.pallas_call(
        functools.partial(prepare_kernel, low, len(after)),
        out_shape=jax.ShapeDtypeStruct((heads, 4, slots, len(pieces) // 2 * tokens // slots, size), jnp.bfloat16),
        in_specs=[pl.BlockSpec(memory_space=pltpu.VMEM)] * (1 + len(after) + len(pieces)),
        out_specs=pl.BlockSpec(memory_space=pltpu.VMEM),
        compiler_params=pltpu.CompilerParams(vmem_limit_bytes=VMEM_LIMIT),
        cost_estimate=pl.CostEstimate(flops=1, bytes_accessed=1, transcendentals=0),
        name="prepare",
    )(gains, *after, *pieces)


def attention_chunk(low, count, units, gains, values, close, pieces, held, total):
    query, key, value, grad = held
    group = lax.axis_index("dp")
    _, _, tokens, size = pieces[0].shape
    slots, near = close.shape[2:4]
    rows = tokens // slots
    unit = near + rows * len(pieces)
    for head in range(count):
        for array, kept in enumerate(held):
            for slot in range(slots):
                kept[head, slot * unit : slot * unit + near, :] = close[head, array, slot]
                if array == VALUES:
                    kept[head, slot * unit + near : (slot + 1) * unit, :] = values[low + head, slot]
            if array == VALUES:
                continue
            for source, piece in enumerate(pieces):
                block = piece[head, OTHERS.index(array)]
                if array < 2:
                    block = normalized(block, gains[array, low + head : low + head + 1, :])
                for slot in range(slots):
                    start = slot * unit + near + source * rows
                    kept[head, start : start + rows, :] = block[slot * rows : (slot + 1) * rows]
    factor = size ** (-0.5) * math.log2(math.e)

    def clip(head, slot, span):
        where = slice(slot * unit, (slot + span) * unit)
        q, k = query[head, where, :], key[head, where, :]
        expo = jnp.exp2(contract_last(k, q) * factor)
        dprob = contract_last(value[head, where, :], grad[head, where, :])
        prob = expo * (1.0 / jnp.sum(expo, axis=0, keepdims=True))
        delta = jnp.sum(prob * dprob, axis=0, keepdims=True)
        dscore = (prob * (dprob - delta)).astype(jnp.bfloat16)
        mixed = jnp.dot(dscore, q, preferred_element_type=jnp.float32)
        return jnp.sum(mixed * k.astype(jnp.float32), axis=0, keepdims=True)

    begins = sum(jnp.where(units[group, slot] > 0, 1 << slot, 0) for slot in range(slots))
    for layout in layouts(slots):

        @pl.when(begins == sum(1 << slot for slot, _ in layout))
        def _():
            for head in range(count):
                total[head : head + 1, :] = sum(clip(head, slot, span) for slot, span in layout)


def chunk_kernel(low, units, gains, values, close, *refs):
    pieces, out, held = refs[:-5], refs[-5], refs[-4:]
    attention_chunk(low, out.shape[0], units, gains, values, close, pieces, held, out)


def last_kernel(low, sources, earlier, peers, units, gains, values, close, *refs):
    pieces = refs[:sources]
    before = refs[sources : sources + earlier]
    outs = refs[sources + earlier : sources + earlier + len(peers)]
    held, total = refs[sources + earlier + len(peers) : -1], refs[-1]
    attention_chunk(low, total.shape[0], units, gains, values, close, pieces, held, total)
    group = lax.axis_index("dp")
    size = total.shape[-1]
    width = outs[0].shape[-1]
    scaled = jnp.concatenate([ref[...] for ref in before] + [total[...]], axis=0) * (size ** (-0.5))
    for side in range(2):
        grads = scaled / gains[side]
        for out, flip in zip(outs, peers):
            shift = lax.rem(size - jnp.bitwise_xor(group, flip) * width, size)
            out[side] = pltpu.roll(grads, shift, 1)[:, :width]


def attend(low, count, units, gains, values, close, pieces, earlier=None, peers=None):
    _, _, tokens, size = pieces[0].shape
    all_tokens = close.shape[2] * close.shape[3] + tokens * len(pieces)
    held = [pltpu.VMEM((count, all_tokens, size), jnp.bfloat16)] * 4
    if earlier is None:
        kernel = functools.partial(chunk_kernel, low)
        shapes = jax.ShapeDtypeStruct((count, size), jnp.float32)
        earlier = []
        outs = pl.BlockSpec(memory_space=pltpu.VMEM)
    else:
        kernel = functools.partial(last_kernel, low, len(pieces), len(earlier), peers)
        heads = gains.shape[1]
        shapes = [jax.ShapeDtypeStruct((2, heads, size // len(peers)), jnp.float32)] * len(peers)
        held.append(pltpu.VMEM((count, size), jnp.float32))
        outs = [pl.BlockSpec(memory_space=pltpu.VMEM)] * len(peers)
    pairs = count * all_tokens * all_tokens // 2
    return pl.pallas_call(
        kernel,
        out_shape=shapes,
        in_specs=[pl.BlockSpec(memory_space=pltpu.SMEM)]
        + [pl.BlockSpec(memory_space=pltpu.VMEM)] * (3 + len(pieces) + len(earlier)),
        out_specs=outs,
        scratch_shapes=held,
        compiler_params=pltpu.CompilerParams(vmem_limit_bytes=VMEM_LIMIT),
        cost_estimate=pl.CostEstimate(
            flops=6 * pairs * size, bytes_accessed=len(pieces) * count * 4 * tokens * size * 2, transcendentals=pairs
        ),
        name="attend",
    )(units, gains, values, close, *pieces, *earlier)


def seen_kernel(*refs):
    refs[-1][...] = jnp.zeros_like(refs[-1])


def seen(blocks):
    return pl.pallas_call(
        seen_kernel,
        out_shape=jax.ShapeDtypeStruct((TILE, blocks[0].shape[-1]), jnp.float32),
        in_specs=[pl.BlockSpec(memory_space=pl.ANY)] * len(blocks),
        out_specs=pl.BlockSpec(memory_space=pltpu.VMEM),
        compiler_params=pltpu.CompilerParams(vmem_limit_bytes=1024 * 1024),
        cost_estimate=pl.CostEstimate(flops=1, bytes_accessed=1024 * 1024, transcendentals=0),
        name="seen",
    )(*blocks)


def body(sequence, groups, queries, key_rows, value_rows, out_grad, norm_gains, clip_units):
    arrays = (queries, key_rows, value_rows, out_grad)
    heads = norm_gains.shape[1]
    chunks = head_chunks(heads)
    far = list(range(2, sequence)) or [1]
    near = [flip for flip in range(1, sequence) if flip not in far]

    def send(block, flip):
        return lax.ppermute(block, "seq", [(s, s ^ flip) for s in range(sequence)])

    slots = clip_units.shape[1]
    close = near + [0]

    def pack_and_send(plan, after):
        *blocks, token = pack(arrays, plan, heads, after)
        flips = [flip for flip, _, wanted in plan for _ in wanted]
        return [send(block, flip) if flip else block for flip, block in zip(flips, blocks)], token

    def far_plan(number):
        return [(flip, OTHERS, chunks[number : number + 1]) for flip in far]

    *tiles, token = cut(arrays[VALUES], far, heads)
    tiles = [send(block, flip) for flip, block in zip(far, tiles)]
    received, token = pack_and_send(far_plan(0), [token])
    later = far_plan(1) if len(chunks) > 1 else []
    whole = [(flip, pair, chunks) for flip in close for pair in ((0, 1), (2, 3))]
    blocks, _ = pack_and_send(later + whole, [token, seen(tiles)])
    values = arrange(tiles, heads)
    prepared = [
        prepare(low, norm_gains, blocks[len(later) + number :: len(chunks)], slots, [] if number else [seen(received)])
        for number, (low, _) in enumerate(chunks)
    ]
    waiting, sums = blocks[: len(later)], []
    for number, (low, high) in enumerate(chunks[:-1]):
        sums.append(attend(low, high - low, clip_units, norm_gains, values, prepared[number], received))
        received = waiting
        if number + 2 < len(chunks):
            waiting, _ = pack_and_send(far_plan(number + 2), sums[-1:])
    low, high = chunks[-1]
    parts = attend(
        low, high - low, clip_units, norm_gains, values, prepared[-1], received, sums, list(range(groups))
    )
    result = parts[0]
    for flip in range(1, groups):
        result = result + lax.ppermute(parts[flip], "dp", [(g, g ^ flip) for g in range(groups)])
    return result


def solution(mesh):
    return jax.shard_map(
        functools.partial(body, mesh.shape["seq"], mesh.shape["dp"]),
        mesh=mesh,
        in_specs=(
            P(("parts", "dp"), None, "seq", None, None),
            P(("parts", "dp"), None, "seq", None, None),
            P(("parts", "dp"), None, "seq", None, None),
            P(("parts", "dp"), None, "seq", None, None),
            P(None, "seq", None),
            P("parts", None),
        ),
        out_specs=P("parts", "seq", "dp"),
        check_vma=False,
    )
```

```python
import functools
import math

import jax
import jax.numpy as jnp
from jax import lax
from jax.experimental import pallas as pl
from jax.experimental.pallas import tpu as pltpu
from jax.sharding import PartitionSpec as P

MAXCLIP = 3
VALUES = 2
OTHERS = (0, 1, 3)
TILE = 8
EPS = 1e-06
VMEM_LIMIT = 48 * 1024 * 1024
PACK_VMEM_LIMIT = 53 * 1024 * 1024


def head_chunks(heads):
    sizes = {8: (4, 3, 1)}.get(heads)
    if sizes is None:
        sizes = (1,) * heads if heads <= 2 else (heads - heads // 2, heads // 2)
    bounds, start = [], 0
    for size in sizes:
        bounds.append((start, start + size))
        start += size
    return bounds


def tile_start(heads, flip):
    head = jnp.bitwise_xor(lax.axis_index("seq"), flip) * heads
    offset = 0 if heads % TILE == 0 else lax.rem(head, TILE)
    return pl.multiple_of((head // TILE) * TILE, TILE), offset


def cut_kernel(flips, heads, array, *refs):
    outs, token, sems = refs[:-2], refs[-2], refs[-1]
    token[...] = jnp.zeros_like(token)
    copies = []
    for index, flip in enumerate(flips):
        start, _ = tile_start(heads, flip)
        source = array.at[0, :, :, pl.ds(start, outs[index].shape[2]), :]
        copies.append(pltpu.make_async_copy(source, outs[index], sems.at[index]))
        copies[-1].start()
    for copy in copies:
        copy.wait()


def cut(array, flips, heads):
    _, slots, rows, _, size = array.shape
    shape = jax.ShapeDtypeStruct((slots, rows, max(heads, TILE), size), array.dtype)
    return pl.pallas_call(
        functools.partial(cut_kernel, flips, heads),
        out_shape=[shape] * len(flips) + [jax.ShapeDtypeStruct((TILE, size), jnp.float32)],
        in_specs=[pl.BlockSpec(memory_space=pltpu.HBM)],
        out_specs=[pl.BlockSpec(memory_space=pltpu.VMEM)] * (len(flips) + 1),
        scratch_shapes=[pltpu.SemaphoreType.DMA((len(flips),))],
        compiler_params=pltpu.CompilerParams(vmem_limit_bytes=PACK_VMEM_LIMIT),
        name="cut",
    )(array)


def arrange_kernel(*refs):
    pieces, out, wide = refs[:-2], refs[-2], refs[-1]
    heads, slots = out.shape[:2]
    rows, held = pieces[0].shape[1:3]
    _, offset = tile_start(heads, 0)
    for source, piece in enumerate(pieces):
        for slot in range(slots):
            for span in range(held // TILE):
                place = (source * slots + slot) % wide.shape[0]
                block = piece[slot, :, span * TILE : (span + 1) * TILE, :]
                wide[place] = block.astype(jnp.float32).reshape(rows * TILE, wide.shape[-1])
                for head in range(span * TILE, min(heads, (span + 1) * TILE)):
                    out[head, slot, source * rows : (source + 1) * rows, :] = wide[
                        place, pl.ds(offset + head - span * TILE, rows, stride=TILE), :
                    ].astype(jnp.bfloat16)


def arrange(pieces, heads):
    slots, rows, held, size = pieces[0].shape
    moved = len(pieces) * slots * rows * held * size * 2
    return pl.pallas_call(
        arrange_kernel,
        out_shape=jax.ShapeDtypeStruct((heads, slots, len(pieces) * rows, size), jnp.bfloat16),
        in_specs=[pl.BlockSpec(memory_space=pltpu.VMEM)] * len(pieces),
        out_specs=pl.BlockSpec(memory_space=pltpu.VMEM),
        scratch_shapes=[pltpu.VMEM((slots, rows * TILE, size), jnp.float32)],
        compiler_params=pltpu.CompilerParams(vmem_limit_bytes=VMEM_LIMIT),
        cost_estimate=pl.CostEstimate(flops=moved, bytes_accessed=2 * moved, transcendentals=0),
        name="arrange",
    )(*pieces)


def pack_kernel(plan, heads, after, *refs):
    arrays = refs[:4]
    outs = refs[4 + after : 4 + after + sum(len(chunks) for _, _, chunks in plan)]
    token, raw, wide, sems = refs[4 + after + len(outs) :]
    token[...] = jnp.zeros_like(token)
    slots, rows = raw.shape[2], raw.shape[3]
    spans = max(1, heads // TILE)

    def copy(index, array, span, first):
        return pltpu.make_async_copy(
            arrays[array].at[0, :, :, pl.ds(first + span * TILE, TILE), :],
            raw.at[index, array * spans + span],
            sems.at[index, array * spans + span],
        )

    firsts, offsets = zip(*[tile_start(heads, flip) for flip, _, _ in plan])
    for index, (_, wanted, _) in enumerate(plan):
        for array in wanted:
            for span in range(spans):
                copy(index, array, span, firsts[index]).start()
    place = 0
    for index, (_, wanted, chunks) in enumerate(plan):
        for position, array in enumerate(wanted):
            for span in range(spans):
                copy(index, array, span, firsts[index]).wait()
                for slot in range(slots):
                    wide[slot] = (
                        raw[index, array * spans + span, slot]
                        .astype(jnp.float32)
                        .reshape(rows * TILE, wide.shape[-1])
                    )
                    for number, (low, high) in enumerate(chunks):
                        for head in range(max(low, span * TILE), min(high, (span + 1) * TILE)):
                            outs[place + number][head - low, position, slot * rows : (slot + 1) * rows, :] = wide[
                                slot, pl.ds(offsets[index] + head - span * TILE, rows, stride=TILE), :
                            ].astype(jnp.bfloat16)
        place += len(chunks)


def pack(arrays, plan, heads, after=()):
    _, slots, rows, _, size = arrays[0].shape
    spans = max(1, heads // TILE)
    shapes = [
        jax.ShapeDtypeStruct((high - low, len(wanted), slots * rows, size), jnp.bfloat16)
        for _, wanted, chunks in plan
        for low, high in chunks
    ] + [jax.ShapeDtypeStruct((TILE, size), jnp.float32)]
    count = len(plan)
    moved = count * 4 * spans * slots * rows * TILE * size * 2
    return pl.pallas_call(
        functools.partial(pack_kernel, plan, heads, len(after)),
        out_shape=shapes,
        in_specs=[pl.BlockSpec(memory_space=pltpu.HBM)] * 4 + [pl.BlockSpec(memory_space=pl.ANY)] * len(after),
        out_specs=[pl.BlockSpec(memory_space=pltpu.VMEM)] * len(shapes),
        scratch_shapes=[
            pltpu.VMEM((count, 4 * spans, slots, rows, TILE, size), jnp.bfloat16),
            pltpu.VMEM((slots, rows * TILE, size), jnp.float32),
            pltpu.SemaphoreType.DMA((count, 4 * spans)),
        ],
        compiler_params=pltpu.CompilerParams(vmem_limit_bytes=PACK_VMEM_LIMIT),
        cost_estimate=pl.CostEstimate(flops=moved, bytes_accessed=2 * moved, transcendentals=0),
        name="pack",
    )(*arrays, *after)


def contract_last(left, right):
    return lax.dot_general(left, right, (((1,), (1,)), ((), ())), preferred_element_type=jnp.float32)


def layouts(slots):
    found = []

    def extend(start, clips):
        if start == slots:
            found.append(tuple(clips))
        for span in range(1, min(MAXCLIP, slots - start) + 1):
            extend(start + span, clips + [(start, span)])

    extend(0, [])
    return found


def normalized(block, gain):
    wide = block.astype(jnp.float32)
    wide = wide * lax.rsqrt(jnp.mean(wide * wide, axis=-1, keepdims=True) + EPS)
    return (wide * gain).astype(jnp.bfloat16)


def prepare_kernel(low, after, gains, *refs):
    pieces, out = refs[after:-1], refs[-1]
    heads, _, tokens, _ = pieces[0].shape
    slots = out.shape[2]
    rows = tokens // slots
    for head in range(heads):
        for array in range(4):
            for source, piece in enumerate(pieces[array // 2 :: 2]):
                block = piece[head, array % 2]
                if array < 2:
                    block = normalized(block, gains[array, low + head : low + head + 1, :])
                for slot in range(slots):
                    out[head, array, slot, source * rows : (source + 1) * rows, :] = block[
                        slot * rows : (slot + 1) * rows
                    ]


def prepare(low, gains, pieces, slots, after):
    heads, _, tokens, size = pieces[0].shape
    moved = len(pieces) * heads * 2 * tokens * size * 2
    return pl.pallas_call(
        functools.partial(prepare_kernel, low, len(after)),
        out_shape=jax.ShapeDtypeStruct((heads, 4, slots, len(pieces) // 2 * tokens // slots, size), jnp.bfloat16),
        in_specs=[pl.BlockSpec(memory_space=pltpu.VMEM)] * (1 + len(after) + len(pieces)),
        out_specs=pl.BlockSpec(memory_space=pltpu.VMEM),
        compiler_params=pltpu.CompilerParams(vmem_limit_bytes=VMEM_LIMIT),
        cost_estimate=pl.CostEstimate(flops=1, bytes_accessed=1, transcendentals=0),
        name="prepare",
    )(gains, *after, *pieces)


def attention_chunk(low, count, units, gains, values, close, pieces, held, total):
    query, key, value, grad = held
    group = lax.axis_index("dp")
    _, _, tokens, size = pieces[0].shape
    slots, near = close.shape[2:4]
    rows = tokens // slots
    unit = near + rows * len(pieces)
    for head in range(count):
        for array, kept in enumerate(held):
            for slot in range(slots):
                kept[head, slot * unit : slot * unit + near, :] = close[head, array, slot]
                if array == VALUES:
                    kept[head, slot * unit + near : (slot + 1) * unit, :] = values[low + head, slot]
            if array == VALUES:
                continue
            for source, piece in enumerate(pieces):
                block = piece[head, OTHERS.index(array)]
                if array < 2:
                    block = normalized(block, gains[array, low + head : low + head + 1, :])
                for slot in range(slots):
                    start = slot * unit + near + source * rows
                    kept[head, start : start + rows, :] = block[slot * rows : (slot + 1) * rows]
    factor = size ** (-0.5) * math.log2(math.e)

    def clip(head, slot, span):
        where = slice(slot * unit, (slot + span) * unit)
        q, k = query[head, where, :], key[head, where, :]
        expo = jnp.exp2(contract_last(k, q) * factor)
        dprob = contract_last(value[head, where, :], grad[head, where, :])
        prob = expo * (1.0 / jnp.sum(expo, axis=0, keepdims=True))
        delta = jnp.sum(prob * dprob, axis=0, keepdims=True)
        dscore = (prob * (dprob - delta)).astype(jnp.bfloat16)
        mixed = jnp.dot(dscore, q, preferred_element_type=jnp.float32)
        return jnp.sum(mixed * k.astype(jnp.float32), axis=0, keepdims=True)

    begins = sum(jnp.where(units[group, slot] > 0, 1 << slot, 0) for slot in range(slots))
    for layout in layouts(slots):

        @pl.when(begins == sum(1 << slot for slot, _ in layout))
        def _():
            for head in range(count):
                total[head : head + 1, :] = sum(clip(head, slot, span) for slot, span in layout)


def chunk_kernel(low, units, gains, values, close, *refs):
    pieces, out, held = refs[:-5], refs[-5], refs[-4:]
    attention_chunk(low, out.shape[0], units, gains, values, close, pieces, held, out)


def last_kernel(low, sources, earlier, peers, units, gains, values, close, *refs):
    pieces = refs[:sources]
    before = refs[sources : sources + earlier]
    outs = refs[sources + earlier : sources + earlier + len(peers)]
    held, total = refs[sources + earlier + len(peers) : -1], refs[-1]
    attention_chunk(low, total.shape[0], units, gains, values, close, pieces, held, total)
    group = lax.axis_index("dp")
    size = total.shape[-1]
    width = outs[0].shape[-1]
    scaled = jnp.concatenate([ref[...] for ref in before] + [total[...]], axis=0) * (size ** (-0.5))
    for side in range(2):
        grads = scaled / gains[side]
        for out, flip in zip(outs, peers):
            shift = lax.rem(size - jnp.bitwise_xor(group, flip) * width, size)
            out[side] = pltpu.roll(grads, shift, 1)[:, :width]


def attend(low, count, units, gains, values, close, pieces, earlier=None, peers=None):
    _, _, tokens, size = pieces[0].shape
    all_tokens = close.shape[2] * close.shape[3] + tokens * len(pieces)
    held = [pltpu.VMEM((count, all_tokens, size), jnp.bfloat16)] * 4
    if earlier is None:
        kernel = functools.partial(chunk_kernel, low)
        shapes = jax.ShapeDtypeStruct((count, size), jnp.float32)
        earlier = []
        outs = pl.BlockSpec(memory_space=pltpu.VMEM)
    else:
        kernel = functools.partial(last_kernel, low, len(pieces), len(earlier), peers)
        heads = gains.shape[1]
        shapes = [jax.ShapeDtypeStruct((2, heads, size // len(peers)), jnp.float32)] * len(peers)
        held.append(pltpu.VMEM((count, size), jnp.float32))
        outs = [pl.BlockSpec(memory_space=pltpu.VMEM)] * len(peers)
    pairs = count * all_tokens * all_tokens // 2
    return pl.pallas_call(
        kernel,
        out_shape=shapes,
        in_specs=[pl.BlockSpec(memory_space=pltpu.SMEM)]
        + [pl.BlockSpec(memory_space=pltpu.VMEM)] * (3 + len(pieces) + len(earlier)),
        out_specs=outs,
        scratch_shapes=held,
        compiler_params=pltpu.CompilerParams(vmem_limit_bytes=VMEM_LIMIT),
        cost_estimate=pl.CostEstimate(
            flops=6 * pairs * size, bytes_accessed=len(pieces) * count * 4 * tokens * size * 2, transcendentals=pairs
        ),
        name="attend",
    )(units, gains, values, close, *pieces, *earlier)


def seen_kernel(*refs):
    refs[-1][...] = jnp.zeros_like(refs[-1])


def seen(blocks):
    return pl.pallas_call(
        seen_kernel,
        out_shape=jax.ShapeDtypeStruct((TILE, blocks[0].shape[-1]), jnp.float32),
        in_specs=[pl.BlockSpec(memory_space=pl.ANY)] * len(blocks),
        out_specs=pl.BlockSpec(memory_space=pltpu.VMEM),
        compiler_params=pltpu.CompilerParams(vmem_limit_bytes=1024 * 1024),
        cost_estimate=pl.CostEstimate(flops=1, bytes_accessed=1024 * 1024, transcendentals=0),
        name="seen",
    )(*blocks)


def body(sequence, groups, queries, key_rows, value_rows, out_grad, norm_gains, clip_units):
    arrays = (queries, key_rows, value_rows, out_grad)
    heads = norm_gains.shape[1]
    chunks = head_chunks(heads)
    far = list(range(2, sequence)) or [1]
    near = [flip for flip in range(1, sequence) if flip not in far]

    def send(block, flip):
        return lax.ppermute(block, "seq", [(s, s ^ flip) for s in range(sequence)])

    slots = clip_units.shape[1]
    close = near + [0]

    def pack_and_send(plan, after):
        *blocks, token = pack(arrays, plan, heads, after)
        flips = [flip for flip, _, wanted in plan for _ in wanted]
        return [send(block, flip) if flip else block for flip, block in zip(flips, blocks)], token

    def far_plan(number):
        return [(flip, OTHERS, chunks[number : number + 1]) for flip in far]

    *tiles, token = cut(arrays[VALUES], far, heads)
    tiles = [send(block, flip) for flip, block in zip(far, tiles)]
    received, token = pack_and_send(far_plan(0), [token])
    later = far_plan(1) if len(chunks) > 1 else []
    whole = [(flip, pair, chunks) for flip in close for pair in ((0, 1), (2, 3))]
    blocks, _ = pack_and_send(later + whole, [token, seen(tiles)])
    values = arrange(tiles, heads)
    prepared = [
        prepare(low, norm_gains, blocks[len(later) + number :: len(chunks)], slots, [] if number else [seen(received)])
        for number, (low, _) in enumerate(chunks)
    ]
    waiting, sums = blocks[: len(later)], []
    for number, (low, high) in enumerate(chunks[:-1]):
        sums.append(attend(low, high - low, clip_units, norm_gains, values, prepared[number], received))
        received = waiting
        if number + 2 < len(chunks):
            waiting, _ = pack_and_send(far_plan(number + 2), sums[-1:])
    low, high = chunks[-1]
    parts = attend(
        low, high - low, clip_units, norm_gains, values, prepared[-1], received, sums, list(range(groups))
    )
    result = parts[0]
    for flip in range(1, groups):
        result = result + lax.ppermute(parts[flip], "dp", [(g, g ^ flip) for g in range(groups)])
    return result


def solution(mesh):
    return jax.shard_map(
        functools.partial(body, mesh.shape["seq"], mesh.shape["dp"]),
        mesh=mesh,
        in_specs=(
            P(("parts", "dp"), None, "seq", None, None),
            P(("parts", "dp"), None, "seq", None, None),
            P(("parts", "dp"), None, "seq", None, None),
            P(("parts", "dp"), None, "seq", None, None),
            P(None, "seq", None),
            P("parts", None),
        ),
        out_specs=P("parts", "seq", "dp"),
        check_vma=False,
    )
```

```python
import functools
import math

import jax
import jax.numpy as jnp
from jax import lax
from jax.experimental import pallas as pl
from jax.experimental.pallas import tpu as pltpu
from jax.sharding import PartitionSpec as P

MAXCLIP = 3
VALUES = 2
OTHERS = (0, 1, 3)
TILE = 8
EPS = 1e-06
VMEM_LIMIT = 48 * 1024 * 1024
PACK_VMEM_LIMIT = 53 * 1024 * 1024


def head_chunks(heads):
    sizes = {8: (4, 3, 1)}.get(heads)
    if sizes is None:
        sizes = (1,) * heads if heads <= 2 else (heads - heads // 2, heads // 2)
    bounds, start = [], 0
    for size in sizes:
        bounds.append((start, start + size))
        start += size
    return bounds


def tile_start(heads, flip):
    head = jnp.bitwise_xor(lax.axis_index("seq"), flip) * heads
    offset = 0 if heads % TILE == 0 else lax.rem(head, TILE)
    return pl.multiple_of((head // TILE) * TILE, TILE), offset


def cut_kernel(flips, heads, array, *refs):
    outs, token, sems = refs[:-2], refs[-2], refs[-1]
    token[...] = jnp.zeros_like(token)
    copies = []
    for index, flip in enumerate(flips):
        start, _ = tile_start(heads, flip)
        source = array.at[0, :, :, pl.ds(start, outs[index].shape[2]), :]
        copies.append(pltpu.make_async_copy(source, outs[index], sems.at[index]))
        copies[-1].start()
    for copy in copies:
        copy.wait()


def cut(array, flips, heads):
    _, slots, rows, _, size = array.shape
    shape = jax.ShapeDtypeStruct((slots, rows, max(heads, TILE), size), array.dtype)
    return pl.pallas_call(
        functools.partial(cut_kernel, flips, heads),
        out_shape=[shape] * len(flips) + [jax.ShapeDtypeStruct((TILE, size), jnp.float32)],
        in_specs=[pl.BlockSpec(memory_space=pltpu.HBM)],
        out_specs=[pl.BlockSpec(memory_space=pltpu.VMEM)] * (len(flips) + 1),
        scratch_shapes=[pltpu.SemaphoreType.DMA((len(flips),))],
        compiler_params=pltpu.CompilerParams(vmem_limit_bytes=PACK_VMEM_LIMIT),
        name="cut",
    )(array)


def arrange_kernel(*refs):
    pieces, out, wide = refs[:-2], refs[-2], refs[-1]
    heads, slots = out.shape[:2]
    rows, held = pieces[0].shape[1:3]
    _, offset = tile_start(heads, 0)
    for source, piece in enumerate(pieces):
        for slot in range(slots):
            for span in range(held // TILE):
                place = (source * slots + slot) % wide.shape[0]
                block = piece[slot, :, span * TILE : (span + 1) * TILE, :]
                wide[place] = block.astype(jnp.float32).reshape(rows * TILE, wide.shape[-1])
                for head in range(span * TILE, min(heads, (span + 1) * TILE)):
                    out[head, slot, source * rows : (source + 1) * rows, :] = wide[
                        place, pl.ds(offset + head - span * TILE, rows, stride=TILE), :
                    ].astype(jnp.bfloat16)


def arrange(pieces, heads):
    slots, rows, held, size = pieces[0].shape
    moved = len(pieces) * slots * rows * held * size * 2
    return pl.pallas_call(
        arrange_kernel,
        out_shape=jax.ShapeDtypeStruct((heads, slots, len(pieces) * rows, size), jnp.bfloat16),
        in_specs=[pl.BlockSpec(memory_space=pltpu.VMEM)] * len(pieces),
        out_specs=pl.BlockSpec(memory_space=pltpu.VMEM),
        scratch_shapes=[pltpu.VMEM((slots, rows * TILE, size), jnp.float32)],
        compiler_params=pltpu.CompilerParams(vmem_limit_bytes=VMEM_LIMIT),
        cost_estimate=pl.CostEstimate(flops=moved, bytes_accessed=2 * moved, transcendentals=0),
        name="arrange",
    )(*pieces)


def pack_kernel(plan, heads, after, *refs):
    arrays = refs[:4]
    outs = refs[4 + after : 4 + after + sum(len(chunks) for _, _, chunks in plan)]
    token, raw, wide, sems = refs[4 + after + len(outs) :]
    token[...] = jnp.zeros_like(token)
    slots, rows = raw.shape[2], raw.shape[3]
    spans = max(1, heads // TILE)

    def copy(index, array, span, first):
        return pltpu.make_async_copy(
            arrays[array].at[0, :, :, pl.ds(first + span * TILE, TILE), :],
            raw.at[index, array * spans + span],
            sems.at[index, array * spans + span],
        )

    firsts, offsets = zip(*[tile_start(heads, flip) for flip, _, _ in plan])
    for index, (_, wanted, _) in enumerate(plan):
        for array in wanted:
            for span in range(spans):
                copy(index, array, span, firsts[index]).start()
    place = 0
    for index, (_, wanted, chunks) in enumerate(plan):
        for position, array in enumerate(wanted):
            for span in range(spans):
                copy(index, array, span, firsts[index]).wait()
                for slot in range(slots):
                    wide[slot] = (
                        raw[index, array * spans + span, slot]
                        .astype(jnp.float32)
                        .reshape(rows * TILE, wide.shape[-1])
                    )
                    for number, (low, high) in enumerate(chunks):
                        for head in range(max(low, span * TILE), min(high, (span + 1) * TILE)):
                            outs[place + number][head - low, position, slot * rows : (slot + 1) * rows, :] = wide[
                                slot, pl.ds(offsets[index] + head - span * TILE, rows, stride=TILE), :
                            ].astype(jnp.bfloat16)
        place += len(chunks)


def pack(arrays, plan, heads, after=()):
    _, slots, rows, _, size = arrays[0].shape
    spans = max(1, heads // TILE)
    shapes = [
        jax.ShapeDtypeStruct((high - low, len(wanted), slots * rows, size), jnp.bfloat16)
        for _, wanted, chunks in plan
        for low, high in chunks
    ] + [jax.ShapeDtypeStruct((TILE, size), jnp.float32)]
    count = len(plan)
    moved = count * 4 * spans * slots * rows * TILE * size * 2
    return pl.pallas_call(
        functools.partial(pack_kernel, plan, heads, len(after)),
        out_shape=shapes,
        in_specs=[pl.BlockSpec(memory_space=pltpu.HBM)] * 4 + [pl.BlockSpec(memory_space=pl.ANY)] * len(after),
        out_specs=[pl.BlockSpec(memory_space=pltpu.VMEM)] * len(shapes),
        scratch_shapes=[
            pltpu.VMEM((count, 4 * spans, slots, rows, TILE, size), jnp.bfloat16),
            pltpu.VMEM((slots, rows * TILE, size), jnp.float32),
            pltpu.SemaphoreType.DMA((count, 4 * spans)),
        ],
        compiler_params=pltpu.CompilerParams(vmem_limit_bytes=PACK_VMEM_LIMIT),
        cost_estimate=pl.CostEstimate(flops=moved, bytes_accessed=2 * moved, transcendentals=0),
        name="pack",
    )(*arrays, *after)


def contract_last(left, right):
    return lax.dot_general(left, right, (((1,), (1,)), ((), ())), preferred_element_type=jnp.float32)


def layouts(slots):
    found = []

    def extend(start, clips):
        if start == slots:
            found.append(tuple(clips))
        for span in range(1, min(MAXCLIP, slots - start) + 1):
            extend(start + span, clips + [(start, span)])

    extend(0, [])
    return found


def normalized(block, gain):
    wide = block.astype(jnp.float32)
    wide = wide * lax.rsqrt(jnp.mean(wide * wide, axis=-1, keepdims=True) + EPS)
    return (wide * gain).astype(jnp.bfloat16)


def prepare_kernel(low, after, gains, *refs):
    pieces, out = refs[after:-1], refs[-1]
    heads, _, tokens, _ = pieces[0].shape
    slots = out.shape[2]
    rows = tokens // slots
    for head in range(heads):
        for array in range(4):
            for source, piece in enumerate(pieces[array // 2 :: 2]):
                block = piece[head, array % 2]
                if array < 2:
                    block = normalized(block, gains[array, low + head : low + head + 1, :])
                for slot in range(slots):
                    out[head, array, slot, source * rows : (source + 1) * rows, :] = block[
                        slot * rows : (slot + 1) * rows
                    ]


def prepare(low, gains, pieces, slots, after):
    heads, _, tokens, size = pieces[0].shape
    moved = len(pieces) * heads * 2 * tokens * size * 2
    return pl.pallas_call(
        functools.partial(prepare_kernel, low, len(after)),
        out_shape=jax.ShapeDtypeStruct((heads, 4, slots, len(pieces) // 2 * tokens // slots, size), jnp.bfloat16),
        in_specs=[pl.BlockSpec(memory_space=pltpu.VMEM)] * (1 + len(after) + len(pieces)),
        out_specs=pl.BlockSpec(memory_space=pltpu.VMEM),
        compiler_params=pltpu.CompilerParams(vmem_limit_bytes=VMEM_LIMIT),
        cost_estimate=pl.CostEstimate(flops=1, bytes_accessed=1, transcendentals=0),
        name="prepare",
    )(gains, *after, *pieces)


def attention_chunk(low, count, units, gains, values, close, pieces, held, total):
    query, key, value, grad = held
    group = lax.axis_index("dp")
    _, _, tokens, size = pieces[0].shape
    slots, near = close.shape[2:4]
    rows = tokens // slots
    unit = near + rows * len(pieces)
    for head in range(count):
        for array, kept in enumerate(held):
            for slot in range(slots):
                kept[head, slot * unit : slot * unit + near, :] = close[head, array, slot]
                if array == VALUES:
                    kept[head, slot * unit + near : (slot + 1) * unit, :] = values[low + head, slot]
            if array == VALUES:
                continue
            for source, piece in enumerate(pieces):
                block = piece[head, OTHERS.index(array)]
                if array < 2:
                    block = normalized(block, gains[array, low + head : low + head + 1, :])
                for slot in range(slots):
                    start = slot * unit + near + source * rows
                    kept[head, start : start + rows, :] = block[slot * rows : (slot + 1) * rows]
    factor = size ** (-0.5) * math.log2(math.e)

    def clip(head, slot, span):
        where = slice(slot * unit, (slot + span) * unit)
        q, k = query[head, where, :], key[head, where, :]
        expo = jnp.exp2(contract_last(k, q) * factor)
        dprob = contract_last(value[head, where, :], grad[head, where, :])
        prob = expo * (1.0 / jnp.sum(expo, axis=0, keepdims=True))
        delta = jnp.sum(prob * dprob, axis=0, keepdims=True)
        dscore = (prob * (dprob - delta)).astype(jnp.bfloat16)
        mixed = jnp.dot(dscore, q, preferred_element_type=jnp.float32)
        return jnp.sum(mixed * k.astype(jnp.float32), axis=0, keepdims=True)

    begins = sum(jnp.where(units[group, slot] > 0, 1 << slot, 0) for slot in range(slots))
    for layout in layouts(slots):

        @pl.when(begins == sum(1 << slot for slot, _ in layout))
        def _():
            for head in range(count):
                total[head : head + 1, :] = sum(clip(head, slot, span) for slot, span in layout)


def chunk_kernel(low, units, gains, values, close, *refs):
    pieces, out, held = refs[:-5], refs[-5], refs[-4:]
    attention_chunk(low, out.shape[0], units, gains, values, close, pieces, held, out)


def last_kernel(low, sources, earlier, peers, units, gains, values, close, *refs):
    pieces = refs[:sources]
    before = refs[sources : sources + earlier]
    outs = refs[sources + earlier : sources + earlier + len(peers)]
    held, total = refs[sources + earlier + len(peers) : -1], refs[-1]
    attention_chunk(low, total.shape[0], units, gains, values, close, pieces, held, total)
    group = lax.axis_index("dp")
    size = total.shape[-1]
    width = outs[0].shape[-1]
    scaled = jnp.concatenate([ref[...] for ref in before] + [total[...]], axis=0) * (size ** (-0.5))
    for side in range(2):
        grads = scaled / gains[side]
        for out, flip in zip(outs, peers):
            shift = lax.rem(size - jnp.bitwise_xor(group, flip) * width, size)
            out[side] = pltpu.roll(grads, shift, 1)[:, :width]


def attend(low, count, units, gains, values, close, pieces, earlier=None, peers=None):
    _, _, tokens, size = pieces[0].shape
    all_tokens = close.shape[2] * close.shape[3] + tokens * len(pieces)
    held = [pltpu.VMEM((count, all_tokens, size), jnp.bfloat16)] * 4
    if earlier is None:
        kernel = functools.partial(chunk_kernel, low)
        shapes = jax.ShapeDtypeStruct((count, size), jnp.float32)
        earlier = []
        outs = pl.BlockSpec(memory_space=pltpu.VMEM)
    else:
        kernel = functools.partial(last_kernel, low, len(pieces), len(earlier), peers)
        heads = gains.shape[1]
        shapes = [jax.ShapeDtypeStruct((2, heads, size // len(peers)), jnp.float32)] * len(peers)
        held.append(pltpu.VMEM((count, size), jnp.float32))
        outs = [pl.BlockSpec(memory_space=pltpu.VMEM)] * len(peers)
    pairs = count * all_tokens * all_tokens // 2
    return pl.pallas_call(
        kernel,
        out_shape=shapes,
        in_specs=[pl.BlockSpec(memory_space=pltpu.SMEM)]
        + [pl.BlockSpec(memory_space=pltpu.VMEM)] * (3 + len(pieces) + len(earlier)),
        out_specs=outs,
        scratch_shapes=held,
        compiler_params=pltpu.CompilerParams(vmem_limit_bytes=VMEM_LIMIT),
        cost_estimate=pl.CostEstimate(
            flops=6 * pairs * size, bytes_accessed=len(pieces) * count * 4 * tokens * size * 2, transcendentals=pairs
        ),
        name="attend",
    )(units, gains, values, close, *pieces, *earlier)


def seen_kernel(*refs):
    refs[-1][...] = jnp.zeros_like(refs[-1])


def seen(blocks):
    return pl.pallas_call(
        seen_kernel,
        out_shape=jax.ShapeDtypeStruct((TILE, blocks[0].shape[-1]), jnp.float32),
        in_specs=[pl.BlockSpec(memory_space=pl.ANY)] * len(blocks),
        out_specs=pl.BlockSpec(memory_space=pltpu.VMEM),
        compiler_params=pltpu.CompilerParams(vmem_limit_bytes=1024 * 1024),
        cost_estimate=pl.CostEstimate(flops=1, bytes_accessed=1024 * 1024, transcendentals=0),
        name="seen",
    )(*blocks)


def body(sequence, groups, queries, key_rows, value_rows, out_grad, norm_gains, clip_units):
    arrays = (queries, key_rows, value_rows, out_grad)
    heads = norm_gains.shape[1]
    chunks = head_chunks(heads)
    far = list(range(2, sequence)) or [1]
    near = [flip for flip in range(1, sequence) if flip not in far]

    def send(block, flip):
        return lax.ppermute(block, "seq", [(s, s ^ flip) for s in range(sequence)])

    slots = clip_units.shape[1]
    close = near + [0]

    def pack_and_send(plan, after):
        *blocks, token = pack(arrays, plan, heads, after)
        flips = [flip for flip, _, wanted in plan for _ in wanted]
        return [send(block, flip) if flip else block for flip, block in zip(flips, blocks)], token

    def far_plan(number):
        return [(flip, OTHERS, chunks[number : number + 1]) for flip in far]

    *tiles, token = cut(arrays[VALUES], far, heads)
    tiles = [send(block, flip) for flip, block in zip(far, tiles)]
    received, token = pack_and_send(far_plan(0), [token])
    later = far_plan(1) if len(chunks) > 1 else []
    whole = [(flip, pair, chunks) for flip in close for pair in ((0, 1), (2, 3))]
    blocks, _ = pack_and_send(later + whole, [token, seen(tiles)])
    values = arrange(tiles, heads)
    prepared = [
        prepare(low, norm_gains, blocks[len(later) + number :: len(chunks)], slots, [] if number else [seen(received)])
        for number, (low, _) in enumerate(chunks)
    ]
    waiting, sums = blocks[: len(later)], []
    for number, (low, high) in enumerate(chunks[:-1]):
        sums.append(attend(low, high - low, clip_units, norm_gains, values, prepared[number], received))
        received = waiting
        if number + 2 < len(chunks):
            waiting, _ = pack_and_send(far_plan(number + 2), sums[-1:])
    low, high = chunks[-1]
    parts = attend(
        low, high - low, clip_units, norm_gains, values, prepared[-1], received, sums, list(range(groups))
    )
    result = parts[0]
    for flip in reversed(range(1, groups)):
        result = result + lax.ppermute(parts[flip], "dp", [(g, g ^ flip) for g in range(groups)])
    return result


def solution(mesh):
    return jax.shard_map(
        functools.partial(body, mesh.shape["seq"], mesh.shape["dp"]),
        mesh=mesh,
        in_specs=(
            P(("parts", "dp"), None, "seq", None, None),
            P(("parts", "dp"), None, "seq", None, None),
            P(("parts", "dp"), None, "seq", None, None),
            P(("parts", "dp"), None, "seq", None, None),
            P(None, "seq", None),
            P("parts", None),
        ),
        out_specs=P("parts", "seq", "dp"),
        check_vma=False,
    )
```

```python
import functools
import math

import jax
import jax.numpy as jnp
from jax import lax
from jax.experimental import pallas as pl
from jax.experimental.pallas import tpu as pltpu
from jax.sharding import PartitionSpec as P

MAXCLIP = 3
VALUES = 2
OTHERS = (0, 1, 3)
TILE = 8
EPS = 1e-06
VMEM_LIMIT = 48 * 1024 * 1024
PACK_VMEM_LIMIT = 53 * 1024 * 1024


def head_chunks(heads):
    sizes = {8: (4, 3, 1)}.get(heads)
    if sizes is None:
        sizes = (1,) * heads if heads <= 2 else (heads - heads // 2, heads // 2)
    bounds, start = [], 0
    for size in sizes:
        bounds.append((start, start + size))
        start += size
    return bounds


def tile_start(heads, flip):
    head = jnp.bitwise_xor(lax.axis_index("seq"), flip) * heads
    offset = 0 if heads % TILE == 0 else lax.rem(head, TILE)
    return pl.multiple_of((head // TILE) * TILE, TILE), offset


def cut_kernel(flips, heads, array, *refs):
    outs, token, sems = refs[:-2], refs[-2], refs[-1]
    token[...] = jnp.zeros_like(token)
    copies = []
    for index, flip in enumerate(flips):
        start, _ = tile_start(heads, flip)
        source = array.at[0, :, :, pl.ds(start, outs[index].shape[2]), :]
        copies.append(pltpu.make_async_copy(source, outs[index], sems.at[index]))
        copies[-1].start()
    for copy in copies:
        copy.wait()


def cut(array, flips, heads):
    _, slots, rows, _, size = array.shape
    shape = jax.ShapeDtypeStruct((slots, rows, max(heads, TILE), size), array.dtype)
    return pl.pallas_call(
        functools.partial(cut_kernel, flips, heads),
        out_shape=[shape] * len(flips) + [jax.ShapeDtypeStruct((TILE, size), jnp.float32)],
        in_specs=[pl.BlockSpec(memory_space=pltpu.HBM)],
        out_specs=[pl.BlockSpec(memory_space=pltpu.VMEM)] * (len(flips) + 1),
        scratch_shapes=[pltpu.SemaphoreType.DMA((len(flips),))],
        compiler_params=pltpu.CompilerParams(vmem_limit_bytes=PACK_VMEM_LIMIT),
        name="cut",
    )(array)


def arrange_kernel(*refs):
    pieces, out, wide = refs[:-2], refs[-2], refs[-1]
    heads, slots = out.shape[:2]
    rows, held = pieces[0].shape[1:3]
    _, offset = tile_start(heads, 0)
    for source, piece in enumerate(pieces):
        for slot in range(slots):
            for span in range(held // TILE):
                place = (source * slots + slot) % wide.shape[0]
                block = piece[slot, :, span * TILE : (span + 1) * TILE, :]
                wide[place] = block.astype(jnp.float32).reshape(rows * TILE, wide.shape[-1])
                for head in range(span * TILE, min(heads, (span + 1) * TILE)):
                    out[head, slot, source * rows : (source + 1) * rows, :] = wide[
                        place, pl.ds(offset + head - span * TILE, rows, stride=TILE), :
                    ].astype(jnp.bfloat16)


def arrange(pieces, heads):
    slots, rows, held, size = pieces[0].shape
    moved = len(pieces) * slots * rows * held * size * 2
    return pl.pallas_call(
        arrange_kernel,
        out_shape=jax.ShapeDtypeStruct((heads, slots, len(pieces) * rows, size), jnp.bfloat16),
        in_specs=[pl.BlockSpec(memory_space=pltpu.VMEM)] * len(pieces),
        out_specs=pl.BlockSpec(memory_space=pltpu.VMEM),
        scratch_shapes=[pltpu.VMEM((slots, rows * TILE, size), jnp.float32)],
        compiler_params=pltpu.CompilerParams(vmem_limit_bytes=VMEM_LIMIT),
        cost_estimate=pl.CostEstimate(flops=moved, bytes_accessed=2 * moved, transcendentals=0),
        name="arrange",
    )(*pieces)


def pack_kernel(plan, heads, after, *refs):
    arrays = refs[:4]
    outs = refs[4 + after : 4 + after + sum(len(chunks) for _, _, chunks in plan)]
    token, raw, wide, sems = refs[4 + after + len(outs) :]
    token[...] = jnp.zeros_like(token)
    slots, rows = raw.shape[2], raw.shape[3]
    spans = max(1, heads // TILE)

    def copy(index, array, span, first):
        return pltpu.make_async_copy(
            arrays[array].at[0, :, :, pl.ds(first + span * TILE, TILE), :],
            raw.at[index, array * spans + span],
            sems.at[index, array * spans + span],
        )

    firsts, offsets = zip(*[tile_start(heads, flip) for flip, _, _ in plan])
    for index, (_, wanted, _) in enumerate(plan):
        for array in wanted:
            for span in range(spans):
                copy(index, array, span, firsts[index]).start()
    place = 0
    for index, (_, wanted, chunks) in enumerate(plan):
        for position, array in enumerate(wanted):
            for span in range(spans):
                copy(index, array, span, firsts[index]).wait()
                for slot in range(slots):
                    wide[slot] = (
                        raw[index, array * spans + span, slot]
                        .astype(jnp.float32)
                        .reshape(rows * TILE, wide.shape[-1])
                    )
                    for number, (low, high) in enumerate(chunks):
                        for head in range(max(low, span * TILE), min(high, (span + 1) * TILE)):
                            outs[place + number][head - low, position, slot * rows : (slot + 1) * rows, :] = wide[
                                slot, pl.ds(offsets[index] + head - span * TILE, rows, stride=TILE), :
                            ].astype(jnp.bfloat16)
        place += len(chunks)


def pack(arrays, plan, heads, after=()):
    _, slots, rows, _, size = arrays[0].shape
    spans = max(1, heads // TILE)
    shapes = [
        jax.ShapeDtypeStruct((high - low, len(wanted), slots * rows, size), jnp.bfloat16)
        for _, wanted, chunks in plan
        for low, high in chunks
    ] + [jax.ShapeDtypeStruct((TILE, size), jnp.float32)]
    count = len(plan)
    moved = count * 4 * spans * slots * rows * TILE * size * 2
    return pl.pallas_call(
        functools.partial(pack_kernel, plan, heads, len(after)),
        out_shape=shapes,
        in_specs=[pl.BlockSpec(memory_space=pltpu.HBM)] * 4 + [pl.BlockSpec(memory_space=pl.ANY)] * len(after),
        out_specs=[pl.BlockSpec(memory_space=pltpu.VMEM)] * len(shapes),
        scratch_shapes=[
            pltpu.VMEM((count, 4 * spans, slots, rows, TILE, size), jnp.bfloat16),
            pltpu.VMEM((slots, rows * TILE, size), jnp.float32),
            pltpu.SemaphoreType.DMA((count, 4 * spans)),
        ],
        compiler_params=pltpu.CompilerParams(vmem_limit_bytes=PACK_VMEM_LIMIT),
        cost_estimate=pl.CostEstimate(flops=moved, bytes_accessed=2 * moved, transcendentals=0),
        name="pack",
    )(*arrays, *after)


def contract_last(left, right):
    return lax.dot_general(left, right, (((1,), (1,)), ((), ())), preferred_element_type=jnp.float32)


def layouts(slots):
    found = []

    def extend(start, clips):
        if start == slots:
            found.append(tuple(clips))
        for span in range(1, min(MAXCLIP, slots - start) + 1):
            extend(start + span, clips + [(start, span)])

    extend(0, [])
    return found


def normalized(block, gain):
    wide = block.astype(jnp.float32)
    wide = wide * lax.rsqrt(jnp.mean(wide * wide, axis=-1, keepdims=True) + EPS)
    return (wide * gain).astype(jnp.bfloat16)


def prepare_kernel(low, after, gains, *refs):
    pieces, out = refs[after:-1], refs[-1]
    heads, _, tokens, _ = pieces[0].shape
    slots = out.shape[2]
    rows = tokens // slots
    for head in range(heads):
        for array in range(4):
            for source, piece in enumerate(pieces[array // 2 :: 2]):
                block = piece[head, array % 2]
                if array < 2:
                    block = normalized(block, gains[array, low + head : low + head + 1, :])
                for slot in range(slots):
                    out[head, array, slot, source * rows : (source + 1) * rows, :] = block[
                        slot * rows : (slot + 1) * rows
                    ]


def prepare(low, gains, pieces, slots, after):
    heads, _, tokens, size = pieces[0].shape
    moved = len(pieces) * heads * 2 * tokens * size * 2
    return pl.pallas_call(
        functools.partial(prepare_kernel, low, len(after)),
        out_shape=jax.ShapeDtypeStruct((heads, 4, slots, len(pieces) // 2 * tokens // slots, size), jnp.bfloat16),
        in_specs=[pl.BlockSpec(memory_space=pltpu.VMEM)] * (1 + len(after) + len(pieces)),
        out_specs=pl.BlockSpec(memory_space=pltpu.VMEM),
        compiler_params=pltpu.CompilerParams(vmem_limit_bytes=VMEM_LIMIT),
        cost_estimate=pl.CostEstimate(flops=1, bytes_accessed=1, transcendentals=0),
        name="prepare",
    )(gains, *after, *pieces)


def attention_chunk(low, count, units, gains, values, close, pieces, held, total):
    query, key, value, grad = held
    group = lax.axis_index("dp")
    _, _, tokens, size = pieces[0].shape
    slots, near = close.shape[2:4]
    rows = tokens // slots
    unit = near + rows * len(pieces)
    for head in range(count):
        for array, kept in enumerate(held):
            for slot in range(slots):
                kept[head, slot * unit : slot * unit + near, :] = close[head, array, slot]
                if array == VALUES:
                    kept[head, slot * unit + near : (slot + 1) * unit, :] = values[low + head, slot]
            if array == VALUES:
                continue
            for source, piece in enumerate(pieces):
                block = piece[head, OTHERS.index(array)]
                if array < 2:
                    block = normalized(block, gains[array, low + head : low + head + 1, :])
                for slot in range(slots):
                    start = slot * unit + near + source * rows
                    kept[head, start : start + rows, :] = block[slot * rows : (slot + 1) * rows]
    factor = size ** (-0.5) * math.log2(math.e)

    def clip(head, slot, span):
        where = slice(slot * unit, (slot + span) * unit)
        q, k = query[head, where, :], key[head, where, :]
        expo = jnp.exp2(contract_last(k, q) * factor)
        dprob = contract_last(value[head, where, :], grad[head, where, :])
        prob = expo * (1.0 / jnp.sum(expo, axis=0, keepdims=True))
        delta = jnp.sum(prob * dprob, axis=0, keepdims=True)
        dscore = (prob * (dprob - delta)).astype(jnp.bfloat16)
        mixed = jnp.dot(dscore, q, preferred_element_type=jnp.float32)
        return jnp.sum(mixed * k.astype(jnp.float32), axis=0, keepdims=True)

    table = units[...]
    rows_of, slots_of = (lax.broadcasted_iota(jnp.int32, table.shape, dim) for dim in (0, 1))
    starts = jnp.where((rows_of == group) & (table > 0), lax.shift_left(jnp.int32(1), slots_of), 0)
    begins = jnp.sum(starts)
    for layout in layouts(slots):

        @pl.when(begins == sum(1 << slot for slot, _ in layout))
        def _():
            for head in range(count):
                total[head : head + 1, :] = sum(clip(head, slot, span) for slot, span in layout)


def chunk_kernel(low, units, gains, values, close, *refs):
    pieces, out, held = refs[:-5], refs[-5], refs[-4:]
    attention_chunk(low, out.shape[0], units, gains, values, close, pieces, held, out)


def last_kernel(low, sources, earlier, peers, units, gains, values, close, *refs):
    pieces = refs[:sources]
    before = refs[sources : sources + earlier]
    outs = refs[sources + earlier : sources + earlier + len(peers)]
    held, total = refs[sources + earlier + len(peers) : -1], refs[-1]
    attention_chunk(low, total.shape[0], units, gains, values, close, pieces, held, total)
    group = lax.axis_index("dp")
    size = total.shape[-1]
    width = outs[0].shape[-1]
    scaled = jnp.concatenate([ref[...] for ref in before] + [total[...]], axis=0) * (size ** (-0.5))
    for side in range(2):
        grads = scaled / gains[side]
        for out, flip in zip(outs, peers):
            shift = lax.rem(size - jnp.bitwise_xor(group, flip) * width, size)
            out[side] = pltpu.roll(grads, shift, 1)[:, :width]


def attend(low, count, units, gains, values, close, pieces, earlier=None, peers=None):
    _, _, tokens, size = pieces[0].shape
    all_tokens = close.shape[2] * close.shape[3] + tokens * len(pieces)
    held = [pltpu.VMEM((count, all_tokens, size), jnp.bfloat16)] * 4
    if earlier is None:
        kernel = functools.partial(chunk_kernel, low)
        shapes = jax.ShapeDtypeStruct((count, size), jnp.float32)
        earlier = []
        outs = pl.BlockSpec(memory_space=pltpu.VMEM)
    else:
        kernel = functools.partial(last_kernel, low, len(pieces), len(earlier), peers)
        heads = gains.shape[1]
        shapes = [jax.ShapeDtypeStruct((2, heads, size // len(peers)), jnp.float32)] * len(peers)
        held.append(pltpu.VMEM((count, size), jnp.float32))
        outs = [pl.BlockSpec(memory_space=pltpu.VMEM)] * len(peers)
    pairs = count * all_tokens * all_tokens // 2
    return pl.pallas_call(
        kernel,
        out_shape=shapes,
        in_specs=[pl.BlockSpec(memory_space=pltpu.VMEM)] * (4 + len(pieces) + len(earlier)),
        out_specs=outs,
        scratch_shapes=held,
        compiler_params=pltpu.CompilerParams(vmem_limit_bytes=VMEM_LIMIT),
        cost_estimate=pl.CostEstimate(
            flops=6 * pairs * size, bytes_accessed=len(pieces) * count * 4 * tokens * size * 2, transcendentals=pairs
        ),
        name="attend",
    )(units, gains, values, close, *pieces, *earlier)


def seen_kernel(*refs):
    refs[-1][...] = jnp.zeros_like(refs[-1])


def seen(blocks):
    return pl.pallas_call(
        seen_kernel,
        out_shape=jax.ShapeDtypeStruct((TILE, blocks[0].shape[-1]), jnp.float32),
        in_specs=[pl.BlockSpec(memory_space=pl.ANY)] * len(blocks),
        out_specs=pl.BlockSpec(memory_space=pltpu.VMEM),
        compiler_params=pltpu.CompilerParams(vmem_limit_bytes=1024 * 1024),
        cost_estimate=pl.CostEstimate(flops=1, bytes_accessed=1024 * 1024, transcendentals=0),
        name="seen",
    )(*blocks)


def body(sequence, groups, queries, key_rows, value_rows, out_grad, norm_gains, clip_units):
    arrays = (queries, key_rows, value_rows, out_grad)
    heads = norm_gains.shape[1]
    chunks = head_chunks(heads)
    far = list(range(2, sequence)) or [1]
    near = [flip for flip in range(1, sequence) if flip not in far]

    def send(block, flip):
        return lax.ppermute(block, "seq", [(s, s ^ flip) for s in range(sequence)])

    slots = clip_units.shape[1]
    close = near + [0]

    def pack_and_send(plan, after):
        *blocks, token = pack(arrays, plan, heads, after)
        flips = [flip for flip, _, wanted in plan for _ in wanted]
        return [send(block, flip) if flip else block for flip, block in zip(flips, blocks)], token

    def far_plan(number):
        return [(flip, OTHERS, chunks[number : number + 1]) for flip in far]

    *tiles, token = cut(arrays[VALUES], far, heads)
    tiles = [send(block, flip) for flip, block in zip(far, tiles)]
    received, token = pack_and_send(far_plan(0), [token])
    later = far_plan(1) if len(chunks) > 1 else []
    whole = [(flip, pair, chunks) for flip in close for pair in ((0, 1), (2, 3))]
    blocks, _ = pack_and_send(later + whole, [token, seen(tiles)])
    values = arrange(tiles, heads)
    prepared = [
        prepare(low, norm_gains, blocks[len(later) + number :: len(chunks)], slots, [] if number else [seen(received)])
        for number, (low, _) in enumerate(chunks)
    ]
    waiting, sums = blocks[: len(later)], []
    for number, (low, high) in enumerate(chunks[:-1]):
        sums.append(attend(low, high - low, clip_units, norm_gains, values, prepared[number], received))
        received = waiting
        if number + 2 < len(chunks):
            waiting, _ = pack_and_send(far_plan(number + 2), sums[-1:])
    low, high = chunks[-1]
    parts = attend(
        low, high - low, clip_units, norm_gains, values, prepared[-1], received, sums, list(range(groups))
    )
    result = parts[0]
    for flip in reversed(range(1, groups)):
        result = result + lax.ppermute(parts[flip], "dp", [(g, g ^ flip) for g in range(groups)])
    return result


def solution(mesh):
    return jax.shard_map(
        functools.partial(body, mesh.shape["seq"], mesh.shape["dp"]),
        mesh=mesh,
        in_specs=(
            P(("parts", "dp"), None, "seq", None, None),
            P(("parts", "dp"), None, "seq", None, None),
            P(("parts", "dp"), None, "seq", None, None),
            P(("parts", "dp"), None, "seq", None, None),
            P(None, "seq", None),
            P("parts", None),
        ),
        out_specs=P("parts", "seq", "dp"),
        check_vma=False,
    )
```

```python
import functools
import math

import jax
import jax.numpy as jnp
from jax import lax
from jax.experimental import pallas as pl
from jax.experimental.pallas import tpu as pltpu
from jax.sharding import PartitionSpec as P

MAXCLIP = 3
VALUES = 2
OTHERS = (0, 1, 3)
TILE = 8
EPS = 1e-06
VMEM_LIMIT = 48 * 1024 * 1024
PACK_VMEM_LIMIT = 53 * 1024 * 1024


def head_chunks(heads):
    sizes = {8: (4, 3, 1)}.get(heads)
    if sizes is None:
        sizes = (1,) * heads if heads <= 2 else (heads - heads // 2, heads // 2)
    bounds, start = [], 0
    for size in sizes:
        bounds.append((start, start + size))
        start += size
    return bounds


def tile_start(heads, flip):
    head = jnp.bitwise_xor(lax.axis_index("seq"), flip) * heads
    offset = 0 if heads % TILE == 0 else lax.rem(head, TILE)
    return pl.multiple_of((head // TILE) * TILE, TILE), offset


def cut_kernel(flips, heads, array, *refs):
    outs, token, sems = refs[:-2], refs[-2], refs[-1]
    token[...] = jnp.zeros_like(token)
    copies = []
    for index, flip in enumerate(flips):
        start, _ = tile_start(heads, flip)
        source = array.at[0, :, :, pl.ds(start, outs[index].shape[2]), :]
        copies.append(pltpu.make_async_copy(source, outs[index], sems.at[index]))
        copies[-1].start()
    for copy in copies:
        copy.wait()


def cut(array, flips, heads):
    _, slots, rows, _, size = array.shape
    shape = jax.ShapeDtypeStruct((slots, rows, max(heads, TILE), size), array.dtype)
    return pl.pallas_call(
        functools.partial(cut_kernel, flips, heads),
        out_shape=[shape] * len(flips) + [jax.ShapeDtypeStruct((TILE, size), jnp.float32)],
        in_specs=[pl.BlockSpec(memory_space=pltpu.HBM)],
        out_specs=[pl.BlockSpec(memory_space=pltpu.VMEM)] * (len(flips) + 1),
        scratch_shapes=[pltpu.SemaphoreType.DMA((len(flips),))],
        compiler_params=pltpu.CompilerParams(vmem_limit_bytes=PACK_VMEM_LIMIT),
        name="cut",
    )(array)


def arrange_kernel(*refs):
    pieces, out, wide = refs[:-2], refs[-2], refs[-1]
    heads, slots = out.shape[:2]
    rows, held = pieces[0].shape[1:3]
    _, offset = tile_start(heads, 0)
    for source, piece in enumerate(pieces):
        for slot in range(slots):
            for span in range(held // TILE):
                place = (source * slots + slot) % wide.shape[0]
                block = piece[slot, :, span * TILE : (span + 1) * TILE, :]
                wide[place] = block.astype(jnp.float32).reshape(rows * TILE, wide.shape[-1])
                for head in range(span * TILE, min(heads, (span + 1) * TILE)):
                    out[head, slot, source * rows : (source + 1) * rows, :] = wide[
                        place, pl.ds(offset + head - span * TILE, rows, stride=TILE), :
                    ].astype(jnp.bfloat16)


def arrange(pieces, heads):
    slots, rows, held, size = pieces[0].shape
    moved = len(pieces) * slots * rows * held * size * 2
    return pl.pallas_call(
        arrange_kernel,
        out_shape=jax.ShapeDtypeStruct((heads, slots, len(pieces) * rows, size), jnp.bfloat16),
        in_specs=[pl.BlockSpec(memory_space=pltpu.VMEM)] * len(pieces),
        out_specs=pl.BlockSpec(memory_space=pltpu.VMEM),
        scratch_shapes=[pltpu.VMEM((slots, rows * TILE, size), jnp.float32)],
        compiler_params=pltpu.CompilerParams(vmem_limit_bytes=VMEM_LIMIT),
        cost_estimate=pl.CostEstimate(flops=moved, bytes_accessed=2 * moved, transcendentals=0),
        name="arrange",
    )(*pieces)


def pack_kernel(plan, heads, after, *refs):
    arrays = refs[:4]
    outs = refs[4 + after : 4 + after + sum(len(chunks) for _, _, chunks in plan)]
    token, raw, wide, sems = refs[4 + after + len(outs) :]
    token[...] = jnp.zeros_like(token)
    slots, rows = raw.shape[2], raw.shape[3]
    spans = max(1, heads // TILE)

    def copy(index, array, span, first):
        return pltpu.make_async_copy(
            arrays[array].at[0, :, :, pl.ds(first + span * TILE, TILE), :],
            raw.at[index, array * spans + span],
            sems.at[index, array * spans + span],
        )

    firsts, offsets = zip(*[tile_start(heads, flip) for flip, _, _ in plan])
    for index, (_, wanted, _) in enumerate(plan):
        for array in wanted:
            for span in range(spans):
                copy(index, array, span, firsts[index]).start()
    place = 0
    for index, (_, wanted, chunks) in enumerate(plan):
        for position, array in enumerate(wanted):
            for span in range(spans):
                copy(index, array, span, firsts[index]).wait()
                for slot in range(slots):
                    wide[slot] = (
                        raw[index, array * spans + span, slot]
                        .astype(jnp.float32)
                        .reshape(rows * TILE, wide.shape[-1])
                    )
                    for number, (low, high) in enumerate(chunks):
                        for head in range(max(low, span * TILE), min(high, (span + 1) * TILE)):
                            outs[place + number][head - low, position, slot * rows : (slot + 1) * rows, :] = wide[
                                slot, pl.ds(offsets[index] + head - span * TILE, rows, stride=TILE), :
                            ].astype(jnp.bfloat16)
        place += len(chunks)


def pack(arrays, plan, heads, after=()):
    _, slots, rows, _, size = arrays[0].shape
    spans = max(1, heads // TILE)
    shapes = [
        jax.ShapeDtypeStruct((high - low, len(wanted), slots * rows, size), jnp.bfloat16)
        for _, wanted, chunks in plan
        for low, high in chunks
    ] + [jax.ShapeDtypeStruct((TILE, size), jnp.float32)]
    count = len(plan)
    moved = count * 4 * spans * slots * rows * TILE * size * 2
    return pl.pallas_call(
        functools.partial(pack_kernel, plan, heads, len(after)),
        out_shape=shapes,
        in_specs=[pl.BlockSpec(memory_space=pltpu.HBM)] * 4 + [pl.BlockSpec(memory_space=pl.ANY)] * len(after),
        out_specs=[pl.BlockSpec(memory_space=pltpu.VMEM)] * len(shapes),
        scratch_shapes=[
            pltpu.VMEM((count, 4 * spans, slots, rows, TILE, size), jnp.bfloat16),
            pltpu.VMEM((slots, rows * TILE, size), jnp.float32),
            pltpu.SemaphoreType.DMA((count, 4 * spans)),
        ],
        compiler_params=pltpu.CompilerParams(vmem_limit_bytes=PACK_VMEM_LIMIT),
        cost_estimate=pl.CostEstimate(flops=moved, bytes_accessed=2 * moved, transcendentals=0),
        name="pack",
    )(*arrays, *after)


def contract_last(left, right):
    return lax.dot_general(left, right, (((1,), (1,)), ((), ())), preferred_element_type=jnp.float32)


def layouts(slots):
    found = []

    def extend(start, clips):
        if start == slots:
            found.append(tuple(clips))
        for span in range(1, min(MAXCLIP, slots - start) + 1):
            extend(start + span, clips + [(start, span)])

    extend(0, [])
    return found


def normalized(block, gain):
    wide = block.astype(jnp.float32)
    wide = wide * lax.rsqrt(jnp.mean(wide * wide, axis=-1, keepdims=True) + EPS)
    return (wide * gain).astype(jnp.bfloat16)


def prepare_kernel(low, after, gains, *refs):
    pieces, out = refs[after:-1], refs[-1]
    heads, _, tokens, _ = pieces[0].shape
    slots = out.shape[2]
    rows = tokens // slots
    for head in range(heads):
        for array in range(4):
            for source, piece in enumerate(pieces[array // 2 :: 2]):
                block = piece[head, array % 2]
                if array < 2:
                    block = normalized(block, gains[array, low + head : low + head + 1, :])
                for slot in range(slots):
                    out[head, array, slot, source * rows : (source + 1) * rows, :] = block[
                        slot * rows : (slot + 1) * rows
                    ]


def prepare(low, gains, pieces, slots, after):
    heads, _, tokens, size = pieces[0].shape
    moved = len(pieces) * heads * 2 * tokens * size * 2
    return pl.pallas_call(
        functools.partial(prepare_kernel, low, len(after)),
        out_shape=jax.ShapeDtypeStruct((heads, 4, slots, len(pieces) // 2 * tokens // slots, size), jnp.bfloat16),
        in_specs=[pl.BlockSpec(memory_space=pltpu.VMEM)] * (1 + len(after) + len(pieces)),
        out_specs=pl.BlockSpec(memory_space=pltpu.VMEM),
        compiler_params=pltpu.CompilerParams(vmem_limit_bytes=VMEM_LIMIT),
        cost_estimate=pl.CostEstimate(flops=1, bytes_accessed=1, transcendentals=0),
        name="prepare",
    )(gains, *after, *pieces)


def attention_chunk(low, count, units, gains, values, close, pieces, held, total):
    query, key, value, grad = held
    group = lax.axis_index("dp")
    _, _, tokens, size = pieces[0].shape
    slots, near = close.shape[2:4]
    rows = tokens // slots
    unit = near + rows * len(pieces)
    for head in range(count):
        for array, kept in enumerate(held):
            for slot in range(slots):
                kept[head, slot * unit : slot * unit + near, :] = close[head, array, slot]
                if array == VALUES:
                    kept[head, slot * unit + near : (slot + 1) * unit, :] = values[low + head, slot]
            if array == VALUES:
                continue
            for source, piece in enumerate(pieces):
                block = piece[head, OTHERS.index(array)]
                if array < 2:
                    block = normalized(block, gains[array, low + head : low + head + 1, :])
                for slot in range(slots):
                    start = slot * unit + near + source * rows
                    kept[head, start : start + rows, :] = block[slot * rows : (slot + 1) * rows]
    factor = size ** (-0.5) * math.log2(math.e)

    def clip(head, slot, span):
        where = slice(slot * unit, (slot + span) * unit)
        q, k = query[head, where, :], key[head, where, :]
        expo = jnp.exp2(contract_last(k, q) * factor)
        dprob = contract_last(value[head, where, :], grad[head, where, :])
        prob = expo * (1.0 / jnp.sum(expo, axis=0, keepdims=True))
        delta = jnp.sum(prob * dprob, axis=0, keepdims=True)
        dscore = (prob * (dprob - delta)).astype(jnp.bfloat16)
        mixed = jnp.dot(dscore, q, preferred_element_type=jnp.float32)
        return jnp.sum(mixed * k.astype(jnp.float32), axis=0, keepdims=True)

    table = units[...]
    rows_of, slots_of = (lax.broadcasted_iota(jnp.int32, table.shape, dim) for dim in (0, 1))
    starts = jnp.where((rows_of == group) & (table > 0), lax.shift_left(jnp.int32(1), slots_of), 0)
    begins = jnp.sum(starts)
    for layout in layouts(slots):

        @pl.when(begins == sum(1 << slot for slot, _ in layout))
        def _():
            for head in range(count):
                total[head : head + 1, :] = sum(clip(head, slot, span) for slot, span in layout)


def chunk_kernel(low, units, gains, values, close, *refs):
    pieces, out, held = refs[:-5], refs[-5], refs[-4:]
    attention_chunk(low, out.shape[0], units, gains, values, close, pieces, held, out)


def last_kernel(low, sources, units, gains, values, close, *refs):
    pieces, before = refs[:sources], refs[sources:-6]
    out, held, total = refs[-6], refs[-5:-1], refs[-1]
    row = 0
    for ref in before:
        out[row : row + ref.shape[0], :] = ref[...]
        row += ref.shape[0]
    attention_chunk(low, total.shape[0], units, gains, values, close, pieces, held, total)
    out[row:, :] = total[...]


def attend(low, count, units, gains, values, close, pieces, earlier=None):
    _, _, tokens, size = pieces[0].shape
    all_tokens = close.shape[2] * close.shape[3] + tokens * len(pieces)
    held = [pltpu.VMEM((count, all_tokens, size), jnp.bfloat16)] * 4
    if earlier is None:
        kernel = functools.partial(chunk_kernel, low)
        rows, earlier = count, []
    else:
        kernel = functools.partial(last_kernel, low, len(pieces))
        rows = low + count
        held.append(pltpu.VMEM((count, size), jnp.float32))
    pairs = count * all_tokens * all_tokens // 2
    return pl.pallas_call(
        kernel,
        out_shape=jax.ShapeDtypeStruct((rows, size), jnp.float32),
        in_specs=[pl.BlockSpec(memory_space=pltpu.VMEM)] * (4 + len(pieces) + len(earlier)),
        out_specs=pl.BlockSpec(memory_space=pltpu.VMEM),
        scratch_shapes=held,
        compiler_params=pltpu.CompilerParams(vmem_limit_bytes=VMEM_LIMIT),
        cost_estimate=pl.CostEstimate(
            flops=6 * pairs * size, bytes_accessed=len(pieces) * count * 4 * tokens * size * 2, transcendentals=pairs
        ),
        name="attend",
    )(units, gains, values, close, *pieces, *earlier)


def finish_kernel(gains, *refs):
    sums, out = refs[:-1], refs[-1]
    size, width = sums[0].shape[-1], out.shape[-1]
    shift = lax.rem(size - lax.axis_index("dp") * width, size)
    total = sum(ref[...] for ref in sums) * (size ** (-0.5))
    for side in range(2):
        out[side] = pltpu.roll(total / gains[side], shift, 1)[:, :width]


def finish(gains, sums):
    heads, size = sums[0].shape
    return pl.pallas_call(
        finish_kernel,
        out_shape=jax.ShapeDtypeStruct((2, heads, size // len(sums)), jnp.float32),
        in_specs=[pl.BlockSpec(memory_space=pltpu.VMEM)] * (1 + len(sums)),
        out_specs=pl.BlockSpec(memory_space=pltpu.VMEM),
        compiler_params=pltpu.CompilerParams(vmem_limit_bytes=VMEM_LIMIT),
        cost_estimate=pl.CostEstimate(flops=1, bytes_accessed=1, transcendentals=0),
        name="finish",
    )(gains, *sums)


def seen_kernel(*refs):
    refs[-1][...] = jnp.zeros_like(refs[-1])


def seen(blocks):
    return pl.pallas_call(
        seen_kernel,
        out_shape=jax.ShapeDtypeStruct((TILE, blocks[0].shape[-1]), jnp.float32),
        in_specs=[pl.BlockSpec(memory_space=pl.ANY)] * len(blocks),
        out_specs=pl.BlockSpec(memory_space=pltpu.VMEM),
        compiler_params=pltpu.CompilerParams(vmem_limit_bytes=1024 * 1024),
        cost_estimate=pl.CostEstimate(flops=1, bytes_accessed=1024 * 1024, transcendentals=0),
        name="seen",
    )(*blocks)


def body(sequence, groups, queries, key_rows, value_rows, out_grad, norm_gains, clip_units):
    arrays = (queries, key_rows, value_rows, out_grad)
    heads = norm_gains.shape[1]
    chunks = head_chunks(heads)
    far = list(range(2, sequence)) or [1]
    near = [flip for flip in range(1, sequence) if flip not in far]

    def send(block, flip):
        return lax.ppermute(block, "seq", [(s, s ^ flip) for s in range(sequence)])

    slots = clip_units.shape[1]
    close = near + [0]

    def pack_and_send(plan, after):
        *blocks, token = pack(arrays, plan, heads, after)
        flips = [flip for flip, _, wanted in plan for _ in wanted]
        return [send(block, flip) if flip else block for flip, block in zip(flips, blocks)], token

    def far_plan(number):
        return [(flip, OTHERS, chunks[number : number + 1]) for flip in far]

    *tiles, token = cut(arrays[VALUES], far, heads)
    tiles = [send(block, flip) for flip, block in zip(far, tiles)]
    received, token = pack_and_send(far_plan(0), [token])
    later = far_plan(1) if len(chunks) > 1 else []
    whole = [(flip, pair, chunks) for flip in close for pair in ((0, 1), (2, 3))]
    blocks, _ = pack_and_send(later + whole, [token, seen(tiles)])
    values = arrange(tiles, heads)
    prepared = [
        prepare(low, norm_gains, blocks[len(later) + number :: len(chunks)], slots, [] if number else [seen(received)])
        for number, (low, _) in enumerate(chunks)
    ]
    waiting, sums = blocks[: len(later)], []
    for number, (low, high) in enumerate(chunks[:-1]):
        sums.append(attend(low, high - low, clip_units, norm_gains, values, prepared[number], received))
        received = waiting
        if number + 2 < len(chunks):
            waiting, _ = pack_and_send(far_plan(number + 2), sums[-1:])
    low, high = chunks[-1]
    sums = [attend(low, high - low, clip_units, norm_gains, values, prepared[-1], received, sums)]
    for flip in reversed(range(1, groups)):
        sums.append(lax.ppermute(sums[0], "dp", [(g, g ^ flip) for g in range(groups)]))
    return finish(norm_gains, sums)


def solution(mesh):
    return jax.shard_map(
        functools.partial(body, mesh.shape["seq"], mesh.shape["dp"]),
        mesh=mesh,
        in_specs=(
            P(("parts", "dp"), None, "seq", None, None),
            P(("parts", "dp"), None, "seq", None, None),
            P(("parts", "dp"), None, "seq", None, None),
            P(("parts", "dp"), None, "seq", None, None),
            P(None, "seq", None),
            P("parts", None),
        ),
        out_specs=P("parts", "seq", "dp"),
        check_vma=False,
    )
```

```python
import functools
import math

import jax
import jax.numpy as jnp
from jax import lax
from jax.experimental import pallas as pl
from jax.experimental.pallas import tpu as pltpu
from jax.sharding import PartitionSpec as P

MAXCLIP = 3
VALUES = 2
OTHERS = (0, 1, 3)
TILE = 8
EPS = 1e-06
VMEM_LIMIT = 48 * 1024 * 1024
PACK_VMEM_LIMIT = 53 * 1024 * 1024


def head_chunks(heads):
    sizes = {8: (4, 3, 1)}.get(heads)
    if sizes is None:
        sizes = (1,) * heads if heads <= 2 else (heads - heads // 2, heads // 2)
    bounds, start = [], 0
    for size in sizes:
        bounds.append((start, start + size))
        start += size
    return bounds


def tile_start(heads, flip):
    head = jnp.bitwise_xor(lax.axis_index("seq"), flip) * heads
    offset = 0 if heads % TILE == 0 else lax.rem(head, TILE)
    return pl.multiple_of((head // TILE) * TILE, TILE), offset


def cut_kernel(flips, heads, array, *refs):
    outs, token, sems = refs[:-2], refs[-2], refs[-1]
    token[...] = jnp.zeros_like(token)
    copies = []
    for index, flip in enumerate(flips):
        start, _ = tile_start(heads, flip)
        source = array.at[0, :, :, pl.ds(start, outs[index].shape[2]), :]
        copies.append(pltpu.make_async_copy(source, outs[index], sems.at[index]))
        copies[-1].start()
    for copy in copies:
        copy.wait()


def cut(array, flips, heads):
    _, slots, rows, _, size = array.shape
    shape = jax.ShapeDtypeStruct((slots, rows, max(heads, TILE), size), array.dtype)
    return pl.pallas_call(
        functools.partial(cut_kernel, flips, heads),
        out_shape=[shape] * len(flips) + [jax.ShapeDtypeStruct((TILE, size), jnp.float32)],
        in_specs=[pl.BlockSpec(memory_space=pltpu.HBM)],
        out_specs=[pl.BlockSpec(memory_space=pltpu.VMEM)] * (len(flips) + 1),
        scratch_shapes=[pltpu.SemaphoreType.DMA((len(flips),))],
        compiler_params=pltpu.CompilerParams(vmem_limit_bytes=PACK_VMEM_LIMIT),
        name="cut",
    )(array)


def arrange_kernel(*refs):
    pieces, out, wide = refs[:-2], refs[-2], refs[-1]
    heads, slots = out.shape[:2]
    rows, held = pieces[0].shape[1:3]
    _, offset = tile_start(heads, 0)
    for source, piece in enumerate(pieces):
        for slot in range(slots):
            for span in range(held // TILE):
                place = (source * slots + slot) % wide.shape[0]
                block = piece[slot, :, span * TILE : (span + 1) * TILE, :]
                wide[place] = block.astype(jnp.float32).reshape(rows * TILE, wide.shape[-1])
                for head in range(span * TILE, min(heads, (span + 1) * TILE)):
                    out[head, slot, source * rows : (source + 1) * rows, :] = wide[
                        place, pl.ds(offset + head - span * TILE, rows, stride=TILE), :
                    ].astype(jnp.bfloat16)


def arrange(pieces, heads):
    slots, rows, held, size = pieces[0].shape
    moved = len(pieces) * slots * rows * held * size * 2
    return pl.pallas_call(
        arrange_kernel,
        out_shape=jax.ShapeDtypeStruct((heads, slots, len(pieces) * rows, size), jnp.bfloat16),
        in_specs=[pl.BlockSpec(memory_space=pltpu.VMEM)] * len(pieces),
        out_specs=pl.BlockSpec(memory_space=pltpu.VMEM),
        scratch_shapes=[pltpu.VMEM((slots, rows * TILE, size), jnp.float32)],
        compiler_params=pltpu.CompilerParams(vmem_limit_bytes=VMEM_LIMIT),
        cost_estimate=pl.CostEstimate(flops=moved, bytes_accessed=2 * moved, transcendentals=0),
        name="arrange",
    )(*pieces)


def pack_kernel(plan, heads, after, *refs):
    arrays = refs[:4]
    outs = refs[4 + after : 4 + after + sum(len(chunks) for _, _, chunks in plan)]
    token, raw, wide, sems = refs[4 + after + len(outs) :]
    token[...] = jnp.zeros_like(token)
    slots, rows = raw.shape[2], raw.shape[3]
    spans = max(1, heads // TILE)

    def copy(index, array, span, first):
        return pltpu.make_async_copy(
            arrays[array].at[0, :, :, pl.ds(first + span * TILE, TILE), :],
            raw.at[index, array * spans + span],
            sems.at[index, array * spans + span],
        )

    firsts, offsets = zip(*[tile_start(heads, flip) for flip, _, _ in plan])
    for index, (_, wanted, _) in enumerate(plan):
        for array in wanted:
            for span in range(spans):
                copy(index, array, span, firsts[index]).start()
    place = 0
    for index, (_, wanted, chunks) in enumerate(plan):
        for position, array in enumerate(wanted):
            for span in range(spans):
                copy(index, array, span, firsts[index]).wait()
                for slot in range(slots):
                    wide[slot] = (
                        raw[index, array * spans + span, slot]
                        .astype(jnp.float32)
                        .reshape(rows * TILE, wide.shape[-1])
                    )
                    for number, (low, high) in enumerate(chunks):
                        for head in range(max(low, span * TILE), min(high, (span + 1) * TILE)):
                            outs[place + number][head - low, position, slot * rows : (slot + 1) * rows, :] = wide[
                                slot, pl.ds(offsets[index] + head - span * TILE, rows, stride=TILE), :
                            ].astype(jnp.bfloat16)
        place += len(chunks)


def pack(arrays, plan, heads, after=()):
    _, slots, rows, _, size = arrays[0].shape
    spans = max(1, heads // TILE)
    shapes = [
        jax.ShapeDtypeStruct((high - low, len(wanted), slots * rows, size), jnp.bfloat16)
        for _, wanted, chunks in plan
        for low, high in chunks
    ] + [jax.ShapeDtypeStruct((TILE, size), jnp.float32)]
    count = len(plan)
    moved = count * 4 * spans * slots * rows * TILE * size * 2
    return pl.pallas_call(
        functools.partial(pack_kernel, plan, heads, len(after)),
        out_shape=shapes,
        in_specs=[pl.BlockSpec(memory_space=pltpu.HBM)] * 4 + [pl.BlockSpec(memory_space=pl.ANY)] * len(after),
        out_specs=[pl.BlockSpec(memory_space=pltpu.VMEM)] * len(shapes),
        scratch_shapes=[
            pltpu.VMEM((count, 4 * spans, slots, rows, TILE, size), jnp.bfloat16),
            pltpu.VMEM((slots, rows * TILE, size), jnp.float32),
            pltpu.SemaphoreType.DMA((count, 4 * spans)),
        ],
        compiler_params=pltpu.CompilerParams(vmem_limit_bytes=PACK_VMEM_LIMIT),
        cost_estimate=pl.CostEstimate(flops=moved, bytes_accessed=2 * moved, transcendentals=0),
        name="pack",
    )(*arrays, *after)


def contract_last(left, right):
    return lax.dot_general(left, right, (((1,), (1,)), ((), ())), preferred_element_type=jnp.float32)


def layouts(slots):
    found = []

    def extend(start, clips):
        if start == slots:
            found.append(tuple(clips))
        for span in range(1, min(MAXCLIP, slots - start) + 1):
            extend(start + span, clips + [(start, span)])

    extend(0, [])
    return found


def normalized(block, gain):
    wide = block.astype(jnp.float32)
    wide = wide * lax.rsqrt(jnp.mean(wide * wide, axis=-1, keepdims=True) + EPS)
    return (wide * gain).astype(jnp.bfloat16)


def prepare_kernel(low, after, gains, *refs):
    pieces, out = refs[after:-1], refs[-1]
    heads, _, tokens, _ = pieces[0].shape
    slots = out.shape[2]
    rows = tokens // slots
    for head in range(heads):
        for array in range(4):
            for source, piece in enumerate(pieces[array // 2 :: 2]):
                block = piece[head, array % 2]
                if array < 2:
                    block = normalized(block, gains[array, low + head : low + head + 1, :])
                for slot in range(slots):
                    out[head, array, slot, source * rows : (source + 1) * rows, :] = block[
                        slot * rows : (slot + 1) * rows
                    ]


def prepare(low, gains, pieces, slots, after):
    heads, _, tokens, size = pieces[0].shape
    moved = len(pieces) * heads * 2 * tokens * size * 2
    return pl.pallas_call(
        functools.partial(prepare_kernel, low, len(after)),
        out_shape=jax.ShapeDtypeStruct((heads, 4, slots, len(pieces) // 2 * tokens // slots, size), jnp.bfloat16),
        in_specs=[pl.BlockSpec(memory_space=pltpu.VMEM)] * (1 + len(after) + len(pieces)),
        out_specs=pl.BlockSpec(memory_space=pltpu.VMEM),
        compiler_params=pltpu.CompilerParams(vmem_limit_bytes=VMEM_LIMIT),
        cost_estimate=pl.CostEstimate(flops=1, bytes_accessed=1, transcendentals=0),
        name="prepare",
    )(gains, *after, *pieces)


def attention_chunk(low, count, units, gains, values, close, pieces, held, total):
    query, key, value, grad = held
    group = lax.axis_index("dp")
    _, _, tokens, size = pieces[0].shape
    slots, near = close.shape[2:4]
    rows = tokens // slots
    unit = near + rows * len(pieces)
    for head in range(count):
        for array, kept in enumerate(held):
            for slot in range(slots):
                kept[head, slot * unit : slot * unit + near, :] = close[head, array, slot]
                if array == VALUES:
                    kept[head, slot * unit + near : (slot + 1) * unit, :] = values[low + head, slot]
            if array == VALUES:
                continue
            for source, piece in enumerate(pieces):
                block = piece[head, OTHERS.index(array)]
                if array < 2:
                    block = normalized(block, gains[array, low + head : low + head + 1, :])
                for slot in range(slots):
                    start = slot * unit + near + source * rows
                    kept[head, start : start + rows, :] = block[slot * rows : (slot + 1) * rows]
    factor = size ** (-0.5) * math.log2(math.e)

    def clip(head, slot, span):
        where = slice(slot * unit, (slot + span) * unit)
        q, k = query[head, where, :], key[head, where, :]
        expo = jnp.exp2(contract_last(k, q) * factor)
        dprob = contract_last(value[head, where, :], grad[head, where, :])
        prob = expo * (1.0 / jnp.sum(expo, axis=0, keepdims=True))
        delta = jnp.sum(prob * dprob, axis=0, keepdims=True)
        dscore = (prob * (dprob - delta)).astype(jnp.bfloat16)
        mixed = jnp.dot(dscore, q, preferred_element_type=jnp.float32)
        return jnp.sum(mixed * k.astype(jnp.float32), axis=0, keepdims=True)

    table = units[...]
    rows_of, slots_of = (lax.broadcasted_iota(jnp.int32, table.shape, dim) for dim in (0, 1))
    starts = jnp.where((rows_of == group) & (table > 0), lax.shift_left(jnp.int32(1), slots_of), 0)
    begins = jnp.sum(starts)
    for layout in layouts(slots):

        @pl.when(begins == sum(1 << slot for slot, _ in layout))
        def _():
            for head in range(count):
                total[head : head + 1, :] = sum(clip(head, slot, span) for slot, span in layout)


def chunk_kernel(low, units, gains, values, close, *refs):
    pieces, out, held = refs[:-5], refs[-5], refs[-4:]
    attention_chunk(low, out.shape[0], units, gains, values, close, pieces, held, out)


def last_kernel(low, sources, earlier, peers, units, gains, values, close, *refs):
    pieces = refs[:sources]
    before = refs[sources : sources + earlier]
    outs = refs[sources + earlier : sources + earlier + len(peers)]
    held, total = refs[sources + earlier + len(peers) : -1], refs[-1]
    attention_chunk(low, total.shape[0], units, gains, values, close, pieces, held, total)
    group = lax.axis_index("dp")
    size = total.shape[-1]
    width = outs[0].shape[-1]
    scaled = jnp.concatenate([ref[...] for ref in before] + [total[...]], axis=0) * (size ** (-0.5))
    for side in range(2):
        grads = scaled / gains[side]
        for out, targets in zip(outs, peers):
            target = sum(jnp.where(group == place, whom, 0) for place, whom in enumerate(targets))
            shift = lax.rem(size - target * width, size)
            out[side] = pltpu.roll(grads, shift, 1)[:, :width]


def attend(low, count, units, gains, values, close, pieces, earlier=None, peers=None):
    _, _, tokens, size = pieces[0].shape
    all_tokens = close.shape[2] * close.shape[3] + tokens * len(pieces)
    held = [pltpu.VMEM((count, all_tokens, size), jnp.bfloat16)] * 4
    if earlier is None:
        kernel = functools.partial(chunk_kernel, low)
        shapes = jax.ShapeDtypeStruct((count, size), jnp.float32)
        earlier = []
        outs = pl.BlockSpec(memory_space=pltpu.VMEM)
    else:
        kernel = functools.partial(last_kernel, low, len(pieces), len(earlier), peers)
        heads = gains.shape[1]
        shapes = [jax.ShapeDtypeStruct((2, heads, size // len(peers)), jnp.float32)] * len(peers)
        held.append(pltpu.VMEM((count, size), jnp.float32))
        outs = [pl.BlockSpec(memory_space=pltpu.VMEM)] * len(peers)
    pairs = count * all_tokens * all_tokens // 2
    return pl.pallas_call(
        kernel,
        out_shape=shapes,
        in_specs=[pl.BlockSpec(memory_space=pltpu.VMEM)] * (4 + len(pieces) + len(earlier)),
        out_specs=outs,
        scratch_shapes=held,
        compiler_params=pltpu.CompilerParams(vmem_limit_bytes=VMEM_LIMIT),
        cost_estimate=pl.CostEstimate(
            flops=6 * pairs * size, bytes_accessed=len(pieces) * count * 4 * tokens * size * 2, transcendentals=pairs
        ),
        name="attend",
    )(units, gains, values, close, *pieces, *earlier)


def seen_kernel(*refs):
    refs[-1][...] = jnp.zeros_like(refs[-1])


def seen(blocks):
    return pl.pallas_call(
        seen_kernel,
        out_shape=jax.ShapeDtypeStruct((TILE, blocks[0].shape[-1]), jnp.float32),
        in_specs=[pl.BlockSpec(memory_space=pl.ANY)] * len(blocks),
        out_specs=pl.BlockSpec(memory_space=pltpu.VMEM),
        compiler_params=pltpu.CompilerParams(vmem_limit_bytes=1024 * 1024),
        cost_estimate=pl.CostEstimate(flops=1, bytes_accessed=1024 * 1024, transcendentals=0),
        name="seen",
    )(*blocks)


def ring_targets(groups):
    ring = [0] + list(range(1, groups, 2)) + list(range(2, groups, 2))[::-1]
    return [[ring[(ring.index(place) + step) % groups] for place in range(groups)] for step in range(groups)]


def body(sequence, groups, queries, key_rows, value_rows, out_grad, norm_gains, clip_units):
    arrays = (queries, key_rows, value_rows, out_grad)
    heads = norm_gains.shape[1]
    chunks = head_chunks(heads)
    far = list(range(2, sequence)) or [1]
    near = [flip for flip in range(1, sequence) if flip not in far]

    def send(block, flip):
        return lax.ppermute(block, "seq", [(s, s ^ flip) for s in range(sequence)])

    slots = clip_units.shape[1]
    peers = ring_targets(groups)
    close = near + [0]

    def pack_and_send(plan, after):
        *blocks, token = pack(arrays, plan, heads, after)
        flips = [flip for flip, _, wanted in plan for _ in wanted]
        return [send(block, flip) if flip else block for flip, block in zip(flips, blocks)], token

    def far_plan(number):
        return [(flip, OTHERS, chunks[number : number + 1]) for flip in far]

    *tiles, token = cut(arrays[VALUES], far, heads)
    tiles = [send(block, flip) for flip, block in zip(far, tiles)]
    received, token = pack_and_send(far_plan(0), [token])
    later = far_plan(1) if len(chunks) > 1 else []
    whole = [(flip, pair, chunks) for flip in close for pair in ((0, 1), (2, 3))]
    blocks, _ = pack_and_send(later + whole, [token, seen(tiles)])
    values = arrange(tiles, heads)
    prepared = [
        prepare(low, norm_gains, blocks[len(later) + number :: len(chunks)], slots, [] if number else [seen(received)])
        for number, (low, _) in enumerate(chunks)
    ]
    waiting, sums = blocks[: len(later)], []
    for number, (low, high) in enumerate(chunks[:-1]):
        sums.append(attend(low, high - low, clip_units, norm_gains, values, prepared[number], received))
        received = waiting
        if number + 2 < len(chunks):
            waiting, _ = pack_and_send(far_plan(number + 2), sums[-1:])
    low, high = chunks[-1]
    parts = attend(
        low, high - low, clip_units, norm_gains, values, prepared[-1], received, sums, peers
    )
    result = parts[0]
    for part, targets in zip(parts[1:], peers[1:]):
        result = result + lax.ppermute(part, "dp", list(enumerate(targets)))
    return result


def solution(mesh):
    return jax.shard_map(
        functools.partial(body, mesh.shape["seq"], mesh.shape["dp"]),
        mesh=mesh,
        in_specs=(
            P(("parts", "dp"), None, "seq", None, None),
            P(("parts", "dp"), None, "seq", None, None),
            P(("parts", "dp"), None, "seq", None, None),
            P(("parts", "dp"), None, "seq", None, None),
            P(None, "seq", None),
            P("parts", None),
        ),
        out_specs=P("parts", "seq", "dp"),
        check_vma=False,
    )
```

```python
import functools
import math

import jax
import jax.numpy as jnp
from jax import lax
from jax.experimental import pallas as pl
from jax.experimental.pallas import tpu as pltpu
from jax.sharding import PartitionSpec as P

MAXCLIP = 3
VALUES = 2
OTHERS = (0, 1, 3)
TILE = 8
EPS = 1e-06
VMEM_LIMIT = 48 * 1024 * 1024
PACK_VMEM_LIMIT = 53 * 1024 * 1024


def head_chunks(heads):
    sizes = {8: (4, 3, 1)}.get(heads)
    if sizes is None:
        sizes = (1,) * heads if heads <= 2 else (heads - heads // 2, heads // 2)
    bounds, start = [], 0
    for size in sizes:
        bounds.append((start, start + size))
        start += size
    return bounds


def tile_start(heads, flip):
    head = jnp.bitwise_xor(lax.axis_index("seq"), flip) * heads
    offset = 0 if heads % TILE == 0 else lax.rem(head, TILE)
    return pl.multiple_of((head // TILE) * TILE, TILE), offset


def cut_kernel(flips, heads, after, array, *refs):
    outs, token, sems = refs[after:-2], refs[-2], refs[-1]
    token[...] = jnp.zeros_like(token)
    copies = []
    for index, flip in enumerate(flips):
        start, _ = tile_start(heads, flip)
        source = array.at[0, :, :, pl.ds(start, outs[index].shape[2]), :]
        copies.append(pltpu.make_async_copy(source, outs[index], sems.at[index]))
        copies[-1].start()
    for copy in copies:
        copy.wait()


def cut(array, flips, heads, after):
    _, slots, rows, _, size = array.shape
    shape = jax.ShapeDtypeStruct((slots, rows, max(heads, TILE), size), array.dtype)
    return pl.pallas_call(
        functools.partial(cut_kernel, flips, heads, len(after)),
        out_shape=[shape] * len(flips) + [jax.ShapeDtypeStruct((TILE, size), jnp.float32)],
        in_specs=[pl.BlockSpec(memory_space=pltpu.HBM)] + [pl.BlockSpec(memory_space=pl.ANY)] * len(after),
        out_specs=[pl.BlockSpec(memory_space=pltpu.VMEM)] * (len(flips) + 1),
        scratch_shapes=[pltpu.SemaphoreType.DMA((len(flips),))],
        compiler_params=pltpu.CompilerParams(vmem_limit_bytes=PACK_VMEM_LIMIT),
        name="cut",
    )(array, *after)


def arrange_kernel(*refs):
    pieces, out, wide = refs[:-2], refs[-2], refs[-1]
    heads, slots = out.shape[:2]
    rows, held = pieces[0].shape[1:3]
    _, offset = tile_start(heads, 0)
    for source, piece in enumerate(pieces):
        for slot in range(slots):
            for span in range(held // TILE):
                place = (source * slots + slot) % wide.shape[0]
                block = piece[slot, :, span * TILE : (span + 1) * TILE, :]
                wide[place] = block.astype(jnp.float32).reshape(rows * TILE, wide.shape[-1])
                for head in range(span * TILE, min(heads, (span + 1) * TILE)):
                    out[head, slot, source * rows : (source + 1) * rows, :] = wide[
                        place, pl.ds(offset + head - span * TILE, rows, stride=TILE), :
                    ].astype(jnp.bfloat16)


def arrange(pieces, heads):
    slots, rows, held, size = pieces[0].shape
    moved = len(pieces) * slots * rows * held * size * 2
    return pl.pallas_call(
        arrange_kernel,
        out_shape=jax.ShapeDtypeStruct((heads, slots, len(pieces) * rows, size), jnp.bfloat16),
        in_specs=[pl.BlockSpec(memory_space=pltpu.VMEM)] * len(pieces),
        out_specs=pl.BlockSpec(memory_space=pltpu.VMEM),
        scratch_shapes=[pltpu.VMEM((slots, rows * TILE, size), jnp.float32)],
        compiler_params=pltpu.CompilerParams(vmem_limit_bytes=VMEM_LIMIT),
        cost_estimate=pl.CostEstimate(flops=moved, bytes_accessed=2 * moved, transcendentals=0),
        name="arrange",
    )(*pieces)


def pack_kernel(plan, heads, after, *refs):
    arrays = refs[:4]
    outs = refs[4 + after : 4 + after + sum(len(chunks) for _, _, chunks in plan)]
    token, raw, wide, sems = refs[4 + after + len(outs) :]
    token[...] = jnp.zeros_like(token)
    slots, rows = raw.shape[2], raw.shape[3]
    spans = max(1, heads // TILE)

    def copy(index, array, span, first):
        return pltpu.make_async_copy(
            arrays[array].at[0, :, :, pl.ds(first + span * TILE, TILE), :],
            raw.at[index, array * spans + span],
            sems.at[index, array * spans + span],
        )

    firsts, offsets = zip(*[tile_start(heads, flip) for flip, _, _ in plan])
    for index, (_, wanted, _) in enumerate(plan):
        for array in wanted:
            for span in range(spans):
                copy(index, array, span, firsts[index]).start()
    place = 0
    for index, (_, wanted, chunks) in enumerate(plan):
        for position, array in enumerate(wanted):
            for span in range(spans):
                copy(index, array, span, firsts[index]).wait()
                for slot in range(slots):
                    wide[slot] = (
                        raw[index, array * spans + span, slot]
                        .astype(jnp.float32)
                        .reshape(rows * TILE, wide.shape[-1])
                    )
                    for number, (low, high) in enumerate(chunks):
                        for head in range(max(low, span * TILE), min(high, (span + 1) * TILE)):
                            outs[place + number][head - low, position, slot * rows : (slot + 1) * rows, :] = wide[
                                slot, pl.ds(offsets[index] + head - span * TILE, rows, stride=TILE), :
                            ].astype(jnp.bfloat16)
        place += len(chunks)


def pack(arrays, plan, heads, after=()):
    _, slots, rows, _, size = arrays[0].shape
    spans = max(1, heads // TILE)
    shapes = [
        jax.ShapeDtypeStruct((high - low, len(wanted), slots * rows, size), jnp.bfloat16)
        for _, wanted, chunks in plan
        for low, high in chunks
    ] + [jax.ShapeDtypeStruct((TILE, size), jnp.float32)]
    count = len(plan)
    moved = count * 4 * spans * slots * rows * TILE * size * 2
    return pl.pallas_call(
        functools.partial(pack_kernel, plan, heads, len(after)),
        out_shape=shapes,
        in_specs=[pl.BlockSpec(memory_space=pltpu.HBM)] * 4 + [pl.BlockSpec(memory_space=pl.ANY)] * len(after),
        out_specs=[pl.BlockSpec(memory_space=pltpu.VMEM)] * len(shapes),
        scratch_shapes=[
            pltpu.VMEM((count, 4 * spans, slots, rows, TILE, size), jnp.bfloat16),
            pltpu.VMEM((slots, rows * TILE, size), jnp.float32),
            pltpu.SemaphoreType.DMA((count, 4 * spans)),
        ],
        compiler_params=pltpu.CompilerParams(vmem_limit_bytes=PACK_VMEM_LIMIT),
        cost_estimate=pl.CostEstimate(flops=moved, bytes_accessed=2 * moved, transcendentals=0),
        name="pack",
    )(*arrays, *after)


def contract_last(left, right):
    return lax.dot_general(left, right, (((1,), (1,)), ((), ())), preferred_element_type=jnp.float32)


def layouts(slots):
    found = []

    def extend(start, clips):
        if start == slots:
            found.append(tuple(clips))
        for span in range(1, min(MAXCLIP, slots - start) + 1):
            extend(start + span, clips + [(start, span)])

    extend(0, [])
    return found


def normalized(block, gain):
    wide = block.astype(jnp.float32)
    wide = wide * lax.rsqrt(jnp.mean(wide * wide, axis=-1, keepdims=True) + EPS)
    return (wide * gain).astype(jnp.bfloat16)


def prepare_kernel(low, after, gains, *refs):
    pieces, out = refs[after:-1], refs[-1]
    heads, _, tokens, _ = pieces[0].shape
    slots = out.shape[2]
    rows = tokens // slots
    for head in range(heads):
        for array in range(4):
            for source, piece in enumerate(pieces[array // 2 :: 2]):
                block = piece[head, array % 2]
                if array < 2:
                    block = normalized(block, gains[array, low + head : low + head + 1, :])
                for slot in range(slots):
                    out[head, array, slot, source * rows : (source + 1) * rows, :] = block[
                        slot * rows : (slot + 1) * rows
                    ]


def prepare(low, gains, pieces, slots, after):
    heads, _, tokens, size = pieces[0].shape
    moved = len(pieces) * heads * 2 * tokens * size * 2
    return pl.pallas_call(
        functools.partial(prepare_kernel, low, len(after)),
        out_shape=jax.ShapeDtypeStruct((heads, 4, slots, len(pieces) // 2 * tokens // slots, size), jnp.bfloat16),
        in_specs=[pl.BlockSpec(memory_space=pltpu.VMEM)] * (1 + len(after) + len(pieces)),
        out_specs=pl.BlockSpec(memory_space=pltpu.VMEM),
        compiler_params=pltpu.CompilerParams(vmem_limit_bytes=VMEM_LIMIT),
        cost_estimate=pl.CostEstimate(flops=1, bytes_accessed=1, transcendentals=0),
        name="prepare",
    )(gains, *after, *pieces)


def attention_chunk(low, count, units, gains, values, close, pieces, held, total):
    query, key, value, grad = held
    group = lax.axis_index("dp")
    _, _, tokens, size = pieces[0].shape
    slots, near = close.shape[2:4]
    rows = tokens // slots
    unit = near + rows * len(pieces)
    for head in range(count):
        for array, kept in enumerate(held):
            for slot in range(slots):
                kept[head, slot * unit : slot * unit + near, :] = close[head, array, slot]
                if array == VALUES:
                    kept[head, slot * unit + near : (slot + 1) * unit, :] = values[low + head, slot]
            if array == VALUES:
                continue
            for source, piece in enumerate(pieces):
                block = piece[head, OTHERS.index(array)]
                if array < 2:
                    block = normalized(block, gains[array, low + head : low + head + 1, :])
                for slot in range(slots):
                    start = slot * unit + near + source * rows
                    kept[head, start : start + rows, :] = block[slot * rows : (slot + 1) * rows]
    factor = size ** (-0.5) * math.log2(math.e)

    def clip(head, slot, span):
        where = slice(slot * unit, (slot + span) * unit)
        q, k = query[head, where, :], key[head, where, :]
        expo = jnp.exp2(contract_last(k, q) * factor)
        dprob = contract_last(value[head, where, :], grad[head, where, :])
        prob = expo * (1.0 / jnp.sum(expo, axis=0, keepdims=True))
        delta = jnp.sum(prob * dprob, axis=0, keepdims=True)
        dscore = (prob * (dprob - delta)).astype(jnp.bfloat16)
        mixed = jnp.dot(dscore, q, preferred_element_type=jnp.float32)
        return jnp.sum(mixed * k.astype(jnp.float32), axis=0, keepdims=True)

    table = units[...]
    rows_of, slots_of = (lax.broadcasted_iota(jnp.int32, table.shape, dim) for dim in (0, 1))
    starts = jnp.where((rows_of == group) & (table > 0), lax.shift_left(jnp.int32(1), slots_of), 0)
    begins = jnp.sum(starts)
    for layout in layouts(slots):

        @pl.when(begins == sum(1 << slot for slot, _ in layout))
        def _():
            for head in range(count):
                total[head : head + 1, :] = sum(clip(head, slot, span) for slot, span in layout)


def chunk_kernel(low, units, gains, values, close, *refs):
    pieces, out, held = refs[:-5], refs[-5], refs[-4:]
    attention_chunk(low, out.shape[0], units, gains, values, close, pieces, held, out)


def last_kernel(low, sources, earlier, peers, units, gains, values, close, *refs):
    pieces = refs[:sources]
    before = refs[sources : sources + earlier]
    outs = refs[sources + earlier : sources + earlier + len(peers)]
    held, total = refs[sources + earlier + len(peers) : -1], refs[-1]
    attention_chunk(low, total.shape[0], units, gains, values, close, pieces, held, total)
    group = lax.axis_index("dp")
    size = total.shape[-1]
    width = outs[0].shape[-1]
    scaled = jnp.concatenate([ref[...] for ref in before] + [total[...]], axis=0) * (size ** (-0.5))
    for side in range(2):
        grads = scaled / gains[side]
        for out, targets in zip(outs, peers):
            target = sum(jnp.where(group == place, whom, 0) for place, whom in enumerate(targets))
            shift = lax.rem(size - target * width, size)
            out[side] = pltpu.roll(grads, shift, 1)[:, :width]


def attend(low, count, units, gains, values, close, pieces, earlier=None, peers=None):
    _, _, tokens, size = pieces[0].shape
    all_tokens = close.shape[2] * close.shape[3] + tokens * len(pieces)
    held = [pltpu.VMEM((count, all_tokens, size), jnp.bfloat16)] * 4
    if earlier is None:
        kernel = functools.partial(chunk_kernel, low)
        shapes = jax.ShapeDtypeStruct((count, size), jnp.float32)
        earlier = []
        outs = pl.BlockSpec(memory_space=pltpu.VMEM)
    else:
        kernel = functools.partial(last_kernel, low, len(pieces), len(earlier), peers)
        heads = gains.shape[1]
        shapes = [jax.ShapeDtypeStruct((2, heads, size // len(peers)), jnp.float32)] * len(peers)
        held.append(pltpu.VMEM((count, size), jnp.float32))
        outs = [pl.BlockSpec(memory_space=pltpu.VMEM)] * len(peers)
    pairs = count * all_tokens * all_tokens // 2
    return pl.pallas_call(
        kernel,
        out_shape=shapes,
        in_specs=[pl.BlockSpec(memory_space=pltpu.VMEM)] * (4 + len(pieces) + len(earlier)),
        out_specs=outs,
        scratch_shapes=held,
        compiler_params=pltpu.CompilerParams(vmem_limit_bytes=VMEM_LIMIT),
        cost_estimate=pl.CostEstimate(
            flops=6 * pairs * size, bytes_accessed=len(pieces) * count * 4 * tokens * size * 2, transcendentals=pairs
        ),
        name="attend",
    )(units, gains, values, close, *pieces, *earlier)


def seen_kernel(*refs):
    refs[-1][...] = jnp.zeros_like(refs[-1])


def seen(blocks):
    return pl.pallas_call(
        seen_kernel,
        out_shape=jax.ShapeDtypeStruct((TILE, blocks[0].shape[-1]), jnp.float32),
        in_specs=[pl.BlockSpec(memory_space=pl.ANY)] * len(blocks),
        out_specs=pl.BlockSpec(memory_space=pltpu.VMEM),
        compiler_params=pltpu.CompilerParams(vmem_limit_bytes=1024 * 1024),
        cost_estimate=pl.CostEstimate(flops=1, bytes_accessed=1024 * 1024, transcendentals=0),
        name="seen",
    )(*blocks)


def ring_targets(groups):
    ring = [0] + list(range(1, groups, 2)) + list(range(2, groups, 2))[::-1]
    return [[ring[(ring.index(place) + step) % groups] for place in range(groups)] for step in range(groups)]


def body(sequence, groups, queries, key_rows, value_rows, out_grad, norm_gains, clip_units):
    arrays = (queries, key_rows, value_rows, out_grad)
    heads = norm_gains.shape[1]
    chunks = head_chunks(heads)
    far = list(range(2, sequence)) or [1]
    near = [flip for flip in range(1, sequence) if flip not in far]

    def send(block, flip):
        return lax.ppermute(block, "seq", [(s, s ^ flip) for s in range(sequence)])

    slots = clip_units.shape[1]
    peers = ring_targets(groups)
    close = near + [0]

    def pack_and_send(plan, after):
        *blocks, token = pack(arrays, plan, heads, after)
        flips = [flip for flip, _, wanted in plan for _ in wanted]
        return [send(block, flip) if flip else block for flip, block in zip(flips, blocks)], token

    def far_plan(number):
        return [(flip, OTHERS, chunks[number : number + 1]) for flip in far]

    tiles, tokens = [], []
    for flip in far:
        block, token = cut(arrays[VALUES], [flip], heads, tokens)
        tiles.append(send(block, flip))
        tokens = [token]
    received, token = pack_and_send(far_plan(0), tokens)
    later = far_plan(1) if len(chunks) > 1 else []
    whole = [(flip, pair, chunks) for flip in close for pair in ((0, 1), (2, 3))]
    arrived = []
    for tile in tiles:
        arrived = [seen([tile] + arrived)]
    blocks, _ = pack_and_send(later + whole, [token] + arrived)
    values = arrange(tiles, heads)
    prepared = [
        prepare(low, norm_gains, blocks[len(later) + number :: len(chunks)], slots, [] if number else [seen(received)])
        for number, (low, _) in enumerate(chunks)
    ]
    waiting, sums = blocks[: len(later)], []
    for number, (low, high) in enumerate(chunks[:-1]):
        sums.append(attend(low, high - low, clip_units, norm_gains, values, prepared[number], received))
        received = waiting
        if number + 2 < len(chunks):
            waiting, _ = pack_and_send(far_plan(number + 2), sums[-1:])
    low, high = chunks[-1]
    parts = attend(
        low, high - low, clip_units, norm_gains, values, prepared[-1], received, sums, peers
    )
    result = parts[0]
    for part, targets in zip(parts[1:], peers[1:]):
        result = result + lax.ppermute(part, "dp", list(enumerate(targets)))
    return result


def solution(mesh):
    return jax.shard_map(
        functools.partial(body, mesh.shape["seq"], mesh.shape["dp"]),
        mesh=mesh,
        in_specs=(
            P(("parts", "dp"), None, "seq", None, None),
            P(("parts", "dp"), None, "seq", None, None),
            P(("parts", "dp"), None, "seq", None, None),
            P(("parts", "dp"), None, "seq", None, None),
            P(None, "seq", None),
            P("parts", None),
        ),
        out_specs=P("parts", "seq", "dp"),
        check_vma=False,
    )
```

```python
import functools
import math

import jax
import jax.numpy as jnp
from jax import lax
from jax.experimental import pallas as pl
from jax.experimental.pallas import tpu as pltpu
from jax.sharding import PartitionSpec as P

MAXCLIP = 3
VALUES = 2
OTHERS = (0, 1, 3)
TILE = 8
EPS = 1e-06
VMEM_LIMIT = 48 * 1024 * 1024
PACK_VMEM_LIMIT = 53 * 1024 * 1024


def head_chunks(heads):
    sizes = {8: (4, 3, 1)}.get(heads)
    if sizes is None:
        sizes = (1,) * heads if heads <= 2 else (heads - heads // 2, heads // 2)
    bounds, start = [], 0
    for size in sizes:
        bounds.append((start, start + size))
        start += size
    return bounds


def tile_start(heads, flip):
    head = jnp.bitwise_xor(lax.axis_index("seq"), flip) * heads
    offset = 0 if heads % TILE == 0 else lax.rem(head, TILE)
    return pl.multiple_of((head // TILE) * TILE, TILE), offset


def cut_kernel(flips, heads, array, *refs):
    outs, token, sems = refs[:-2], refs[-2], refs[-1]
    token[...] = jnp.zeros_like(token)
    copies = []
    for index, flip in enumerate(flips):
        start, _ = tile_start(heads, flip)
        source = array.at[0, :, :, pl.ds(start, outs[index].shape[2]), :]
        copies.append(pltpu.make_async_copy(source, outs[index], sems.at[index]))
        copies[-1].start()
    for copy in copies:
        copy.wait()


def cut(array, flips, heads):
    _, slots, rows, _, size = array.shape
    shape = jax.ShapeDtypeStruct((slots, rows, max(heads, TILE), size), array.dtype)
    return pl.pallas_call(
        functools.partial(cut_kernel, flips, heads),
        out_shape=[shape] * len(flips) + [jax.ShapeDtypeStruct((TILE, size), jnp.float32)],
        in_specs=[pl.BlockSpec(memory_space=pltpu.HBM)],
        out_specs=[pl.BlockSpec(memory_space=pltpu.VMEM)] * (len(flips) + 1),
        scratch_shapes=[pltpu.SemaphoreType.DMA((len(flips),))],
        compiler_params=pltpu.CompilerParams(vmem_limit_bytes=PACK_VMEM_LIMIT),
        name="cut",
    )(array)


def arrange_kernel(*refs):
    pieces, out, wide = refs[:-2], refs[-2], refs[-1]
    heads, slots = out.shape[:2]
    rows, held = pieces[0].shape[1:3]
    _, offset = tile_start(heads, 0)
    for source, piece in enumerate(pieces):
        for slot in range(slots):
            for span in range(held // TILE):
                place = (source * slots + slot) % wide.shape[0]
                block = piece[slot, :, span * TILE : (span + 1) * TILE, :]
                wide[place] = block.astype(jnp.float32).reshape(rows * TILE, wide.shape[-1])
                for head in range(span * TILE, min(heads, (span + 1) * TILE)):
                    out[head, slot, source * rows : (source + 1) * rows, :] = wide[
                        place, pl.ds(offset + head - span * TILE, rows, stride=TILE), :
                    ].astype(jnp.bfloat16)


def arrange(pieces, heads):
    slots, rows, held, size = pieces[0].shape
    moved = len(pieces) * slots * rows * held * size * 2
    return pl.pallas_call(
        arrange_kernel,
        out_shape=jax.ShapeDtypeStruct((heads, slots, len(pieces) * rows, size), jnp.bfloat16),
        in_specs=[pl.BlockSpec(memory_space=pltpu.VMEM)] * len(pieces),
        out_specs=pl.BlockSpec(memory_space=pltpu.VMEM),
        scratch_shapes=[pltpu.VMEM((slots, rows * TILE, size), jnp.float32)],
        compiler_params=pltpu.CompilerParams(vmem_limit_bytes=VMEM_LIMIT),
        cost_estimate=pl.CostEstimate(flops=moved, bytes_accessed=2 * moved, transcendentals=0),
        name="arrange",
    )(*pieces)


def pack_kernel(plan, heads, after, *refs):
    arrays = refs[:4]
    outs = refs[4 + after : 4 + after + sum(len(chunks) for _, _, chunks in plan)]
    token, raw, wide, sems = refs[4 + after + len(outs) :]
    token[...] = jnp.zeros_like(token)
    slots, rows = raw.shape[2], raw.shape[3]
    spans = max(1, heads // TILE)

    def copy(index, array, span, first):
        return pltpu.make_async_copy(
            arrays[array].at[0, :, :, pl.ds(first + span * TILE, TILE), :],
            raw.at[index, array * spans + span],
            sems.at[index, array * spans + span],
        )

    firsts, offsets = zip(*[tile_start(heads, flip) for flip, _, _ in plan])
    for index, (_, wanted, _) in enumerate(plan):
        for array in wanted:
            for span in range(spans):
                copy(index, array, span, firsts[index]).start()
    place = 0
    for index, (_, wanted, chunks) in enumerate(plan):
        for position, array in enumerate(wanted):
            for span in range(spans):
                copy(index, array, span, firsts[index]).wait()
                for slot in range(slots):
                    wide[slot] = (
                        raw[index, array * spans + span, slot]
                        .astype(jnp.float32)
                        .reshape(rows * TILE, wide.shape[-1])
                    )
                    for number, (low, high) in enumerate(chunks):
                        for head in range(max(low, span * TILE), min(high, (span + 1) * TILE)):
                            outs[place + number][head - low, position, slot * rows : (slot + 1) * rows, :] = wide[
                                slot, pl.ds(offsets[index] + head - span * TILE, rows, stride=TILE), :
                            ].astype(jnp.bfloat16)
        place += len(chunks)


def pack(arrays, plan, heads, after=()):
    _, slots, rows, _, size = arrays[0].shape
    spans = max(1, heads // TILE)
    shapes = [
        jax.ShapeDtypeStruct((high - low, len(wanted), slots * rows, size), jnp.bfloat16)
        for _, wanted, chunks in plan
        for low, high in chunks
    ] + [jax.ShapeDtypeStruct((TILE, size), jnp.float32)]
    count = len(plan)
    moved = count * 4 * spans * slots * rows * TILE * size * 2
    return pl.pallas_call(
        functools.partial(pack_kernel, plan, heads, len(after)),
        out_shape=shapes,
        in_specs=[pl.BlockSpec(memory_space=pltpu.HBM)] * 4 + [pl.BlockSpec(memory_space=pl.ANY)] * len(after),
        out_specs=[pl.BlockSpec(memory_space=pltpu.VMEM)] * len(shapes),
        scratch_shapes=[
            pltpu.VMEM((count, 4 * spans, slots, rows, TILE, size), jnp.bfloat16),
            pltpu.VMEM((slots, rows * TILE, size), jnp.float32),
            pltpu.SemaphoreType.DMA((count, 4 * spans)),
        ],
        compiler_params=pltpu.CompilerParams(vmem_limit_bytes=PACK_VMEM_LIMIT),
        cost_estimate=pl.CostEstimate(flops=moved, bytes_accessed=2 * moved, transcendentals=0),
        name="pack",
    )(*arrays, *after)


def contract_last(left, right):
    return lax.dot_general(left, right, (((1,), (1,)), ((), ())), preferred_element_type=jnp.float32)


def layouts(slots):
    found = []

    def extend(start, clips):
        if start == slots:
            found.append(tuple(clips))
        for span in range(1, min(MAXCLIP, slots - start) + 1):
            extend(start + span, clips + [(start, span)])

    extend(0, [])
    return found


def normalized(block, gain):
    wide = block.astype(jnp.float32)
    wide = wide * lax.rsqrt(jnp.mean(wide * wide, axis=-1, keepdims=True) + EPS)
    return (wide * gain).astype(jnp.bfloat16)


def prepare_kernel(low, after, gains, *refs):
    pieces, out = refs[after:-1], refs[-1]
    heads, _, tokens, _ = pieces[0].shape
    slots = out.shape[2]
    rows = tokens // slots
    for head in range(heads):
        for array in range(4):
            for source, piece in enumerate(pieces[array // 2 :: 2]):
                block = piece[head, array % 2]
                if array < 2:
                    block = normalized(block, gains[array, low + head : low + head + 1, :])
                for slot in range(slots):
                    out[head, array, slot, source * rows : (source + 1) * rows, :] = block[
                        slot * rows : (slot + 1) * rows
                    ]


def prepare(low, gains, pieces, slots, after):
    heads, _, tokens, size = pieces[0].shape
    moved = len(pieces) * heads * 2 * tokens * size * 2
    return pl.pallas_call(
        functools.partial(prepare_kernel, low, len(after)),
        out_shape=jax.ShapeDtypeStruct((heads, 4, slots, len(pieces) // 2 * tokens // slots, size), jnp.bfloat16),
        in_specs=[pl.BlockSpec(memory_space=pltpu.VMEM)] * (1 + len(after) + len(pieces)),
        out_specs=pl.BlockSpec(memory_space=pltpu.VMEM),
        compiler_params=pltpu.CompilerParams(vmem_limit_bytes=VMEM_LIMIT),
        cost_estimate=pl.CostEstimate(flops=1, bytes_accessed=1, transcendentals=0),
        name="prepare",
    )(gains, *after, *pieces)


def attention_chunk(low, count, units, gains, values, close, pieces, held, total):
    query, key, value, grad = held
    group = lax.axis_index("dp")
    _, _, tokens, size = pieces[0].shape
    slots, near = close.shape[2:4]
    rows = tokens // slots
    unit = near + rows * len(pieces)
    for head in range(count):
        for array, kept in enumerate(held):
            for slot in range(slots):
                kept[head, slot * unit : slot * unit + near, :] = close[head, array, slot]
                if array == VALUES:
                    kept[head, slot * unit + near : (slot + 1) * unit, :] = values[low + head, slot]
            if array == VALUES:
                continue
            for source, piece in enumerate(pieces):
                block = piece[head, OTHERS.index(array)]
                if array < 2:
                    block = normalized(block, gains[array, low + head : low + head + 1, :])
                for slot in range(slots):
                    start = slot * unit + near + source * rows
                    kept[head, start : start + rows, :] = block[slot * rows : (slot + 1) * rows]
    factor = size ** (-0.5) * math.log2(math.e)

    def attention(head, layout):
        blocks = [
            (slice(slot * unit, (slot + span) * unit), slice(place * unit, (place + 1) * unit))
            for slot, span in layout
            for place in range(slot, slot + span)
        ]
        scores = [contract_last(key[head, keys, :], query[head, own, :]) for keys, own in blocks]
        dprobs = [contract_last(value[head, keys, :], grad[head, own, :]) for keys, own in blocks]
        expos = [jnp.exp2(score * factor) for score in scores]
        shares = [1.0 / jnp.sum(expo, axis=0, keepdims=True) for expo in expos]
        probs = [expo * share for expo, share in zip(expos, shares)]
        deltas = [jnp.sum(prob * dprob, axis=0, keepdims=True) for prob, dprob in zip(probs, dprobs)]
        dscores = [
            (prob * (dprob - delta)).astype(jnp.bfloat16) for prob, dprob, delta in zip(probs, dprobs, deltas)
        ]
        mixed = [
            jnp.dot(dscore, query[head, own, :], preferred_element_type=jnp.float32)
            for dscore, (_, own) in zip(dscores, blocks)
        ]
        return sum(
            jnp.sum(part * key[head, keys, :].astype(jnp.float32), axis=0, keepdims=True)
            for part, (keys, _) in zip(mixed, blocks)
        )

    table = units[...]
    rows_of, slots_of = (lax.broadcasted_iota(jnp.int32, table.shape, dim) for dim in (0, 1))
    starts = jnp.where((rows_of == group) & (table > 0), lax.shift_left(jnp.int32(1), slots_of), 0)
    begins = jnp.sum(starts)
    for layout in layouts(slots):

        @pl.when(begins == sum(1 << slot for slot, _ in layout))
        def _():
            for head in range(count):
                total[head : head + 1, :] = attention(head, layout)


def chunk_kernel(low, units, gains, values, close, *refs):
    pieces, out, held = refs[:-5], refs[-5], refs[-4:]
    attention_chunk(low, out.shape[0], units, gains, values, close, pieces, held, out)


def last_kernel(low, sources, earlier, peers, units, gains, values, close, *refs):
    pieces = refs[:sources]
    before = refs[sources : sources + earlier]
    outs = refs[sources + earlier : sources + earlier + len(peers)]
    held, total = refs[sources + earlier + len(peers) : -1], refs[-1]
    attention_chunk(low, total.shape[0], units, gains, values, close, pieces, held, total)
    group = lax.axis_index("dp")
    size = total.shape[-1]
    width = outs[0].shape[-1]
    scaled = jnp.concatenate([ref[...] for ref in before] + [total[...]], axis=0) * (size ** (-0.5))
    for side in range(2):
        grads = scaled / gains[side]
        for out, targets in zip(outs, peers):
            target = sum(jnp.where(group == place, whom, 0) for place, whom in enumerate(targets))
            shift = lax.rem(size - target * width, size)
            out[side] = pltpu.roll(grads, shift, 1)[:, :width]


def attend(low, count, units, gains, values, close, pieces, earlier=None, peers=None):
    _, _, tokens, size = pieces[0].shape
    all_tokens = close.shape[2] * close.shape[3] + tokens * len(pieces)
    held = [pltpu.VMEM((count, all_tokens, size), jnp.bfloat16)] * 4
    if earlier is None:
        kernel = functools.partial(chunk_kernel, low)
        shapes = jax.ShapeDtypeStruct((count, size), jnp.float32)
        earlier = []
        outs = pl.BlockSpec(memory_space=pltpu.VMEM)
    else:
        kernel = functools.partial(last_kernel, low, len(pieces), len(earlier), peers)
        heads = gains.shape[1]
        shapes = [jax.ShapeDtypeStruct((2, heads, size // len(peers)), jnp.float32)] * len(peers)
        held.append(pltpu.VMEM((count, size), jnp.float32))
        outs = [pl.BlockSpec(memory_space=pltpu.VMEM)] * len(peers)
    pairs = count * all_tokens * all_tokens // 2
    return pl.pallas_call(
        kernel,
        out_shape=shapes,
        in_specs=[pl.BlockSpec(memory_space=pltpu.VMEM)] * (4 + len(pieces) + len(earlier)),
        out_specs=outs,
        scratch_shapes=held,
        compiler_params=pltpu.CompilerParams(vmem_limit_bytes=VMEM_LIMIT),
        cost_estimate=pl.CostEstimate(
            flops=6 * pairs * size, bytes_accessed=len(pieces) * count * 4 * tokens * size * 2, transcendentals=pairs
        ),
        name="attend",
    )(units, gains, values, close, *pieces, *earlier)


def seen_kernel(*refs):
    refs[-1][...] = jnp.zeros_like(refs[-1])


def seen(blocks):
    return pl.pallas_call(
        seen_kernel,
        out_shape=jax.ShapeDtypeStruct((TILE, blocks[0].shape[-1]), jnp.float32),
        in_specs=[pl.BlockSpec(memory_space=pl.ANY)] * len(blocks),
        out_specs=pl.BlockSpec(memory_space=pltpu.VMEM),
        compiler_params=pltpu.CompilerParams(vmem_limit_bytes=1024 * 1024),
        cost_estimate=pl.CostEstimate(flops=1, bytes_accessed=1024 * 1024, transcendentals=0),
        name="seen",
    )(*blocks)


def ring_targets(groups):
    ring = [0] + list(range(1, groups, 2)) + list(range(2, groups, 2))[::-1]
    return [[ring[(ring.index(place) + step) % groups] for place in range(groups)] for step in range(groups)]


def body(sequence, groups, queries, key_rows, value_rows, out_grad, norm_gains, clip_units):
    arrays = (queries, key_rows, value_rows, out_grad)
    heads = norm_gains.shape[1]
    chunks = head_chunks(heads)
    far = list(range(2, sequence)) or [1]
    near = [flip for flip in range(1, sequence) if flip not in far]

    def send(block, flip):
        return lax.ppermute(block, "seq", [(s, s ^ flip) for s in range(sequence)])

    slots = clip_units.shape[1]
    peers = ring_targets(groups)
    close = near + [0]

    def pack_and_send(plan, after):
        *blocks, token = pack(arrays, plan, heads, after)
        flips = [flip for flip, _, wanted in plan for _ in wanted]
        return [send(block, flip) if flip else block for flip, block in zip(flips, blocks)], token

    def far_plan(number):
        return [(flip, OTHERS, chunks[number : number + 1]) for flip in far]

    *tiles, token = cut(arrays[VALUES], far, heads)
    tiles = [send(block, flip) for flip, block in zip(far, tiles)]
    received, token = pack_and_send(far_plan(0), [token])
    later = far_plan(1) if len(chunks) > 1 else []
    whole = [(flip, pair, chunks) for flip in close for pair in ((0, 1), (2, 3))]
    blocks, _ = pack_and_send(later + whole, [token, seen(tiles)])
    values = arrange(tiles, heads)
    prepared = [
        prepare(low, norm_gains, blocks[len(later) + number :: len(chunks)], slots, [] if number else [seen(received)])
        for number, (low, _) in enumerate(chunks)
    ]
    waiting, sums = blocks[: len(later)], []
    for number, (low, high) in enumerate(chunks[:-1]):
        sums.append(attend(low, high - low, clip_units, norm_gains, values, prepared[number], received))
        received = waiting
        if number + 2 < len(chunks):
            waiting, _ = pack_and_send(far_plan(number + 2), sums[-1:])
    low, high = chunks[-1]
    parts = attend(
        low, high - low, clip_units, norm_gains, values, prepared[-1], received, sums, peers
    )
    result = parts[0]
    for part, targets in zip(parts[1:], peers[1:]):
        result = result + lax.ppermute(part, "dp", list(enumerate(targets)))
    return result


def solution(mesh):
    return jax.shard_map(
        functools.partial(body, mesh.shape["seq"], mesh.shape["dp"]),
        mesh=mesh,
        in_specs=(
            P(("parts", "dp"), None, "seq", None, None),
            P(("parts", "dp"), None, "seq", None, None),
            P(("parts", "dp"), None, "seq", None, None),
            P(("parts", "dp"), None, "seq", None, None),
            P(None, "seq", None),
            P("parts", None),
        ),
        out_specs=P("parts", "seq", "dp"),
        check_vma=False,
    )
```

```python
import functools
import math

import jax
import jax.numpy as jnp
from jax import lax
from jax.experimental import pallas as pl
from jax.experimental.pallas import tpu as pltpu
from jax.sharding import PartitionSpec as P

MAXCLIP = 3
VALUES = 2
OTHERS = (0, 1, 3)
TILE = 8
EPS = 1e-06
VMEM_LIMIT = 48 * 1024 * 1024
PACK_VMEM_LIMIT = 53 * 1024 * 1024


def head_chunks(heads):
    sizes = {8: (4, 3, 1)}.get(heads)
    if sizes is None:
        sizes = (1,) * heads if heads <= 2 else (heads - heads // 2, heads // 2)
    bounds, start = [], 0
    for size in sizes:
        bounds.append((start, start + size))
        start += size
    return bounds


def tile_start(heads, flip):
    head = jnp.bitwise_xor(lax.axis_index("seq"), flip) * heads
    offset = 0 if heads % TILE == 0 else lax.rem(head, TILE)
    return pl.multiple_of((head // TILE) * TILE, TILE), offset


def cut_kernel(flips, heads, array, *refs):
    outs, token, sems = refs[:-2], refs[-2], refs[-1]
    token[...] = jnp.zeros_like(token)
    copies = []
    for index, flip in enumerate(flips):
        start, _ = tile_start(heads, flip)
        source = array.at[0, :, :, pl.ds(start, outs[index].shape[2]), :]
        copies.append(pltpu.make_async_copy(source, outs[index], sems.at[index]))
        copies[-1].start()
    for copy in copies:
        copy.wait()


def cut(array, flips, heads):
    _, slots, rows, _, size = array.shape
    shape = jax.ShapeDtypeStruct((slots, rows, max(heads, TILE), size), array.dtype)
    return pl.pallas_call(
        functools.partial(cut_kernel, flips, heads),
        out_shape=[shape] * len(flips) + [jax.ShapeDtypeStruct((TILE, size), jnp.float32)],
        in_specs=[pl.BlockSpec(memory_space=pltpu.HBM)],
        out_specs=[pl.BlockSpec(memory_space=pltpu.VMEM)] * (len(flips) + 1),
        scratch_shapes=[pltpu.SemaphoreType.DMA((len(flips),))],
        compiler_params=pltpu.CompilerParams(vmem_limit_bytes=PACK_VMEM_LIMIT),
        name="cut",
    )(array)


def arrange_kernel(*refs):
    pieces, out, wide = refs[:-2], refs[-2], refs[-1]
    heads, slots = out.shape[:2]
    rows, held = pieces[0].shape[1:3]
    _, offset = tile_start(heads, 0)
    for source, piece in enumerate(pieces):
        for slot in range(slots):
            for span in range(held // TILE):
                place = (source * slots + slot) % wide.shape[0]
                block = piece[slot, :, span * TILE : (span + 1) * TILE, :]
                wide[place] = block.astype(jnp.float32).reshape(rows * TILE, wide.shape[-1])
                for head in range(span * TILE, min(heads, (span + 1) * TILE)):
                    out[head, slot, source * rows : (source + 1) * rows, :] = wide[
                        place, pl.ds(offset + head - span * TILE, rows, stride=TILE), :
                    ].astype(jnp.bfloat16)


def arrange(pieces, heads):
    slots, rows, held, size = pieces[0].shape
    moved = len(pieces) * slots * rows * held * size * 2
    return pl.pallas_call(
        arrange_kernel,
        out_shape=jax.ShapeDtypeStruct((heads, slots, len(pieces) * rows, size), jnp.bfloat16),
        in_specs=[pl.BlockSpec(memory_space=pltpu.VMEM)] * len(pieces),
        out_specs=pl.BlockSpec(memory_space=pltpu.VMEM),
        scratch_shapes=[pltpu.VMEM((slots, rows * TILE, size), jnp.float32)],
        compiler_params=pltpu.CompilerParams(vmem_limit_bytes=VMEM_LIMIT),
        cost_estimate=pl.CostEstimate(flops=moved, bytes_accessed=2 * moved, transcendentals=0),
        name="arrange",
    )(*pieces)


def pack_kernel(plan, heads, after, *refs):
    arrays = refs[:4]
    outs = refs[4 + after : 4 + after + sum(len(chunks) for _, _, chunks in plan)]
    token, raw, wide, sems = refs[4 + after + len(outs) :]
    token[...] = jnp.zeros_like(token)
    slots, rows = raw.shape[2], raw.shape[3]
    spans = max(1, heads // TILE)

    def copy(index, array, span, first):
        return pltpu.make_async_copy(
            arrays[array].at[0, :, :, pl.ds(first + span * TILE, TILE), :],
            raw.at[index, array * spans + span],
            sems.at[index, array * spans + span],
        )

    firsts, offsets = zip(*[tile_start(heads, flip) for flip, _, _ in plan])
    for index, (_, wanted, _) in enumerate(plan):
        for array in wanted:
            for span in range(spans):
                copy(index, array, span, firsts[index]).start()
    place = 0
    for index, (_, wanted, chunks) in enumerate(plan):
        for position, array in enumerate(wanted):
            for span in range(spans):
                copy(index, array, span, firsts[index]).wait()
                for slot in range(slots):
                    wide[slot] = (
                        raw[index, array * spans + span, slot]
                        .astype(jnp.float32)
                        .reshape(rows * TILE, wide.shape[-1])
                    )
                    for number, (low, high) in enumerate(chunks):
                        for head in range(max(low, span * TILE), min(high, (span + 1) * TILE)):
                            outs[place + number][head - low, position, slot * rows : (slot + 1) * rows, :] = wide[
                                slot, pl.ds(offsets[index] + head - span * TILE, rows, stride=TILE), :
                            ].astype(jnp.bfloat16)
        place += len(chunks)


def pack(arrays, plan, heads, after=()):
    _, slots, rows, _, size = arrays[0].shape
    spans = max(1, heads // TILE)
    shapes = [
        jax.ShapeDtypeStruct((high - low, len(wanted), slots * rows, size), jnp.bfloat16)
        for _, wanted, chunks in plan
        for low, high in chunks
    ] + [jax.ShapeDtypeStruct((TILE, size), jnp.float32)]
    count = len(plan)
    moved = count * 4 * spans * slots * rows * TILE * size * 2
    return pl.pallas_call(
        functools.partial(pack_kernel, plan, heads, len(after)),
        out_shape=shapes,
        in_specs=[pl.BlockSpec(memory_space=pltpu.HBM)] * 4 + [pl.BlockSpec(memory_space=pl.ANY)] * len(after),
        out_specs=[pl.BlockSpec(memory_space=pltpu.VMEM)] * len(shapes),
        scratch_shapes=[
            pltpu.VMEM((count, 4 * spans, slots, rows, TILE, size), jnp.bfloat16),
            pltpu.VMEM((slots, rows * TILE, size), jnp.float32),
            pltpu.SemaphoreType.DMA((count, 4 * spans)),
        ],
        compiler_params=pltpu.CompilerParams(vmem_limit_bytes=PACK_VMEM_LIMIT),
        cost_estimate=pl.CostEstimate(flops=moved, bytes_accessed=2 * moved, transcendentals=0),
        name="pack",
    )(*arrays, *after)


def contract_last(left, right):
    return lax.dot_general(left, right, (((1,), (1,)), ((), ())), preferred_element_type=jnp.float32)


def layouts(slots):
    found = []

    def extend(start, clips):
        if start == slots:
            found.append(tuple(clips))
        for span in range(1, min(MAXCLIP, slots - start) + 1):
            extend(start + span, clips + [(start, span)])

    extend(0, [])
    return found


def normalized(block, gain):
    wide = block.astype(jnp.float32)
    wide = wide * lax.rsqrt(jnp.mean(wide * wide, axis=-1, keepdims=True) + EPS)
    return (wide * gain).astype(jnp.bfloat16)


def prepare_kernel(low, after, gains, *refs):
    pieces, out = refs[after:-1], refs[-1]
    heads, _, tokens, _ = pieces[0].shape
    slots = out.shape[2]
    rows = tokens // slots
    for head in range(heads):
        for array in range(4):
            for source, piece in enumerate(pieces[array // 2 :: 2]):
                block = piece[head, array % 2]
                if array < 2:
                    block = normalized(block, gains[array, low + head : low + head + 1, :])
                for slot in range(slots):
                    out[head, array, slot, source * rows : (source + 1) * rows, :] = block[
                        slot * rows : (slot + 1) * rows
                    ]


def prepare(low, gains, pieces, slots, after):
    heads, _, tokens, size = pieces[0].shape
    moved = len(pieces) * heads * 2 * tokens * size * 2
    return pl.pallas_call(
        functools.partial(prepare_kernel, low, len(after)),
        out_shape=jax.ShapeDtypeStruct((heads, 4, slots, len(pieces) // 2 * tokens // slots, size), jnp.bfloat16),
        in_specs=[pl.BlockSpec(memory_space=pltpu.VMEM)] * (1 + len(after) + len(pieces)),
        out_specs=pl.BlockSpec(memory_space=pltpu.VMEM),
        compiler_params=pltpu.CompilerParams(vmem_limit_bytes=VMEM_LIMIT),
        cost_estimate=pl.CostEstimate(flops=1, bytes_accessed=1, transcendentals=0),
        name="prepare",
    )(gains, *after, *pieces)


def attention_chunk(low, count, units, gains, values, close, pieces, held, total):
    query, key, value, grad = held
    group = lax.axis_index("dp")
    _, _, tokens, size = pieces[0].shape
    slots, near = close.shape[2:4]
    rows = tokens // slots
    unit = near + rows * len(pieces)
    for head in range(count):
        for array, kept in enumerate(held):
            for slot in range(slots):
                kept[head, slot * unit : slot * unit + near, :] = close[head, array, slot]
                if array == VALUES:
                    kept[head, slot * unit + near : (slot + 1) * unit, :] = values[low + head, slot]
            if array == VALUES:
                continue
            for source, piece in enumerate(pieces):
                block = piece[head, OTHERS.index(array)]
                if array < 2:
                    block = normalized(block, gains[array, low + head : low + head + 1, :])
                for slot in range(slots):
                    start = slot * unit + near + source * rows
                    kept[head, start : start + rows, :] = block[slot * rows : (slot + 1) * rows]
    factor = size ** (-0.5) * math.log2(math.e)

    def attention(head, layout):
        blocks = [
            (slice(slot * unit, (slot + span) * unit), slice(place * unit, (place + 1) * unit))
            for slot, span in layout
            for place in range(slot, slot + span)
        ]
        scores = [contract_last(key[head, keys, :], query[head, own, :]) for keys, own in blocks]
        dprobs = [contract_last(value[head, keys, :], grad[head, own, :]) for keys, own in blocks]
        expos = [jnp.exp2(score * factor) for score in scores]
        shares = [1.0 / jnp.sum(expo, axis=0, keepdims=True) for expo in expos]
        probs = [expo * share for expo, share in zip(expos, shares)]
        deltas = [jnp.sum(prob * dprob, axis=0, keepdims=True) for prob, dprob in zip(probs, dprobs)]
        dscores = [
            (prob * (dprob - delta)).astype(jnp.bfloat16) for prob, dprob, delta in zip(probs, dprobs, deltas)
        ]
        mixed = [
            jnp.dot(dscore, query[head, own, :], preferred_element_type=jnp.float32)
            for dscore, (_, own) in zip(dscores, blocks)
        ]
        return sum(
            jnp.sum(part * key[head, keys, :].astype(jnp.float32), axis=0, keepdims=True)
            for part, (keys, _) in zip(mixed, blocks)
        )

    table = units[...]
    rows_of, slots_of = (lax.broadcasted_iota(jnp.int32, table.shape, dim) for dim in (0, 1))
    starts = jnp.where((rows_of == group) & (table > 0), lax.shift_left(jnp.int32(1), slots_of), 0)
    begins = jnp.sum(starts)
    for layout in layouts(slots):

        @pl.when(begins == sum(1 << slot for slot, _ in layout))
        def _():
            for head in range(count):
                total[head : head + 1, :] = attention(head, layout)


def chunk_kernel(low, units, gains, values, close, *refs):
    pieces, out, held = refs[:-5], refs[-5], refs[-4:]
    attention_chunk(low, out.shape[0], units, gains, values, close, pieces, held, out)


def last_kernel(low, sources, earlier, peers, units, gains, values, close, *refs):
    pieces = refs[:sources]
    before = refs[sources : sources + earlier]
    outs = refs[sources + earlier : sources + earlier + len(peers)]
    held, total = refs[sources + earlier + len(peers) : -1], refs[-1]
    attention_chunk(low, total.shape[0], units, gains, values, close, pieces, held, total)
    group = lax.axis_index("dp")
    size = total.shape[-1]
    width = outs[0].shape[-1]
    scaled = jnp.concatenate([ref[...] for ref in before] + [total[...]], axis=0) * (size ** (-0.5))
    for side in range(2):
        grads = scaled / gains[side]
        for out, targets in zip(outs, peers):
            target = sum(jnp.where(group == place, whom, 0) for place, whom in enumerate(targets))
            shift = lax.rem(size - target * width, size)
            out[side] = pltpu.roll(grads, shift, 1)[:, :width]


def attend(low, count, units, gains, values, close, pieces, earlier=None, peers=None):
    _, _, tokens, size = pieces[0].shape
    all_tokens = close.shape[2] * close.shape[3] + tokens * len(pieces)
    held = [pltpu.VMEM((count, all_tokens, size), jnp.bfloat16)] * 4
    if earlier is None:
        kernel = functools.partial(chunk_kernel, low)
        shapes = jax.ShapeDtypeStruct((count, size), jnp.float32)
        earlier = []
        outs = pl.BlockSpec(memory_space=pltpu.VMEM)
    else:
        kernel = functools.partial(last_kernel, low, len(pieces), len(earlier), peers)
        heads = gains.shape[1]
        shapes = [jax.ShapeDtypeStruct((2, heads, size // len(peers)), jnp.float32)] * len(peers)
        held.append(pltpu.VMEM((count, size), jnp.float32))
        outs = [pl.BlockSpec(memory_space=pltpu.VMEM)] * len(peers)
    pairs = count * all_tokens * all_tokens // 2
    return pl.pallas_call(
        kernel,
        out_shape=shapes,
        in_specs=[pl.BlockSpec(memory_space=pltpu.VMEM)] * (4 + len(pieces) + len(earlier)),
        out_specs=outs,
        scratch_shapes=held,
        compiler_params=pltpu.CompilerParams(vmem_limit_bytes=VMEM_LIMIT),
        cost_estimate=pl.CostEstimate(
            flops=6 * pairs * size, bytes_accessed=len(pieces) * count * 4 * tokens * size * 2, transcendentals=pairs
        ),
        name="attend",
    )(units, gains, values, close, *pieces, *earlier)


def seen_kernel(*refs):
    refs[-1][...] = jnp.zeros_like(refs[-1])


def seen(blocks):
    return pl.pallas_call(
        seen_kernel,
        out_shape=jax.ShapeDtypeStruct((TILE, blocks[0].shape[-1]), jnp.float32),
        in_specs=[pl.BlockSpec(memory_space=pl.ANY)] * len(blocks),
        out_specs=pl.BlockSpec(memory_space=pltpu.VMEM),
        compiler_params=pltpu.CompilerParams(vmem_limit_bytes=1024 * 1024),
        cost_estimate=pl.CostEstimate(flops=1, bytes_accessed=1024 * 1024, transcendentals=0),
        name="seen",
    )(*blocks)


def ring_targets(groups):
    ring = [0] + list(range(1, groups, 2)) + list(range(2, groups, 2))[::-1]
    return [[ring[(ring.index(place) + step) % groups] for place in range(groups)] for step in range(groups)]


def body(sequence, groups, queries, key_rows, value_rows, out_grad, norm_gains, clip_units):
    arrays = (queries, key_rows, value_rows, out_grad)
    heads = norm_gains.shape[1]
    chunks = head_chunks(heads)
    far = list(range(2, sequence))[::-1] or [1]
    near = [flip for flip in range(1, sequence) if flip not in far]

    def send(block, flip):
        return lax.ppermute(block, "seq", [(s, s ^ flip) for s in range(sequence)])

    slots = clip_units.shape[1]
    peers = ring_targets(groups)
    close = near + [0]

    def pack_and_send(plan, after):
        *blocks, token = pack(arrays, plan, heads, after)
        flips = [flip for flip, _, wanted in plan for _ in wanted]
        return [send(block, flip) if flip else block for flip, block in zip(flips, blocks)], token

    def far_plan(number):
        return [(flip, OTHERS, chunks[number : number + 1]) for flip in far]

    *tiles, token = cut(arrays[VALUES], far, heads)
    tiles = [send(block, flip) for flip, block in zip(far, tiles)]
    received, token = pack_and_send(far_plan(0), [token])
    later = far_plan(1) if len(chunks) > 1 else []
    whole = [(flip, pair, chunks) for flip in close for pair in ((0, 1), (2, 3))]
    blocks, _ = pack_and_send(later + whole, [token, seen(tiles)])
    values = arrange(tiles, heads)
    prepared = [
        prepare(low, norm_gains, blocks[len(later) + number :: len(chunks)], slots, [] if number else [seen(received)])
        for number, (low, _) in enumerate(chunks)
    ]
    waiting, sums = blocks[: len(later)], []
    for number, (low, high) in enumerate(chunks[:-1]):
        sums.append(attend(low, high - low, clip_units, norm_gains, values, prepared[number], received))
        received = waiting
        if number + 2 < len(chunks):
            waiting, _ = pack_and_send(far_plan(number + 2), sums[-1:])
    low, high = chunks[-1]
    parts = attend(
        low, high - low, clip_units, norm_gains, values, prepared[-1], received, sums, peers
    )
    result = parts[0]
    for part, targets in zip(parts[1:], peers[1:]):
        result = result + lax.ppermute(part, "dp", list(enumerate(targets)))
    return result


def solution(mesh):
    return jax.shard_map(
        functools.partial(body, mesh.shape["seq"], mesh.shape["dp"]),
        mesh=mesh,
        in_specs=(
            P(("parts", "dp"), None, "seq", None, None),
            P(("parts", "dp"), None, "seq", None, None),
            P(("parts", "dp"), None, "seq", None, None),
            P(("parts", "dp"), None, "seq", None, None),
            P(None, "seq", None),
            P("parts", None),
        ),
        out_specs=P("parts", "seq", "dp"),
        check_vma=False,
    )
```

```python
import functools
import math

import jax
import jax.numpy as jnp
from jax import lax
from jax.experimental import pallas as pl
from jax.experimental.pallas import tpu as pltpu
from jax.sharding import PartitionSpec as P

MAXCLIP = 3
VALUES = 2
OTHERS = (0, 1, 3)
TILE = 8
EPS = 1e-06
VMEM_LIMIT = 48 * 1024 * 1024
PACK_VMEM_LIMIT = 53 * 1024 * 1024


def head_chunks(heads):
    sizes = {8: (4, 3, 1)}.get(heads)
    if sizes is None:
        sizes = (1,) * heads if heads <= 2 else (heads - heads // 2, heads // 2)
    bounds, start = [], 0
    for size in sizes:
        bounds.append((start, start + size))
        start += size
    return bounds


def tile_start(heads, flip):
    head = jnp.bitwise_xor(lax.axis_index("seq"), flip) * heads
    offset = 0 if heads % TILE == 0 else lax.rem(head, TILE)
    return pl.multiple_of((head // TILE) * TILE, TILE), offset


def cut_kernel(flips, heads, array, *refs):
    outs, token, sems = refs[:-2], refs[-2], refs[-1]
    token[...] = jnp.zeros_like(token)
    copies = []
    for index, flip in enumerate(flips):
        start, _ = tile_start(heads, flip)
        source = array.at[0, :, :, pl.ds(start, outs[index].shape[2]), :]
        copies.append(pltpu.make_async_copy(source, outs[index], sems.at[index]))
        copies[-1].start()
    for copy in copies:
        copy.wait()


def cut(array, flips, heads):
    _, slots, rows, _, size = array.shape
    shape = jax.ShapeDtypeStruct((slots, rows, max(heads, TILE), size), array.dtype)
    return pl.pallas_call(
        functools.partial(cut_kernel, flips, heads),
        out_shape=[shape] * len(flips) + [jax.ShapeDtypeStruct((TILE, size), jnp.float32)],
        in_specs=[pl.BlockSpec(memory_space=pltpu.HBM)],
        out_specs=[pl.BlockSpec(memory_space=pltpu.VMEM)] * (len(flips) + 1),
        scratch_shapes=[pltpu.SemaphoreType.DMA((len(flips),))],
        compiler_params=pltpu.CompilerParams(vmem_limit_bytes=PACK_VMEM_LIMIT),
        name="cut",
    )(array)


def arrange_kernel(*refs):
    pieces, out, wide = refs[:-2], refs[-2], refs[-1]
    heads, slots = out.shape[:2]
    rows, held = pieces[0].shape[1:3]
    _, offset = tile_start(heads, 0)
    for source, piece in enumerate(pieces[::-1]):
        for slot in range(slots):
            for span in range(held // TILE):
                place = (source * slots + slot) % wide.shape[0]
                block = piece[slot, :, span * TILE : (span + 1) * TILE, :]
                wide[place] = block.astype(jnp.float32).reshape(rows * TILE, wide.shape[-1])
                for head in range(span * TILE, min(heads, (span + 1) * TILE)):
                    out[head, slot, source * rows : (source + 1) * rows, :] = wide[
                        place, pl.ds(offset + head - span * TILE, rows, stride=TILE), :
                    ].astype(jnp.bfloat16)


def arrange(pieces, heads):
    slots, rows, held, size = pieces[0].shape
    moved = len(pieces) * slots * rows * held * size * 2
    return pl.pallas_call(
        arrange_kernel,
        out_shape=jax.ShapeDtypeStruct((heads, slots, len(pieces) * rows, size), jnp.bfloat16),
        in_specs=[pl.BlockSpec(memory_space=pltpu.VMEM)] * len(pieces),
        out_specs=pl.BlockSpec(memory_space=pltpu.VMEM),
        scratch_shapes=[pltpu.VMEM((slots, rows * TILE, size), jnp.float32)],
        compiler_params=pltpu.CompilerParams(vmem_limit_bytes=VMEM_LIMIT),
        cost_estimate=pl.CostEstimate(flops=moved, bytes_accessed=2 * moved, transcendentals=0),
        name="arrange",
    )(*pieces)


def pack_kernel(plan, heads, after, *refs):
    arrays = refs[:4]
    outs = refs[4 + after : 4 + after + sum(len(chunks) for _, _, chunks in plan)]
    token, raw, wide, sems = refs[4 + after + len(outs) :]
    token[...] = jnp.zeros_like(token)
    slots, rows = raw.shape[2], raw.shape[3]
    spans = max(1, heads // TILE)

    def copy(index, array, span, first):
        return pltpu.make_async_copy(
            arrays[array].at[0, :, :, pl.ds(first + span * TILE, TILE), :],
            raw.at[index, array * spans + span],
            sems.at[index, array * spans + span],
        )

    firsts, offsets = zip(*[tile_start(heads, flip) for flip, _, _ in plan])
    for index, (_, wanted, _) in enumerate(plan):
        for array in wanted:
            for span in range(spans):
                copy(index, array, span, firsts[index]).start()
    place = 0
    for index, (_, wanted, chunks) in enumerate(plan):
        for position, array in enumerate(wanted):
            for span in range(spans):
                copy(index, array, span, firsts[index]).wait()
                for slot in range(slots):
                    wide[slot] = (
                        raw[index, array * spans + span, slot]
                        .astype(jnp.float32)
                        .reshape(rows * TILE, wide.shape[-1])
                    )
                    for number, (low, high) in enumerate(chunks):
                        for head in range(max(low, span * TILE), min(high, (span + 1) * TILE)):
                            outs[place + number][head - low, position, slot * rows : (slot + 1) * rows, :] = wide[
                                slot, pl.ds(offsets[index] + head - span * TILE, rows, stride=TILE), :
                            ].astype(jnp.bfloat16)
        place += len(chunks)


def pack(arrays, plan, heads, after=()):
    _, slots, rows, _, size = arrays[0].shape
    spans = max(1, heads // TILE)
    shapes = [
        jax.ShapeDtypeStruct((high - low, len(wanted), slots * rows, size), jnp.bfloat16)
        for _, wanted, chunks in plan
        for low, high in chunks
    ] + [jax.ShapeDtypeStruct((TILE, size), jnp.float32)]
    count = len(plan)
    moved = count * 4 * spans * slots * rows * TILE * size * 2
    return pl.pallas_call(
        functools.partial(pack_kernel, plan, heads, len(after)),
        out_shape=shapes,
        in_specs=[pl.BlockSpec(memory_space=pltpu.HBM)] * 4 + [pl.BlockSpec(memory_space=pl.ANY)] * len(after),
        out_specs=[pl.BlockSpec(memory_space=pltpu.VMEM)] * len(shapes),
        scratch_shapes=[
            pltpu.VMEM((count, 4 * spans, slots, rows, TILE, size), jnp.bfloat16),
            pltpu.VMEM((slots, rows * TILE, size), jnp.float32),
            pltpu.SemaphoreType.DMA((count, 4 * spans)),
        ],
        compiler_params=pltpu.CompilerParams(vmem_limit_bytes=PACK_VMEM_LIMIT),
        cost_estimate=pl.CostEstimate(flops=moved, bytes_accessed=2 * moved, transcendentals=0),
        name="pack",
    )(*arrays, *after)


def contract_last(left, right):
    return lax.dot_general(left, right, (((1,), (1,)), ((), ())), preferred_element_type=jnp.float32)


def layouts(slots):
    found = []

    def extend(start, clips):
        if start == slots:
            found.append(tuple(clips))
        for span in range(1, min(MAXCLIP, slots - start) + 1):
            extend(start + span, clips + [(start, span)])

    extend(0, [])
    return found


def normalized(block, gain):
    wide = block.astype(jnp.float32)
    wide = wide * lax.rsqrt(jnp.mean(wide * wide, axis=-1, keepdims=True) + EPS)
    return (wide * gain).astype(jnp.bfloat16)


def prepare_kernel(low, after, gains, *refs):
    pieces, out = refs[after:-1], refs[-1]
    heads, _, tokens, _ = pieces[0].shape
    slots = out.shape[2]
    rows = tokens // slots
    for head in range(heads):
        for array in range(4):
            for source, piece in enumerate(pieces[array // 2 :: 2]):
                block = piece[head, array % 2]
                if array < 2:
                    block = normalized(block, gains[array, low + head : low + head + 1, :])
                for slot in range(slots):
                    out[head, array, slot, source * rows : (source + 1) * rows, :] = block[
                        slot * rows : (slot + 1) * rows
                    ]


def prepare(low, gains, pieces, slots, after):
    heads, _, tokens, size = pieces[0].shape
    moved = len(pieces) * heads * 2 * tokens * size * 2
    return pl.pallas_call(
        functools.partial(prepare_kernel, low, len(after)),
        out_shape=jax.ShapeDtypeStruct((heads, 4, slots, len(pieces) // 2 * tokens // slots, size), jnp.bfloat16),
        in_specs=[pl.BlockSpec(memory_space=pltpu.VMEM)] * (1 + len(after) + len(pieces)),
        out_specs=pl.BlockSpec(memory_space=pltpu.VMEM),
        compiler_params=pltpu.CompilerParams(vmem_limit_bytes=VMEM_LIMIT),
        cost_estimate=pl.CostEstimate(flops=1, bytes_accessed=1, transcendentals=0),
        name="prepare",
    )(gains, *after, *pieces)


def attention_chunk(low, count, units, gains, values, close, pieces, held, total):
    query, key, value, grad = held
    group = lax.axis_index("dp")
    _, _, tokens, size = pieces[0].shape
    slots, near = close.shape[2:4]
    rows = tokens // slots
    unit = near + rows * len(pieces)
    for head in range(count):
        for array, kept in enumerate(held):
            for slot in range(slots):
                kept[head, slot * unit : slot * unit + near, :] = close[head, array, slot]
                if array == VALUES:
                    kept[head, slot * unit + near : (slot + 1) * unit, :] = values[low + head, slot]
            if array == VALUES:
                continue
            for source, piece in enumerate(pieces):
                block = piece[head, OTHERS.index(array)]
                if array < 2:
                    block = normalized(block, gains[array, low + head : low + head + 1, :])
                for slot in range(slots):
                    start = slot * unit + near + source * rows
                    kept[head, start : start + rows, :] = block[slot * rows : (slot + 1) * rows]
    factor = size ** (-0.5) * math.log2(math.e)

    def attention(head, layout):
        blocks = [
            (slice(slot * unit, (slot + span) * unit), slice(place * unit, (place + 1) * unit))
            for slot, span in layout
            for place in range(slot, slot + span)
        ]
        scores = [contract_last(key[head, keys, :], query[head, own, :]) for keys, own in blocks]
        dprobs = [contract_last(value[head, keys, :], grad[head, own, :]) for keys, own in blocks]
        expos = [jnp.exp2(score * factor) for score in scores]
        shares = [1.0 / jnp.sum(expo, axis=0, keepdims=True) for expo in expos]
        probs = [expo * share for expo, share in zip(expos, shares)]
        deltas = [jnp.sum(prob * dprob, axis=0, keepdims=True) for prob, dprob in zip(probs, dprobs)]
        dscores = [
            (prob * (dprob - delta)).astype(jnp.bfloat16) for prob, dprob, delta in zip(probs, dprobs, deltas)
        ]
        mixed = [
            jnp.dot(dscore, query[head, own, :], preferred_element_type=jnp.float32)
            for dscore, (_, own) in zip(dscores, blocks)
        ]
        return sum(
            jnp.sum(part * key[head, keys, :].astype(jnp.float32), axis=0, keepdims=True)
            for part, (keys, _) in zip(mixed, blocks)
        )

    table = units[...]
    rows_of, slots_of = (lax.broadcasted_iota(jnp.int32, table.shape, dim) for dim in (0, 1))
    starts = jnp.where((rows_of == group) & (table > 0), lax.shift_left(jnp.int32(1), slots_of), 0)
    begins = jnp.sum(starts)
    for layout in layouts(slots):

        @pl.when(begins == sum(1 << slot for slot, _ in layout))
        def _():
            for head in range(count):
                total[head : head + 1, :] = attention(head, layout)


def chunk_kernel(low, units, gains, values, close, *refs):
    pieces, out, held = refs[:-5], refs[-5], refs[-4:]
    attention_chunk(low, out.shape[0], units, gains, values, close, pieces, held, out)


def last_kernel(low, sources, earlier, peers, units, gains, values, close, *refs):
    pieces = refs[:sources]
    before = refs[sources : sources + earlier]
    outs = refs[sources + earlier : sources + earlier + len(peers)]
    held, total = refs[sources + earlier + len(peers) : -1], refs[-1]
    attention_chunk(low, total.shape[0], units, gains, values, close, pieces, held, total)
    group = lax.axis_index("dp")
    size = total.shape[-1]
    width = outs[0].shape[-1]
    scaled = jnp.concatenate([ref[...] for ref in before] + [total[...]], axis=0) * (size ** (-0.5))
    for side in range(2):
        grads = scaled / gains[side]
        for out, targets in zip(outs, peers):
            target = sum(jnp.where(group == place, whom, 0) for place, whom in enumerate(targets))
            shift = lax.rem(size - target * width, size)
            out[side] = pltpu.roll(grads, shift, 1)[:, :width]


def attend(low, count, units, gains, values, close, pieces, earlier=None, peers=None):
    _, _, tokens, size = pieces[0].shape
    all_tokens = close.shape[2] * close.shape[3] + tokens * len(pieces)
    held = [pltpu.VMEM((count, all_tokens, size), jnp.bfloat16)] * 4
    if earlier is None:
        kernel = functools.partial(chunk_kernel, low)
        shapes = jax.ShapeDtypeStruct((count, size), jnp.float32)
        earlier = []
        outs = pl.BlockSpec(memory_space=pltpu.VMEM)
    else:
        kernel = functools.partial(last_kernel, low, len(pieces), len(earlier), peers)
        heads = gains.shape[1]
        shapes = [jax.ShapeDtypeStruct((2, heads, size // len(peers)), jnp.float32)] * len(peers)
        held.append(pltpu.VMEM((count, size), jnp.float32))
        outs = [pl.BlockSpec(memory_space=pltpu.VMEM)] * len(peers)
    pairs = count * all_tokens * all_tokens // 2
    return pl.pallas_call(
        kernel,
        out_shape=shapes,
        in_specs=[pl.BlockSpec(memory_space=pltpu.VMEM)] * (4 + len(pieces) + len(earlier)),
        out_specs=outs,
        scratch_shapes=held,
        compiler_params=pltpu.CompilerParams(vmem_limit_bytes=VMEM_LIMIT),
        cost_estimate=pl.CostEstimate(
            flops=6 * pairs * size, bytes_accessed=len(pieces) * count * 4 * tokens * size * 2, transcendentals=pairs
        ),
        name="attend",
    )(units, gains, values, close, *pieces, *earlier)


def seen_kernel(*refs):
    refs[-1][...] = jnp.zeros_like(refs[-1])


def seen(blocks):
    return pl.pallas_call(
        seen_kernel,
        out_shape=jax.ShapeDtypeStruct((TILE, blocks[0].shape[-1]), jnp.float32),
        in_specs=[pl.BlockSpec(memory_space=pl.ANY)] * len(blocks),
        out_specs=pl.BlockSpec(memory_space=pltpu.VMEM),
        compiler_params=pltpu.CompilerParams(vmem_limit_bytes=1024 * 1024),
        cost_estimate=pl.CostEstimate(flops=1, bytes_accessed=1024 * 1024, transcendentals=0),
        name="seen",
    )(*blocks)


def ring_targets(groups):
    ring = [0] + list(range(1, groups, 2)) + list(range(2, groups, 2))[::-1]
    return [[ring[(ring.index(place) + step) % groups] for place in range(groups)] for step in range(groups)]


def body(sequence, groups, queries, key_rows, value_rows, out_grad, norm_gains, clip_units):
    arrays = (queries, key_rows, value_rows, out_grad)
    heads = norm_gains.shape[1]
    chunks = head_chunks(heads)
    far = list(range(2, sequence)) or [1]
    near = [flip for flip in range(1, sequence) if flip not in far]

    def send(block, flip):
        return lax.ppermute(block, "seq", [(s, s ^ flip) for s in range(sequence)])

    slots = clip_units.shape[1]
    peers = ring_targets(groups)
    close = near + [0]

    def pack_and_send(plan, after):
        *blocks, token = pack(arrays, plan, heads, after)
        flips = [flip for flip, _, wanted in plan for _ in wanted]
        return [send(block, flip) if flip else block for flip, block in zip(flips, blocks)], token

    def far_plan(number):
        return [(flip, OTHERS, chunks[number : number + 1]) for flip in far]

    *tiles, token = cut(arrays[VALUES], far[::-1], heads)
    tiles = [send(block, flip) for flip, block in zip(far[::-1], tiles)]
    received, token = pack_and_send(far_plan(0), [token])
    later = far_plan(1) if len(chunks) > 1 else []
    whole = [(flip, pair, chunks) for flip in close for pair in ((0, 1), (2, 3))]
    blocks, _ = pack_and_send(later + whole, [token, seen(tiles)])
    values = arrange(tiles, heads)
    prepared = [
        prepare(low, norm_gains, blocks[len(later) + number :: len(chunks)], slots, [] if number else [seen(received)])
        for number, (low, _) in enumerate(chunks)
    ]
    waiting, sums = blocks[: len(later)], []
    for number, (low, high) in enumerate(chunks[:-1]):
        sums.append(attend(low, high - low, clip_units, norm_gains, values, prepared[number], received))
        received = waiting
        if number + 2 < len(chunks):
            waiting, _ = pack_and_send(far_plan(number + 2), sums[-1:])
    low, high = chunks[-1]
    parts = attend(
        low, high - low, clip_units, norm_gains, values, prepared[-1], received, sums, peers
    )
    result = parts[0]
    for part, targets in zip(parts[1:], peers[1:]):
        result = result + lax.ppermute(part, "dp", list(enumerate(targets)))
    return result


def solution(mesh):
    return jax.shard_map(
        functools.partial(body, mesh.shape["seq"], mesh.shape["dp"]),
        mesh=mesh,
        in_specs=(
            P(("parts", "dp"), None, "seq", None, None),
            P(("parts", "dp"), None, "seq", None, None),
            P(("parts", "dp"), None, "seq", None, None),
            P(("parts", "dp"), None, "seq", None, None),
            P(None, "seq", None),
            P("parts", None),
        ),
        out_specs=P("parts", "seq", "dp"),
        check_vma=False,
    )
```

```python
import functools
import math

import jax
import jax.numpy as jnp
from jax import lax
from jax.experimental import pallas as pl
from jax.experimental.pallas import tpu as pltpu
from jax.sharding import PartitionSpec as P

MAXCLIP = 3
VALUES = 2
OTHERS = (0, 1, 3)
TILE = 8
EPS = 1e-06
VMEM_LIMIT = 48 * 1024 * 1024
PACK_VMEM_LIMIT = 53 * 1024 * 1024


def head_chunks(heads):
    sizes = {8: (4, 3, 1)}.get(heads)
    if sizes is None:
        sizes = (1,) * heads if heads <= 2 else (heads - heads // 2, heads // 2)
    bounds, start = [], 0
    for size in sizes:
        bounds.append((start, start + size))
        start += size
    return bounds


def tile_start(heads, flip):
    head = jnp.bitwise_xor(lax.axis_index("seq"), flip) * heads
    offset = 0 if heads % TILE == 0 else lax.rem(head, TILE)
    return pl.multiple_of((head // TILE) * TILE, TILE), offset


def cut_kernel(flips, heads, array, *refs):
    outs, token, sems = refs[:-2], refs[-2], refs[-1]
    token[...] = jnp.zeros_like(token)
    copies = []
    for index, flip in enumerate(flips):
        start, _ = tile_start(heads, flip)
        source = array.at[0, :, :, pl.ds(start, outs[index].shape[2]), :]
        copies.append(pltpu.make_async_copy(source, outs[index], sems.at[index]))
        copies[-1].start()
    for copy in copies:
        copy.wait()


def cut(array, flips, heads):
    _, slots, rows, _, size = array.shape
    shape = jax.ShapeDtypeStruct((slots, rows, max(heads, TILE), size), array.dtype)
    return pl.pallas_call(
        functools.partial(cut_kernel, flips, heads),
        out_shape=[shape] * len(flips) + [jax.ShapeDtypeStruct((TILE, size), jnp.float32)],
        in_specs=[pl.BlockSpec(memory_space=pltpu.HBM)],
        out_specs=[pl.BlockSpec(memory_space=pltpu.VMEM)] * (len(flips) + 1),
        scratch_shapes=[pltpu.SemaphoreType.DMA((len(flips),))],
        compiler_params=pltpu.CompilerParams(vmem_limit_bytes=PACK_VMEM_LIMIT),
        name="cut",
    )(array)


def arrange_kernel(*refs):
    pieces, out, wide = refs[:-2], refs[-2], refs[-1]
    heads, slots = out.shape[:2]
    rows, held = pieces[0].shape[1:3]
    _, offset = tile_start(heads, 0)
    for source, piece in enumerate(pieces):
        for slot in range(slots):
            for span in range(held // TILE):
                place = (source * slots + slot) % wide.shape[0]
                block = piece[slot, :, span * TILE : (span + 1) * TILE, :]
                wide[place] = block.astype(jnp.float32).reshape(rows * TILE, wide.shape[-1])
                for head in range(span * TILE, min(heads, (span + 1) * TILE)):
                    out[head, slot, source * rows : (source + 1) * rows, :] = wide[
                        place, pl.ds(offset + head - span * TILE, rows, stride=TILE), :
                    ].astype(jnp.bfloat16)


def arrange(pieces, heads):
    slots, rows, held, size = pieces[0].shape
    moved = len(pieces) * slots * rows * held * size * 2
    return pl.pallas_call(
        arrange_kernel,
        out_shape=jax.ShapeDtypeStruct((heads, slots, len(pieces) * rows, size), jnp.bfloat16),
        in_specs=[pl.BlockSpec(memory_space=pltpu.VMEM)] * len(pieces),
        out_specs=pl.BlockSpec(memory_space=pltpu.VMEM),
        scratch_shapes=[pltpu.VMEM((slots, rows * TILE, size), jnp.float32)],
        compiler_params=pltpu.CompilerParams(vmem_limit_bytes=VMEM_LIMIT),
        cost_estimate=pl.CostEstimate(flops=moved, bytes_accessed=2 * moved, transcendentals=0),
        name="arrange",
    )(*pieces)


def pack_kernel(plan, heads, after, *refs):
    arrays = refs[:4]
    outs = refs[4 + after : 4 + after + sum(len(chunks) for _, _, chunks in plan)]
    token, raw, wide, sems = refs[4 + after + len(outs) :]
    token[...] = jnp.zeros_like(token)
    slots, rows = raw.shape[2], raw.shape[3]
    spans = max(1, heads // TILE)

    def copy(index, array, span, first):
        return pltpu.make_async_copy(
            arrays[array].at[0, :, :, pl.ds(first + span * TILE, TILE), :],
            raw.at[index, array * spans + span],
            sems.at[index, array * spans + span],
        )

    firsts, offsets = zip(*[tile_start(heads, flip) for flip, _, _ in plan])
    for index, (_, wanted, _) in enumerate(plan):
        for array in wanted:
            for span in range(spans):
                copy(index, array, span, firsts[index]).start()
    place = 0
    for index, (_, wanted, chunks) in enumerate(plan):
        for position, array in enumerate(wanted):
            for span in range(spans):
                copy(index, array, span, firsts[index]).wait()
                for slot in range(slots):
                    wide[slot] = (
                        raw[index, array * spans + span, slot]
                        .astype(jnp.float32)
                        .reshape(rows * TILE, wide.shape[-1])
                    )
                    for number, (low, high) in enumerate(chunks):
                        for head in range(max(low, span * TILE), min(high, (span + 1) * TILE)):
                            outs[place + number][head - low, position, slot * rows : (slot + 1) * rows, :] = wide[
                                slot, pl.ds(offsets[index] + head - span * TILE, rows, stride=TILE), :
                            ].astype(jnp.bfloat16)
        place += len(chunks)


def pack(arrays, plan, heads, after=()):
    _, slots, rows, _, size = arrays[0].shape
    spans = max(1, heads // TILE)
    shapes = [
        jax.ShapeDtypeStruct((high - low, len(wanted), slots * rows, size), jnp.bfloat16)
        for _, wanted, chunks in plan
        for low, high in chunks
    ] + [jax.ShapeDtypeStruct((TILE, size), jnp.float32)]
    count = len(plan)
    moved = count * 4 * spans * slots * rows * TILE * size * 2
    return pl.pallas_call(
        functools.partial(pack_kernel, plan, heads, len(after)),
        out_shape=shapes,
        in_specs=[pl.BlockSpec(memory_space=pltpu.HBM)] * 4 + [pl.BlockSpec(memory_space=pl.ANY)] * len(after),
        out_specs=[pl.BlockSpec(memory_space=pltpu.VMEM)] * len(shapes),
        scratch_shapes=[
            pltpu.VMEM((count, 4 * spans, slots, rows, TILE, size), jnp.bfloat16),
            pltpu.VMEM((slots, rows * TILE, size), jnp.float32),
            pltpu.SemaphoreType.DMA((count, 4 * spans)),
        ],
        compiler_params=pltpu.CompilerParams(vmem_limit_bytes=PACK_VMEM_LIMIT),
        cost_estimate=pl.CostEstimate(flops=moved, bytes_accessed=2 * moved, transcendentals=0),
        name="pack",
    )(*arrays, *after)


def contract_last(left, right):
    return lax.dot_general(left, right, (((1,), (1,)), ((), ())), preferred_element_type=jnp.float32)


def layouts(slots):
    found = []

    def extend(start, clips):
        if start == slots:
            found.append(tuple(clips))
        for span in range(1, min(MAXCLIP, slots - start) + 1):
            extend(start + span, clips + [(start, span)])

    extend(0, [])
    return found


def normalized(block, gain):
    wide = block.astype(jnp.float32)
    wide = wide * lax.rsqrt(jnp.mean(wide * wide, axis=-1, keepdims=True) + EPS)
    return (wide * gain).astype(jnp.bfloat16)


def prepare_kernel(low, after, gains, *refs):
    pieces, out = refs[after:-1], refs[-1]
    heads, _, tokens, _ = pieces[0].shape
    slots = out.shape[2]
    rows = tokens // slots
    for head in range(heads):
        for array in range(4):
            for source, piece in enumerate(pieces[array // 2 :: 2]):
                block = piece[head, array % 2]
                if array < 2:
                    block = normalized(block, gains[array, low + head : low + head + 1, :])
                for slot in range(slots):
                    out[head, array, slot, source * rows : (source + 1) * rows, :] = block[
                        slot * rows : (slot + 1) * rows
                    ]


def prepare(low, gains, pieces, slots, after):
    heads, _, tokens, size = pieces[0].shape
    moved = len(pieces) * heads * 2 * tokens * size * 2
    return pl.pallas_call(
        functools.partial(prepare_kernel, low, len(after)),
        out_shape=jax.ShapeDtypeStruct((heads, 4, slots, len(pieces) // 2 * tokens // slots, size), jnp.bfloat16),
        in_specs=[pl.BlockSpec(memory_space=pltpu.VMEM)] * (1 + len(after) + len(pieces)),
        out_specs=pl.BlockSpec(memory_space=pltpu.VMEM),
        compiler_params=pltpu.CompilerParams(vmem_limit_bytes=VMEM_LIMIT),
        cost_estimate=pl.CostEstimate(flops=1, bytes_accessed=1, transcendentals=0),
        name="prepare",
    )(gains, *after, *pieces)


def attention_chunk(low, count, units, gains, values, close, pieces, held, total):
    query, key, value, grad = held
    group = lax.axis_index("dp")
    _, _, tokens, size = pieces[0].shape
    slots, near = close.shape[2:4]
    rows = tokens // slots
    unit = near + rows * len(pieces)
    for head in range(count):
        for array, kept in enumerate(held):
            for slot in range(slots):
                kept[head, slot * unit : slot * unit + near, :] = close[head, array, slot]
                if array == VALUES:
                    kept[head, slot * unit + near : (slot + 1) * unit, :] = values[low + head, slot]
            if array == VALUES:
                continue
            for source, piece in enumerate(pieces):
                block = piece[head, OTHERS.index(array)]
                if array < 2:
                    block = normalized(block, gains[array, low + head : low + head + 1, :])
                for slot in range(slots):
                    start = slot * unit + near + source * rows
                    kept[head, start : start + rows, :] = block[slot * rows : (slot + 1) * rows]
    factor = size ** (-0.5) * math.log2(math.e)

    def attention(head, layout):
        blocks = [
            (slice(slot * unit, (slot + span) * unit), slice(place * unit, (place + 1) * unit))
            for slot, span in layout
            for place in range(slot, slot + span)
        ]
        scores = [contract_last(key[head, keys, :], query[head, own, :]) for keys, own in blocks]
        dprobs = [contract_last(value[head, keys, :], grad[head, own, :]) for keys, own in blocks]
        expos = [jnp.exp2(score * factor) for score in scores]
        shares = [1.0 / jnp.sum(expo, axis=0, keepdims=True) for expo in expos]
        probs = [expo * share for expo, share in zip(expos, shares)]
        deltas = [jnp.sum(prob * dprob, axis=0, keepdims=True) for prob, dprob in zip(probs, dprobs)]
        dscores = [
            (prob * (dprob - delta)).astype(jnp.bfloat16) for prob, dprob, delta in zip(probs, dprobs, deltas)
        ]
        mixed = [
            jnp.dot(dscore, query[head, own, :], preferred_element_type=jnp.float32)
            for dscore, (_, own) in zip(dscores, blocks)
        ]
        return sum(
            jnp.sum(part * key[head, keys, :].astype(jnp.float32), axis=0, keepdims=True)
            for part, (keys, _) in zip(mixed, blocks)
        )

    table = units[...]
    rows_of, slots_of = (lax.broadcasted_iota(jnp.int32, table.shape, dim) for dim in (0, 1))
    starts = jnp.where((rows_of == group) & (table > 0), lax.shift_left(jnp.int32(1), slots_of), 0)
    begins = jnp.sum(starts)
    for layout in layouts(slots):

        @pl.when(begins == sum(1 << slot for slot, _ in layout))
        def _():
            for head in range(count):
                total[head : head + 1, :] = attention(head, layout)


def chunk_kernel(low, units, gains, values, close, *refs):
    pieces, out, held = refs[:-5], refs[-5], refs[-4:]
    attention_chunk(low, out.shape[0], units, gains, values, close, pieces, held, out)


def last_kernel(low, sources, earlier, peers, units, gains, values, close, *refs):
    pieces = refs[:sources]
    before = refs[sources : sources + earlier]
    outs = refs[sources + earlier : sources + earlier + len(peers)]
    held, total = refs[sources + earlier + len(peers) : -1], refs[-1]
    attention_chunk(low, total.shape[0], units, gains, values, close, pieces, held, total)
    group = lax.axis_index("dp")
    size = total.shape[-1]
    width = outs[0].shape[-1]
    scaled = jnp.concatenate([ref[...] for ref in before] + [total[...]], axis=0) * (size ** (-0.5))
    for side in range(2):
        grads = scaled / gains[side]
        for out, targets in zip(outs, peers):
            target = sum(jnp.where(group == place, whom, 0) for place, whom in enumerate(targets))
            shift = lax.rem(size - target * width, size)
            out[side] = pltpu.roll(grads, shift, 1)[:, :width]


def attend(low, count, units, gains, values, close, pieces, earlier=None, peers=None):
    _, _, tokens, size = pieces[0].shape
    all_tokens = close.shape[2] * close.shape[3] + tokens * len(pieces)
    held = [pltpu.VMEM((count, all_tokens, size), jnp.bfloat16)] * 4
    if earlier is None:
        kernel = functools.partial(chunk_kernel, low)
        shapes = jax.ShapeDtypeStruct((count, size), jnp.float32)
        earlier = []
        outs = pl.BlockSpec(memory_space=pltpu.VMEM)
    else:
        kernel = functools.partial(last_kernel, low, len(pieces), len(earlier), peers)
        heads = gains.shape[1]
        shapes = [jax.ShapeDtypeStruct((2, heads, size // len(peers)), jnp.float32)] * len(peers)
        held.append(pltpu.VMEM((count, size), jnp.float32))
        outs = [pl.BlockSpec(memory_space=pltpu.VMEM)] * len(peers)
    pairs = count * all_tokens * all_tokens // 2
    return pl.pallas_call(
        kernel,
        out_shape=shapes,
        in_specs=[pl.BlockSpec(memory_space=pltpu.VMEM)] * (4 + len(pieces) + len(earlier)),
        out_specs=outs,
        scratch_shapes=held,
        compiler_params=pltpu.CompilerParams(vmem_limit_bytes=VMEM_LIMIT),
        cost_estimate=pl.CostEstimate(
            flops=6 * pairs * size, bytes_accessed=len(pieces) * count * 4 * tokens * size * 2, transcendentals=pairs
        ),
        name="attend",
    )(units, gains, values, close, *pieces, *earlier)


def seen_kernel(*refs):
    refs[-1][...] = jnp.zeros_like(refs[-1])


def seen(blocks):
    return pl.pallas_call(
        seen_kernel,
        out_shape=jax.ShapeDtypeStruct((TILE, blocks[0].shape[-1]), jnp.float32),
        in_specs=[pl.BlockSpec(memory_space=pl.ANY)] * len(blocks),
        out_specs=pl.BlockSpec(memory_space=pltpu.VMEM),
        compiler_params=pltpu.CompilerParams(vmem_limit_bytes=1024 * 1024),
        cost_estimate=pl.CostEstimate(flops=1, bytes_accessed=1024 * 1024, transcendentals=0),
        name="seen",
    )(*blocks)


def ring_targets(groups):
    ring = list(range(0, groups, 2)) + list(range(1, groups, 2))
    return [[ring[(ring.index(place) + step) % groups] for place in range(groups)] for step in range(groups)]


def body(sequence, groups, queries, key_rows, value_rows, out_grad, norm_gains, clip_units):
    arrays = (queries, key_rows, value_rows, out_grad)
    heads = norm_gains.shape[1]
    chunks = head_chunks(heads)
    far = list(range(2, sequence)) or [1]
    near = [flip for flip in range(1, sequence) if flip not in far]

    def send(block, flip):
        return lax.ppermute(block, "seq", [(s, s ^ flip) for s in range(sequence)])

    slots = clip_units.shape[1]
    peers = ring_targets(groups)
    close = near + [0]

    def pack_and_send(plan, after):
        *blocks, token = pack(arrays, plan, heads, after)
        flips = [flip for flip, _, wanted in plan for _ in wanted]
        return [send(block, flip) if flip else block for flip, block in zip(flips, blocks)], token

    def far_plan(number):
        return [(flip, OTHERS, chunks[number : number + 1]) for flip in far]

    *tiles, token = cut(arrays[VALUES], far, heads)
    tiles = [send(block, flip) for flip, block in zip(far, tiles)]
    received, token = pack_and_send(far_plan(0), [token])
    later = far_plan(1) if len(chunks) > 1 else []
    whole = [(flip, pair, chunks) for flip in close for pair in ((0, 1), (2, 3))]
    blocks, _ = pack_and_send(later + whole, [token, seen(tiles)])
    values = arrange(tiles, heads)
    prepared = [
        prepare(low, norm_gains, blocks[len(later) + number :: len(chunks)], slots, [] if number else [seen(received)])
        for number, (low, _) in enumerate(chunks)
    ]
    waiting, sums = blocks[: len(later)], []
    for number, (low, high) in enumerate(chunks[:-1]):
        sums.append(attend(low, high - low, clip_units, norm_gains, values, prepared[number], received))
        received = waiting
        if number + 2 < len(chunks):
            waiting, _ = pack_and_send(far_plan(number + 2), sums[-1:])
    low, high = chunks[-1]
    parts = attend(
        low, high - low, clip_units, norm_gains, values, prepared[-1], received, sums, peers
    )
    result = parts[0]
    for part, targets in zip(parts[1:], peers[1:]):
        result = result + lax.ppermute(part, "dp", list(enumerate(targets)))
    return result


def solution(mesh):
    return jax.shard_map(
        functools.partial(body, mesh.shape["seq"], mesh.shape["dp"]),
        mesh=mesh,
        in_specs=(
            P(("parts", "dp"), None, "seq", None, None),
            P(("parts", "dp"), None, "seq", None, None),
            P(("parts", "dp"), None, "seq", None, None),
            P(("parts", "dp"), None, "seq", None, None),
            P(None, "seq", None),
            P("parts", None),
        ),
        out_specs=P("parts", "seq", "dp"),
        check_vma=False,
    )
```

```python
import functools
import math

import jax
import jax.numpy as jnp
from jax import lax
from jax.experimental import pallas as pl
from jax.experimental.pallas import tpu as pltpu
from jax.sharding import PartitionSpec as P

MAXCLIP = 3
VALUES = 2
OTHERS = (0, 1, 3)
TILE = 8
EPS = 1e-06
VMEM_LIMIT = 48 * 1024 * 1024
PACK_VMEM_LIMIT = 53 * 1024 * 1024


def head_chunks(heads):
    sizes = {8: (4, 3, 1)}.get(heads)
    if sizes is None:
        sizes = (1,) * heads if heads <= 2 else (heads - heads // 2, heads // 2)
    bounds, start = [], 0
    for size in sizes:
        bounds.append((start, start + size))
        start += size
    return bounds


def tile_start(heads, flip):
    head = jnp.bitwise_xor(lax.axis_index("seq"), flip) * heads
    offset = 0 if heads % TILE == 0 else lax.rem(head, TILE)
    return pl.multiple_of((head // TILE) * TILE, TILE), offset


def cut_kernel(flips, heads, after, array, *refs):
    outs, token, sems = refs[after:-2], refs[-2], refs[-1]
    token[...] = jnp.zeros_like(token)
    copies = []
    for index, flip in enumerate(flips):
        start, _ = tile_start(heads, flip)
        source = array.at[0, :, :, pl.ds(start, outs[index].shape[2]), :]
        copies.append(pltpu.make_async_copy(source, outs[index], sems.at[index]))
        copies[-1].start()
    for copy in copies:
        copy.wait()


def cut(array, flips, heads, after):
    _, slots, rows, _, size = array.shape
    shape = jax.ShapeDtypeStruct((slots, rows, max(heads, TILE), size), array.dtype)
    return pl.pallas_call(
        functools.partial(cut_kernel, flips, heads, len(after)),
        out_shape=[shape] * len(flips) + [jax.ShapeDtypeStruct((TILE, size), jnp.float32)],
        in_specs=[pl.BlockSpec(memory_space=pltpu.HBM)] + [pl.BlockSpec(memory_space=pl.ANY)] * len(after),
        out_specs=[pl.BlockSpec(memory_space=pltpu.VMEM)] * (len(flips) + 1),
        scratch_shapes=[pltpu.SemaphoreType.DMA((len(flips),))],
        compiler_params=pltpu.CompilerParams(vmem_limit_bytes=PACK_VMEM_LIMIT),
        name="cut",
    )(array, *after)


def arrange_kernel(*refs):
    pieces, out, wide = refs[:-2], refs[-2], refs[-1]
    heads, slots = out.shape[:2]
    rows, held = pieces[0].shape[1:3]
    _, offset = tile_start(heads, 0)
    for source, piece in enumerate(pieces):
        for slot in range(slots):
            for span in range(held // TILE):
                place = (source * slots + slot) % wide.shape[0]
                block = piece[slot, :, span * TILE : (span + 1) * TILE, :]
                wide[place] = block.astype(jnp.float32).reshape(rows * TILE, wide.shape[-1])
                for head in range(span * TILE, min(heads, (span + 1) * TILE)):
                    out[head, slot, source * rows : (source + 1) * rows, :] = wide[
                        place, pl.ds(offset + head - span * TILE, rows, stride=TILE), :
                    ].astype(jnp.bfloat16)


def arrange(pieces, heads):
    slots, rows, held, size = pieces[0].shape
    moved = len(pieces) * slots * rows * held * size * 2
    return pl.pallas_call(
        arrange_kernel,
        out_shape=jax.ShapeDtypeStruct((heads, slots, len(pieces) * rows, size), jnp.bfloat16),
        in_specs=[pl.BlockSpec(memory_space=pltpu.VMEM)] * len(pieces),
        out_specs=pl.BlockSpec(memory_space=pltpu.VMEM),
        scratch_shapes=[pltpu.VMEM((slots, rows * TILE, size), jnp.float32)],
        compiler_params=pltpu.CompilerParams(vmem_limit_bytes=VMEM_LIMIT),
        cost_estimate=pl.CostEstimate(flops=moved, bytes_accessed=2 * moved, transcendentals=0),
        name="arrange",
    )(*pieces)


def pack_kernel(plan, heads, after, *refs):
    arrays = refs[:4]
    outs = refs[4 + after : 4 + after + sum(len(chunks) for _, _, chunks in plan)]
    token, raw, wide, sems = refs[4 + after + len(outs) :]
    token[...] = jnp.zeros_like(token)
    slots, rows = raw.shape[2], raw.shape[3]
    spans = max(1, heads // TILE)

    def copy(index, array, span, first):
        return pltpu.make_async_copy(
            arrays[array].at[0, :, :, pl.ds(first + span * TILE, TILE), :],
            raw.at[index, array * spans + span],
            sems.at[index, array * spans + span],
        )

    firsts, offsets = zip(*[tile_start(heads, flip) for flip, _, _ in plan])
    for index, (_, wanted, _) in enumerate(plan):
        for array in wanted:
            for span in range(spans):
                copy(index, array, span, firsts[index]).start()
    place = 0
    for index, (_, wanted, chunks) in enumerate(plan):
        for position, array in enumerate(wanted):
            for span in range(spans):
                copy(index, array, span, firsts[index]).wait()
                for slot in range(slots):
                    wide[slot] = (
                        raw[index, array * spans + span, slot]
                        .astype(jnp.float32)
                        .reshape(rows * TILE, wide.shape[-1])
                    )
                    for number, (low, high) in enumerate(chunks):
                        for head in range(max(low, span * TILE), min(high, (span + 1) * TILE)):
                            outs[place + number][head - low, position, slot * rows : (slot + 1) * rows, :] = wide[
                                slot, pl.ds(offsets[index] + head - span * TILE, rows, stride=TILE), :
                            ].astype(jnp.bfloat16)
        place += len(chunks)


def pack(arrays, plan, heads, after=()):
    _, slots, rows, _, size = arrays[0].shape
    spans = max(1, heads // TILE)
    shapes = [
        jax.ShapeDtypeStruct((high - low, len(wanted), slots * rows, size), jnp.bfloat16)
        for _, wanted, chunks in plan
        for low, high in chunks
    ] + [jax.ShapeDtypeStruct((TILE, size), jnp.float32)]
    count = len(plan)
    moved = count * 4 * spans * slots * rows * TILE * size * 2
    return pl.pallas_call(
        functools.partial(pack_kernel, plan, heads, len(after)),
        out_shape=shapes,
        in_specs=[pl.BlockSpec(memory_space=pltpu.HBM)] * 4 + [pl.BlockSpec(memory_space=pl.ANY)] * len(after),
        out_specs=[pl.BlockSpec(memory_space=pltpu.VMEM)] * len(shapes),
        scratch_shapes=[
            pltpu.VMEM((count, 4 * spans, slots, rows, TILE, size), jnp.bfloat16),
            pltpu.VMEM((slots, rows * TILE, size), jnp.float32),
            pltpu.SemaphoreType.DMA((count, 4 * spans)),
        ],
        compiler_params=pltpu.CompilerParams(vmem_limit_bytes=PACK_VMEM_LIMIT),
        cost_estimate=pl.CostEstimate(flops=moved, bytes_accessed=2 * moved, transcendentals=0),
        name="pack",
    )(*arrays, *after)


def contract_last(left, right):
    return lax.dot_general(left, right, (((1,), (1,)), ((), ())), preferred_element_type=jnp.float32)


def layouts(slots):
    found = []

    def extend(start, clips):
        if start == slots:
            found.append(tuple(clips))
        for span in range(1, min(MAXCLIP, slots - start) + 1):
            extend(start + span, clips + [(start, span)])

    extend(0, [])
    return found


def normalized(block, gain):
    wide = block.astype(jnp.float32)
    wide = wide * lax.rsqrt(jnp.mean(wide * wide, axis=-1, keepdims=True) + EPS)
    return (wide * gain).astype(jnp.bfloat16)


def prepare_kernel(low, after, gains, *refs):
    pieces, out = refs[after:-1], refs[-1]
    heads, _, tokens, _ = pieces[0].shape
    slots = out.shape[2]
    rows = tokens // slots
    for head in range(heads):
        for array in range(4):
            for source, piece in enumerate(pieces[array // 2 :: 2]):
                block = piece[head, array % 2]
                if array < 2:
                    block = normalized(block, gains[array, low + head : low + head + 1, :])
                for slot in range(slots):
                    out[head, array, slot, source * rows : (source + 1) * rows, :] = block[
                        slot * rows : (slot + 1) * rows
                    ]


def prepare(low, gains, pieces, slots, after):
    heads, _, tokens, size = pieces[0].shape
    moved = len(pieces) * heads * 2 * tokens * size * 2
    return pl.pallas_call(
        functools.partial(prepare_kernel, low, len(after)),
        out_shape=jax.ShapeDtypeStruct((heads, 4, slots, len(pieces) // 2 * tokens // slots, size), jnp.bfloat16),
        in_specs=[pl.BlockSpec(memory_space=pltpu.VMEM)] * (1 + len(after) + len(pieces)),
        out_specs=pl.BlockSpec(memory_space=pltpu.VMEM),
        compiler_params=pltpu.CompilerParams(vmem_limit_bytes=VMEM_LIMIT),
        cost_estimate=pl.CostEstimate(flops=1, bytes_accessed=1, transcendentals=0),
        name="prepare",
    )(gains, *after, *pieces)


def attention_chunk(low, count, units, gains, values, close, pieces, held, total):
    query, key, value, grad = held
    group = lax.axis_index("dp")
    _, _, tokens, size = pieces[0].shape
    slots, near = close.shape[2:4]
    rows = tokens // slots
    unit = near + rows * len(pieces)
    for head in range(count):
        for array, kept in enumerate(held):
            for slot in range(slots):
                kept[head, slot * unit : slot * unit + near, :] = close[head, array, slot]
                if array == VALUES:
                    kept[head, slot * unit + near : (slot + 1) * unit, :] = values[low + head, slot]
            if array == VALUES:
                continue
            for source, piece in enumerate(pieces):
                block = piece[head, OTHERS.index(array)]
                if array < 2:
                    block = normalized(block, gains[array, low + head : low + head + 1, :])
                for slot in range(slots):
                    start = slot * unit + near + source * rows
                    kept[head, start : start + rows, :] = block[slot * rows : (slot + 1) * rows]
    factor = size ** (-0.5) * math.log2(math.e)

    def attention(head, layout):
        blocks = [
            (slice(slot * unit, (slot + span) * unit), slice(place * unit, (place + 1) * unit))
            for slot, span in layout
            for place in range(slot, slot + span)
        ]
        scores = [contract_last(key[head, keys, :], query[head, own, :]) for keys, own in blocks]
        dprobs = [contract_last(value[head, keys, :], grad[head, own, :]) for keys, own in blocks]
        expos = [jnp.exp2(score * factor) for score in scores]
        shares = [1.0 / jnp.sum(expo, axis=0, keepdims=True) for expo in expos]
        probs = [expo * share for expo, share in zip(expos, shares)]
        deltas = [jnp.sum(prob * dprob, axis=0, keepdims=True) for prob, dprob in zip(probs, dprobs)]
        dscores = [
            (prob * (dprob - delta)).astype(jnp.bfloat16) for prob, dprob, delta in zip(probs, dprobs, deltas)
        ]
        mixed = [
            jnp.dot(dscore, query[head, own, :], preferred_element_type=jnp.float32)
            for dscore, (_, own) in zip(dscores, blocks)
        ]
        return sum(
            jnp.sum(part * key[head, keys, :].astype(jnp.float32), axis=0, keepdims=True)
            for part, (keys, _) in zip(mixed, blocks)
        )

    table = units[...]
    rows_of, slots_of = (lax.broadcasted_iota(jnp.int32, table.shape, dim) for dim in (0, 1))
    starts = jnp.where((rows_of == group) & (table > 0), lax.shift_left(jnp.int32(1), slots_of), 0)
    begins = jnp.sum(starts)
    for layout in layouts(slots):

        @pl.when(begins == sum(1 << slot for slot, _ in layout))
        def _():
            for head in range(count):
                total[head : head + 1, :] = attention(head, layout)


def chunk_kernel(low, units, gains, values, close, *refs):
    pieces, out, held = refs[:-5], refs[-5], refs[-4:]
    attention_chunk(low, out.shape[0], units, gains, values, close, pieces, held, out)


def last_kernel(low, sources, earlier, peers, units, gains, values, close, *refs):
    pieces = refs[:sources]
    before = refs[sources : sources + earlier]
    outs = refs[sources + earlier : sources + earlier + len(peers)]
    held, total = refs[sources + earlier + len(peers) : -1], refs[-1]
    attention_chunk(low, total.shape[0], units, gains, values, close, pieces, held, total)
    group = lax.axis_index("dp")
    size = total.shape[-1]
    width = outs[0].shape[-1]
    scaled = jnp.concatenate([ref[...] for ref in before] + [total[...]], axis=0) * (size ** (-0.5))
    for side in range(2):
        grads = scaled / gains[side]
        for out, targets in zip(outs, peers):
            target = sum(jnp.where(group == place, whom, 0) for place, whom in enumerate(targets))
            shift = lax.rem(size - target * width, size)
            out[side] = pltpu.roll(grads, shift, 1)[:, :width]


def attend(low, count, units, gains, values, close, pieces, earlier=None, peers=None):
    _, _, tokens, size = pieces[0].shape
    all_tokens = close.shape[2] * close.shape[3] + tokens * len(pieces)
    held = [pltpu.VMEM((count, all_tokens, size), jnp.bfloat16)] * 4
    if earlier is None:
        kernel = functools.partial(chunk_kernel, low)
        shapes = jax.ShapeDtypeStruct((count, size), jnp.float32)
        earlier = []
        outs = pl.BlockSpec(memory_space=pltpu.VMEM)
    else:
        kernel = functools.partial(last_kernel, low, len(pieces), len(earlier), peers)
        heads = gains.shape[1]
        shapes = [jax.ShapeDtypeStruct((2, heads, size // len(peers)), jnp.float32)] * len(peers)
        held.append(pltpu.VMEM((count, size), jnp.float32))
        outs = [pl.BlockSpec(memory_space=pltpu.VMEM)] * len(peers)
    pairs = count * all_tokens * all_tokens // 2
    return pl.pallas_call(
        kernel,
        out_shape=shapes,
        in_specs=[pl.BlockSpec(memory_space=pltpu.VMEM)] * (4 + len(pieces) + len(earlier)),
        out_specs=outs,
        scratch_shapes=held,
        compiler_params=pltpu.CompilerParams(vmem_limit_bytes=VMEM_LIMIT),
        cost_estimate=pl.CostEstimate(
            flops=6 * pairs * size, bytes_accessed=len(pieces) * count * 4 * tokens * size * 2, transcendentals=pairs
        ),
        name="attend",
    )(units, gains, values, close, *pieces, *earlier)


def seen_kernel(*refs):
    refs[-1][...] = jnp.zeros_like(refs[-1])


def seen(blocks):
    return pl.pallas_call(
        seen_kernel,
        out_shape=jax.ShapeDtypeStruct((TILE, blocks[0].shape[-1]), jnp.float32),
        in_specs=[pl.BlockSpec(memory_space=pl.ANY)] * len(blocks),
        out_specs=pl.BlockSpec(memory_space=pltpu.VMEM),
        compiler_params=pltpu.CompilerParams(vmem_limit_bytes=1024 * 1024),
        cost_estimate=pl.CostEstimate(flops=1, bytes_accessed=1024 * 1024, transcendentals=0),
        name="seen",
    )(*blocks)


def ring_targets(groups):
    ring = [0] + list(range(1, groups, 2)) + list(range(2, groups, 2))[::-1]
    return [[ring[(ring.index(place) + step) % groups] for place in range(groups)] for step in range(groups)]


def body(sequence, groups, queries, key_rows, value_rows, out_grad, norm_gains, clip_units):
    arrays = (queries, key_rows, value_rows, out_grad)
    heads = norm_gains.shape[1]
    chunks = head_chunks(heads)
    far = list(range(2, sequence)) or [1]
    near = [flip for flip in range(1, sequence) if flip not in far]

    def send(block, flip):
        return lax.ppermute(block, "seq", [(s, s ^ flip) for s in range(sequence)])

    slots = clip_units.shape[1]
    peers = ring_targets(groups)
    close = near + [0]

    def pack_and_send(plan, after):
        *blocks, token = pack(arrays, plan, heads, after)
        flips = [flip for flip, _, wanted in plan for _ in wanted]
        return [send(block, flip) if flip else block for flip, block in zip(flips, blocks)], token

    def far_plan(number):
        return [(flip, OTHERS, chunks[number : number + 1]) for flip in far]

    tiles, tokens = [], []
    for flip in far:
        block, token = cut(arrays[VALUES], [flip], heads, tokens)
        tiles.append(send(block, flip))
        tokens = [token]
    received, token = pack_and_send(far_plan(0), tokens)
    later = far_plan(1) if len(chunks) > 1 else []
    whole = [(flip, pair, chunks) for flip in close for pair in ((0, 1), (2, 3))]
    arrived = []
    for tile in tiles:
        arrived = [seen([tile] + arrived)]
    blocks, _ = pack_and_send(later + whole, [token] + arrived)
    values = arrange(tiles, heads)
    prepared = [
        prepare(low, norm_gains, blocks[len(later) + number :: len(chunks)], slots, [] if number else [seen(received)])
        for number, (low, _) in enumerate(chunks)
    ]
    waiting, sums = blocks[: len(later)], []
    for number, (low, high) in enumerate(chunks[:-1]):
        sums.append(attend(low, high - low, clip_units, norm_gains, values, prepared[number], received))
        received = waiting
        if number + 2 < len(chunks):
            waiting, _ = pack_and_send(far_plan(number + 2), sums[-1:])
    low, high = chunks[-1]
    parts = attend(
        low, high - low, clip_units, norm_gains, values, prepared[-1], received, sums, peers
    )
    result = parts[0]
    for part, targets in zip(parts[1:], peers[1:]):
        result = result + lax.ppermute(part, "dp", list(enumerate(targets)))
    return result


def solution(mesh):
    return jax.shard_map(
        functools.partial(body, mesh.shape["seq"], mesh.shape["dp"]),
        mesh=mesh,
        in_specs=(
            P(("parts", "dp"), None, "seq", None, None),
            P(("parts", "dp"), None, "seq", None, None),
            P(("parts", "dp"), None, "seq", None, None),
            P(("parts", "dp"), None, "seq", None, None),
            P(None, "seq", None),
            P("parts", None),
        ),
        out_specs=P("parts", "seq", "dp"),
        check_vma=False,
    )
```
